128 devices in a mesh: section: 2 (over x_lo), dp: 64 (over y, z, x_hi, core).
Axes of the slice: x: 4 (x_hi: 2, x_lo: 2; x = x_hi * 2 + x_lo), y: 4, z: 4, core: 2. Of those that a mesh axis runs over, the one named last changes fastest.
Arguments:
- boundary: float32 [2, 128, 128, 1024], P('section', 'dp'), may hold values from -6 to 6
- w_qkv: float32 [2, 1024, 3072], P('section', 'dp'), may hold values from -0.1875 to 0.1875
- w_out: float32 [2, 1024, 1024], P('section', 'dp'), may hold values from -1.5 to 1.5
- w_gate_up: float32 [2, 1024, 5632], P('section', 'dp'), may hold values from -0.1875 to 0.1875
- w_down_t: float32 [2, 1024, 2816], P('section', 'dp'), may hold values from -0.21875 to 0.21875
- gains: float32 [2, 2048], P('section', 'dp'), may hold values from 0.5 to 1.5
- memory: bfloat16 [128, 2, 512, 1024], P('dp'), may hold values from -6 to 6
- mem_index: int32 [128, 8, 128], P('dp'), may hold values from 0 to 511
- mem_counts: int32 [128], P('dp'), may hold values from 32 to 128, as said below
Outputs:
- ends: float32 [2, 128, 128, 1024], P('section', 'dp')
- grad_qkv: float32 [2, 1024, 3072], P('section', 'dp')
- grad_out: float32 [2, 1024, 1024], P('section', 'dp')
- grad_gate_up: float32 [2, 1024, 5632], P('section', 'dp')
- grad_down_t: float32 [2, 1024, 2816], P('section', 'dp')
- grad_gains: float32 [2, 2048], P('section', 'dp')
The draws below stay inside these ranges and needn't reach their ends.
Inputs may be any that keep to these rules, and one draw needn't show every extreme that they name: `mem_index`: entry [n, h, j] names a row of sequence n's memory that head h reads; rows may repeat. The first mem_counts[n] picked rows of every head of sequence n are valid.
All inputs are finite; a program needn't handle non-finite values.
Results may differ from the reference program's by a relative error of at most 0.023.
Values may be sent and summed in bfloat16 or wider, within the bound.
No kernel may reach another device: no remote copies, remote signals or barrier semaphores. Data moves between devices by JAX's collectives and lax.ppermute only.
A program may use at most 448 MiB of HBM per device.

```python
import jax
import jax.numpy as jnp
from jax import lax

D = 1024
H = 8
HD = 128
FF = 2816
TOPK = 128
MEM = 512
LEN = 128
SEQS = 128


def draw_mem_counts(key, part):
    key = jax.random.fold_in(key, 11)
    first_key, second_key = jax.random.split(key)
    base_counts = jax.random.randint(first_key, (SEQS,), TOPK // 4, TOPK + 1)
    chosen_spots = jax.random.permutation(second_key, SEQS)
    base_counts = base_counts.at[chosen_spots[0]].set(TOPK)
    base_counts = base_counts.at[chosen_spots[1]].set(TOPK // 4)
    return base_counts.astype(jnp.int32)


def place_ends(drawn, stream_key, low, top_value):
    longest = drawn.shape.index(max(drawn.shape))
    spots = []
    for shift in (0, 1):
        where = [jax.random.randint(jax.random.fold_in(stream_key, axis), (), 0, length) for axis, length in enumerate(drawn.shape)]
        where[longest] = (where[longest] + shift) % drawn.shape[longest]
        spots.append(tuple(where))
    return drawn.at[spots[0]].set(low).at[spots[1]].set(top_value)


def block_levels(own_key, dims, cuts, low, top_value):
    factor_of = 1.0
    for axis_at, shards_of in cuts:
        draws = jax.random.uniform(jax.random.fold_in(jax.random.fold_in(own_key, 6), axis_at), (shards_of,), jnp.float32, low / len(cuts), top_value / len(cuts))
        factor_of = factor_of * jnp.repeat(jnp.exp(draws), dims[axis_at] // shards_of).reshape((-1,) + (1,) * (len(dims) - 1 - axis_at))
    return factor_of


def gaussian(own_key, extent, deviation, reach, cuts=(), kind=jnp.bfloat16):
    drawn = jax.random.normal(own_key, extent, jnp.float32) * deviation
    if len(cuts) > 0:
        drawn = block_levels(own_key, extent, cuts, -0.22, 0.18) * drawn
    return jnp.clip(drawn, min=-reach, max=reach).astype(kind)


def setup_inputs(seed: int = 0) -> dict:
    splits = jax.random.split(jax.random.key(seed), 10)
    return {
        "boundary": gaussian(splits[0], (2, SEQS, LEN, D), 1.0, 6.0, ((0, 2), (1, 64)), jnp.float32),
        "w_qkv": gaussian(splits[1], (2, D, 3 * D), D ** -0.5, 0.1875, ((0, 2), (1, 64)), jnp.float32),
        "w_out": gaussian(splits[2], (2, D, D), (max(D // 64, 4)) ** -0.5, 1.5, ((0, 2), (1, 64)), jnp.float32),
        "w_gate_up": gaussian(splits[3], (2, D, 2 * FF), D ** -0.5, 0.1875, ((0, 2), (1, 64)), jnp.float32),
        "w_down_t": gaussian(splits[4], (2, D, FF), (FF // 4) ** -0.5, 0.21875, ((0, 2), (1, 64)), jnp.float32),
        "gains": jnp.clip(1.0 + 0.1 * jax.random.normal(splits[5], (2, 2 * D), jnp.float32), 0.5, 1.5),
        "memory": gaussian(splits[6], (SEQS, 2, MEM, D), 1.0, 6.0, ((0, 64),)),
        "mem_index": place_ends(jax.random.randint(splits[7], (SEQS, H, TOPK), 0, MEM), jax.random.fold_in(splits[7], 1), 0, MEM - 1).astype(jnp.int32),
        "mem_counts": draw_mem_counts(jax.random.fold_in(splits[9], 71), 0),
    }


@jax.custom_vjp
def low(v):
    return lax.optimization_barrier(v.astype(jnp.bfloat16)).astype(jnp.float32)

@jax.custom_vjp
def low_back(v):
    return v

def low_keep(v):
    return (low(v), None)

def low_pass(kept, grad):
    return (grad,)

def back_keep(v):
    return (v, None)

def back_low(kept, grad):
    return (low(grad),)
low.defvjp(low_keep, low_pass)
low_back.defvjp(back_keep, back_low)
HIGHEST = lax.Precision.HIGHEST
MASKED = -1e+30
EPSILON = 1e-06

def rotate(stream):
    length = stream.shape[0]
    half_dim = stream.shape[2] // 2
    rate_list = 10000.0 ** (-jnp.arange(half_dim, dtype=jnp.float32) / half_dim)
    angles = jnp.arange(length, dtype=jnp.float32)[:, None] * rate_list[None, :]
    cosine = jnp.cos(angles)[:, None, :]
    sine_table = jnp.sin(angles)[:, None, :]
    first_half = stream[..., :half_dim]
    second_half = stream[..., half_dim:]
    return jnp.concatenate([first_half * cosine - second_half * sine_table, second_half * cosine + first_half * sine_table], axis=-1)

def normalize(stream, gain_row):
    inverse_rms = lax.rsqrt(lax.optimization_barrier(jnp.mean(stream * stream, axis=-1, keepdims=True)) + EPSILON)
    return stream * inverse_rms * gain_row

def layer_apply(stream, weights, memory_parts):
    w_qkv, w_out, w_gate_up, w_down_t, gains = weights
    length = stream.shape[0]
    scaling = HD ** (-0.5)
    normed = low(normalize(stream, gains[:D]))
    joined = low_back(jnp.dot(normed, w_qkv, precision=HIGHEST))
    queries = joined[:, :D].reshape(length, H, HD)
    key_rows = joined[:, D:2 * D].reshape(length, H, HD)
    value_rows = low(joined[:, 2 * D:].reshape(length, H, HD))
    query_turned = low(rotate(queries))
    key_turned = low(rotate(key_rows))
    local_scores = low_back(jnp.einsum('qhd,khd->hqk', query_turned, key_turned, precision=HIGHEST) * scaling)
    positions = jnp.arange(length)
    local_scores = jnp.where((positions[:, None] >= positions[None, :])[None], local_scores, MASKED)
    row_max = lax.optimization_barrier(jnp.max(local_scores, axis=-1, keepdims=True))
    if memory_parts is not None:
        picked_keys, picked_values, valid_slots = memory_parts
        memory_scores = low_back(jnp.einsum('qhd,hkd->hqk', low(queries), picked_keys, precision=HIGHEST) * scaling)
        memory_scores = jnp.where(valid_slots[None, None, :], memory_scores, MASKED)
        row_max = jnp.maximum(row_max, lax.optimization_barrier(jnp.max(memory_scores, axis=-1, keepdims=True)))
    near_weights = jnp.exp(local_scores - row_max)
    totals = lax.optimization_barrier(jnp.sum(near_weights, axis=-1, keepdims=True))
    if memory_parts is not None:
        far_weights = jnp.exp(memory_scores - row_max)
        totals = totals + lax.optimization_barrier(jnp.sum(far_weights, axis=-1, keepdims=True))
    attended = jnp.einsum('hqk,khd->qhd', low(near_weights / totals), value_rows, precision=HIGHEST)
    if memory_parts is not None:
        attended = attended + jnp.einsum('hqk,hkd->qhd', low(far_weights / totals), picked_values, precision=HIGHEST)
    attended = low(low_back(attended.reshape(length, D)))
    middle = stream + low_back(jnp.dot(attended, w_out, precision=HIGHEST))
    normed_two = low(normalize(middle, gains[D:]))
    gate_up = low_back(jnp.dot(normed_two, w_gate_up, precision=HIGHEST))
    hidden = low(jax.nn.silu(gate_up[:, :FF]) * gate_up[:, FF:])
    return middle + low_back(jnp.dot(hidden, w_down_t.T, precision=HIGHEST))

def reference(boundary, w_qkv, w_out, w_gate_up, w_down_t, gains, memory, mem_index, mem_counts):
    params = (w_qkv, w_out, w_gate_up, w_down_t, gains)
    head_lane = jnp.arange(H)[:, None]
    slot_index = jnp.arange(TOPK)

    def forward(weights, start, memory_rows, picked_rows, valid_count):
        lowered = jax.tree.map(low, weights)
        first_layer = tuple((weight_piece[0] for weight_piece in lowered))
        second_layer = tuple((weight_piece[1] for weight_piece in lowered))
        picked_keys = memory_rows[0].reshape(MEM, H, HD)[picked_rows, head_lane, :]
        picked_values = memory_rows[1].reshape(MEM, H, HD)[picked_rows, head_lane, :]
        middle = layer_apply(start, first_layer, None)
        return layer_apply(middle, second_layer, (picked_keys, picked_values, slot_index < valid_count))

    def sequence_step(grad_sums, sequence_items):
        start, upstream, memory_rows, picked_rows, valid_count = sequence_items
        memory_float = memory_rows.astype(jnp.float32)
        result, pull_back = jax.vjp(lambda weights, stream: forward(weights, stream, memory_float, picked_rows, valid_count), params, start)
        weight_grads, start_grad = pull_back(upstream)
        return (jax.tree.map(jnp.add, grad_sums, weight_grads), (start_grad, result))
    zero_sums = jax.tree.map(jnp.zeros_like, params)
    grad_sums, outputs = lax.scan(sequence_step, zero_sums, (boundary[0], boundary[1], memory, mem_index, mem_counts))
    start_grads, results = outputs
    return (jnp.stack([start_grads, results]), grad_sums[0], grad_sums[1], grad_sums[2], grad_sums[3], grad_sums[4])
```

```python
import jax
import jax.numpy as jnp
from jax import lax
from jax.sharding import Mesh
from jax.sharding import PartitionSpec as P

MASKED = -1e30
EPSILON = 1e-06
LOW = jnp.bfloat16
FULL = jnp.float32
NY, NZ, NX, NC = 4, 4, 2, 2
DP = ("y", "z", "xh", "core")


def hop(block, axis, step):
    count = lax.axis_size(axis)
    return lax.ppermute(block, axis, [(at, (at + step) % count) for at in range(count)])


def ring_gather(block, axis):
    behind = hop(block, axis, 1)
    ahead = hop(block, axis, -1)
    far_low = hop(behind[:2], axis, 1)
    far_high = hop(ahead[2:], axis, -1)
    return [block, ahead, jnp.concatenate([far_low, far_high]), behind]


def gather_rows(block, first, second):
    pair = jnp.stack([block, hop(block, "xh", 1)])
    ahead = hop(pair, first, -1)
    behind = hop(pair, first, 1)
    across = hop(pair, first, 2)
    return ring_gather(jnp.stack([pair, ahead, across, behind]), second)


def total(*terms):
    result = terms[0].astype(FULL)
    for term in terms[1:]:
        result = result + term.astype(FULL)
    return result


def ring_scatter(low, high, axis):
    low_far = hop(low[2], axis, 1)
    high_far = hop(high[2], axis, -1)
    high_back = hop(high[1], axis, 1)
    low_back = hop(low[3], axis, -1)
    low_main = hop(total(low[1], low_far).astype(LOW), axis, 1)
    high_main = hop(total(high[3], high_far).astype(LOW), axis, -1)
    return total(low[0], low_back, low_main), total(high[0], high_back, high_main)


def scatter_rows(low, high, first, second):
    low, high = ring_scatter(low, high, first)
    low, high = low.astype(LOW), high.astype(LOW)
    low, high = ring_scatter([low[i] for i in range(4)], [high[i] for i in range(4)], second)
    low_own, low_off = low[0], low[1].astype(LOW)
    high_own, high_off = high[0], high[1].astype(LOW)
    return total(low_own, hop(low_off, "xh", 1)), total(high_own, hop(high_off, "xh", 1))


def dot(left, right, precision=None):
    return jnp.dot(left, right, preferred_element_type=FULL, precision=precision)


def dot_nt(left, right):
    return lax.dot_general(left, right, (((1,), (1,)), ((), ())), preferred_element_type=FULL)


def dot_tn(left, right):
    return lax.dot_general(left, right, (((0,), (0,)), ((), ())), preferred_element_type=FULL)


def place_matrix(width):
    natural = lax.broadcasted_iota(jnp.int32, (width, width), 0)
    rel = lax.broadcasted_iota(jnp.int32, (width, width), 1)
    run = width // (NY * NZ * NX * NC)
    lane = rel % run
    rel = rel // run
    dx = rel % NX
    dz = rel // NX % NZ
    dy = rel // (NX * NZ) % NY
    dc = rel // (NX * NZ * NY)
    yy = (dy + lax.axis_index("y")) % NY
    zz = (dz + lax.axis_index("z")) % NZ
    xx = (dx + lax.axis_index("xh")) % NX
    cc = (dc + lax.axis_index("core")) % NC
    return (natural == (((yy * NZ + zz) * NX + xx) * NC + cc) * run + lane).astype(LOW)


def rotary_tables(length, head_dim):
    half_dim = head_dim // 2
    rate_list = 10000.0 ** (-jnp.arange(half_dim, dtype=FULL) / half_dim)
    angles = jnp.arange(length, dtype=FULL)[:, None] * rate_list[None, :]
    return (jnp.cos(angles)[:, None, :], jnp.sin(angles)[:, None, :])


def rotate(stream, cosine, sine_table):
    half_dim = stream.shape[-1] // 2
    first, second = stream[..., :half_dim], stream[..., half_dim:]
    return jnp.concatenate([first * cosine - second * sine_table, second * cosine + first * sine_table], axis=-1)


def unit_rows(stream):
    inverse_rms = lax.rsqrt(jnp.mean(stream * stream, axis=-1, keepdims=True) + EPSILON)
    return (stream * inverse_rms, inverse_rms)


def norm_back(grad_unit, unit_part, inverse_rms):
    return inverse_rms * (grad_unit - unit_part * jnp.mean(grad_unit * unit_part, axis=-1, keepdims=True))


def heads_of(stream, count, head_dim):
    return stream.reshape(count, -1, stream.shape[1] // head_dim, head_dim)


def forward(stream, weights, memory, count, head_dim):
    w_qkv, w_out, w_gate_up, w_down, gain_one, gain_two = weights
    width = stream.shape[1]
    scaling = head_dim ** (-0.5)
    unit_one, inverse_one = unit_rows(stream)
    normed_one = (unit_one * gain_one).astype(LOW)
    joined = dot(normed_one, w_qkv)
    queries = heads_of(joined[:, :width], count, head_dim)
    key_rows = heads_of(joined[:, width : 2 * width], count, head_dim)
    value_rows = heads_of(joined[:, 2 * width :], count, head_dim).astype(LOW)
    length = queries.shape[1]
    cosine, sine_table = rotary_tables(length, head_dim)
    query_turned = rotate(queries, cosine, sine_table).astype(LOW)
    key_turned = rotate(key_rows, cosine, sine_table).astype(LOW)
    near = jnp.einsum("nqhd,nkhd->nhqk", query_turned, key_turned, preferred_element_type=FULL) * scaling
    positions = jnp.arange(length)
    near = jnp.where((positions[:, None] >= positions[None, :])[None, None], near, MASKED)
    row_max = jnp.max(near, axis=-1, keepdims=True)
    if memory is not None:
        picked_keys, picked_values, valid = memory
        far = jnp.einsum("nqhd,nhkd->nhqk", queries.astype(LOW), picked_keys, preferred_element_type=FULL) * scaling
        far = jnp.where(valid[:, None, None, :], far, MASKED)
        row_max = jnp.maximum(row_max, jnp.max(far, axis=-1, keepdims=True))
    near = jnp.exp(near - row_max)
    totals = jnp.sum(near, axis=-1, keepdims=True)
    far_probs = None
    if memory is not None:
        far = jnp.exp(far - row_max)
        totals = totals + jnp.sum(far, axis=-1, keepdims=True)
        far_probs = far / totals
    near_probs = near / totals
    attended = jnp.einsum("nhqk,nkhd->nqhd", near_probs.astype(LOW), value_rows, preferred_element_type=FULL)
    if memory is not None:
        attended = attended + jnp.einsum(
            "nhqk,nhkd->nqhd", far_probs.astype(LOW), picked_values, preferred_element_type=FULL
        )
    attended = attended.reshape(stream.shape).astype(LOW)
    middle = stream + dot(attended, w_out)
    unit_two, inverse_two = unit_rows(middle)
    normed_two = (unit_two * gain_two).astype(LOW)
    gate_up = dot(normed_two, w_gate_up)
    ff_width = gate_up.shape[1] // 2
    gate_part, up_part = gate_up[:, :ff_width], gate_up[:, ff_width:]
    hidden = (jax.nn.silu(gate_part) * up_part).astype(LOW)
    result = middle + dot_nt(hidden, w_down)
    saved = (unit_one, inverse_one, normed_one, query_turned, key_turned, value_rows, near_probs, far_probs, attended)
    return result, saved + (unit_two, inverse_two, normed_two, gate_part, up_part, hidden)


def backward(upstream, saved, weights, memory, count, head_dim):
    w_qkv, w_out, w_gate_up, w_down, gain_one, gain_two = weights
    unit_one, inverse_one, normed_one, query_turned, key_turned, value_rows, near_probs, far_probs, attended = saved[:9]
    unit_two, inverse_two, normed_two, gate_part, up_part, hidden = saved[9:]
    scaling = head_dim ** (-0.5)
    upstream_low = upstream.astype(LOW)
    grad_hidden = dot(upstream_low, w_down)
    sigmoid_gate = jax.nn.sigmoid(gate_part)
    grad_gate = grad_hidden * up_part * sigmoid_gate * (1.0 + gate_part * (1.0 - sigmoid_gate))
    grad_up = grad_hidden * gate_part * sigmoid_gate
    grad_ff = jnp.concatenate([grad_gate, grad_up], axis=1).astype(LOW)
    grad_normed_two = dot_nt(grad_ff, w_gate_up)
    grad_gain_two = jnp.sum(grad_normed_two * unit_two, axis=0)
    grad_middle = upstream + norm_back(grad_normed_two * gain_two, unit_two, inverse_two)
    branch_low = grad_middle.astype(LOW)
    grad_attended = heads_of(dot_nt(branch_low, w_out).astype(LOW), count, head_dim)
    grad_near = jnp.einsum("nqhd,nkhd->nhqk", grad_attended, value_rows, preferred_element_type=FULL)
    grad_value = jnp.einsum("nhqk,nqhd->nkhd", near_probs.astype(LOW), grad_attended, preferred_element_type=FULL)
    row_delta = jnp.sum(near_probs * grad_near, axis=-1, keepdims=True)
    if memory is not None:
        picked_keys, picked_values, valid = memory
        grad_far = jnp.einsum("nqhd,nhkd->nhqk", grad_attended, picked_values, preferred_element_type=FULL)
        row_delta = row_delta + jnp.sum(far_probs * grad_far, axis=-1, keepdims=True)
    score_near = (near_probs * (grad_near - row_delta)).astype(LOW)
    grad_query_turned = (
        jnp.einsum("nhqk,nkhd->nqhd", score_near, key_turned, preferred_element_type=FULL) * scaling
    )
    grad_key_turned = (
        jnp.einsum("nhqk,nqhd->nkhd", score_near, query_turned, preferred_element_type=FULL) * scaling
    )
    cosine, sine_table = rotary_tables(grad_attended.shape[1], head_dim)
    grad_queries = rotate(grad_query_turned, cosine, -sine_table)
    if memory is not None:
        score_far = (far_probs * (grad_far - row_delta)).astype(LOW)
        grad_queries = grad_queries + (
            jnp.einsum("nhqk,nhkd->nqhd", score_far, picked_keys, preferred_element_type=FULL) * scaling
        )
    grad_keys = rotate(grad_key_turned, cosine, -sine_table)
    shape = upstream.shape
    grad_joined = jnp.concatenate(
        [grad_queries.reshape(shape), grad_keys.reshape(shape), grad_value.reshape(shape)], axis=1
    ).astype(LOW)
    grad_normed_one = dot_nt(grad_joined, w_qkv)
    grad_gain_one = jnp.sum(grad_normed_one * unit_one, axis=0)
    grad_stream = grad_middle + norm_back(grad_normed_one * gain_one, unit_one, inverse_one)
    acts = (normed_one, grad_joined, attended, branch_low, normed_two, grad_ff, upstream_low, hidden)
    return grad_stream, acts, grad_gain_one, grad_gain_two


def local(boundary, w_qkv, w_out, w_gate_up, w_down_t, gains, memory, mem_index, mem_counts):
    section = lax.axis_index("section")
    last = section == 1
    count, length, width = boundary.shape[1:]
    head_count, slot_count = mem_index.shape[1:]
    head_dim = width // head_count
    rows = w_qkv.shape[1]
    ff_width = w_down_t.shape[2]
    cut = ff_width * 8 // 11
    pad = 128
    place = place_matrix(width)

    gain_block = jnp.pad(gains.reshape(rows, -1).astype(LOW), ((0, 0), (0, pad - gains.shape[1] // rows)))
    first = jnp.concatenate([w_gate_up[0].astype(LOW), w_down_t[0, :, cut:].astype(LOW)], axis=1)
    second = jnp.concatenate(
        [gain_block, w_qkv[0].astype(LOW), w_out[0].astype(LOW), w_down_t[0, :, :cut].astype(LOW)], axis=1
    )
    first = jnp.stack(gather_rows(first, "z", "y"))
    second = jnp.stack(gather_rows(second, "y", "z"), axis=1)
    first = jnp.stack([first, hop(first, "core", 1)]).reshape(width, -1)
    second = jnp.stack([second, hop(second, "core", 1)]).reshape(width, -1)
    gate_full = first[:, : 2 * ff_width]
    down_full = jnp.concatenate([second[:, pad + 4 * width :], first[:, 2 * ff_width :]], axis=1)
    qkv_full = second[:, pad : pad + 3 * width]
    out_full = second[:, pad + 3 * width : pad + 4 * width]
    out_full = dot(dot(place, out_full).astype(LOW), place).astype(LOW)
    gain_flat = dot(place, second[:, :2]).reshape(2, width).astype(LOW)
    gain_rel = dot(gain_flat, place)
    weights = (qkv_full, out_full, gate_full, down_full, gain_rel[:1], gain_rel[1:])

    tables = memory.reshape(count, 2, -1, head_count, head_dim)
    picks = (mem_index[..., None] == jnp.arange(tables.shape[2])).astype(LOW)
    picked = jnp.einsum("nhjm,ntmhd->tnhjd", picks, tables, preferred_element_type=FULL).astype(LOW)
    valid = jnp.arange(slot_count)[None, :] < mem_counts[:, None] * section
    picked_memory = (picked[0], picked[1], valid)

    edge = dot(boundary.reshape(count * length, width), place, lax.Precision.HIGHEST)
    middle, _ = forward(edge, weights, None, count, head_dim)
    moved = lax.ppermute(middle.astype(LOW), "section", [(0, 1)])
    stream = jnp.where(last, moved.astype(FULL), edge)
    result, saved = forward(stream, weights, picked_memory, count, head_dim)
    grad_last, acts_last, one_last, two_last = backward(edge, saved, weights, picked_memory, count, head_dim)
    upstream = lax.ppermute(grad_last.astype(LOW), "section", [(1, 0)]).astype(FULL)
    grad_first, acts_first, one_first, two_first = backward(upstream, saved, weights, None, count, head_dim)
    finals = jnp.where(last, result, grad_first)
    finals = dot(finals, place.T, lax.Precision.HIGHEST).reshape(1, count, length, width)
    acts = [jnp.where(last, a, b) for a, b in zip(acts_last, acts_first)]
    grad_gains = jnp.stack([jnp.where(last, one_last, one_first), jnp.where(last, two_last, two_first)])

    normed_one, grad_joined, attended, branch_low, normed_two, grad_ff, upstream_low, hidden = acts
    attended = dot(attended, place).astype(LOW)
    branch_low = dot_nt(branch_low, place).astype(LOW)
    half = width // 2

    def product(left, right):
        left = jnp.concatenate([left[:, :half], hop(left[:, half:], "core", 1)])
        right = jnp.concatenate([right, hop(right, "core", 1)])
        return dot_tn(left, right).astype(LOW)

    gain_rows = dot(grad_gains, place.T, lax.Precision.HIGHEST).reshape(width, 2)
    gain_rows = lax.dot_general(
        place, gain_rows, (((0,), (0,)), ((), ())), precision=lax.Precision.HIGHEST, preferred_element_type=FULL
    )
    gain_rows = jnp.pad(gain_rows, ((0, 0), (0, pad - 2)))
    gain_rows = total(gain_rows[:half], hop(gain_rows[half:].astype(LOW), "core", 1)).astype(LOW)
    down_grad = product(upstream_low, hidden)
    gate_grad = product(normed_two, grad_ff)
    out_grad = product(attended, branch_low)
    qkv_grad = product(normed_one, grad_joined)
    first = jnp.concatenate([gate_grad, down_grad[:, cut:]], axis=1)
    second = jnp.concatenate([gain_rows, qkv_grad, out_grad, down_grad[:, :cut]], axis=1)
    first = first.reshape(NY, NZ, NX, rows, -1)
    second = second.reshape(NY, NZ, NX, rows, -1)
    one_half, two_half = first.shape[-1] // 2, second.shape[-1] // 256 * 128
    first_low, first_high = scatter_rows(
        [first[i, ..., :one_half] for i in range(4)], [first[i, ..., one_half:] for i in range(4)], "y", "z"
    )
    second_low, second_high = scatter_rows(
        [second[:, i, ..., :two_half] for i in range(4)], [second[:, i, ..., two_half:] for i in range(4)], "z", "y"
    )
    first = jnp.concatenate([first_low, first_high], axis=1)
    second = jnp.concatenate([second_low, second_high], axis=1)
    down_own = jnp.concatenate([second[:, pad + 4 * width :], first[:, 2 * ff_width :]], axis=1)
    return (
        finals,
        second[None, :, pad : pad + 3 * width],
        second[None, :, pad + 3 * width : pad + 4 * width],
        first[None, :, : 2 * ff_width],
        down_own[None],
        second[:, :2].reshape(1, -1),
    )


def solution(mesh):
    mesh = Mesh(mesh.devices.reshape(2, NY, NZ, NX, NC), ("section",) + DP)
    in_specs = (
        P("section", DP, None, None),
        P("section", DP, None),
        P("section", DP, None),
        P("section", DP, None),
        P("section", DP, None),
        P("section", DP),
        P(DP, None, None, None),
        P(DP, None, None),
        P(DP),
    )
    out_specs = in_specs[:6]
    return jax.shard_map(local, mesh=mesh, in_specs=in_specs, out_specs=out_specs, check_vma=False)
```

```python
import functools

import jax
import jax.numpy as jnp
from jax import lax
from jax.experimental import pallas as pl
from jax.experimental.pallas import tpu as pltpu
from jax.sharding import Mesh
from jax.sharding import PartitionSpec as P

MASKED = -1e30
EPSILON = 1e-06
LOW = jnp.bfloat16
FULL = jnp.float32
NY, NZ, NX, NC = 4, 4, 2, 2
DP = ("y", "z", "xh", "core")
D, HEADS, HD, FF = 1024, 8, 128, 2816
COUNT, LENGTH = 2, 128
ROWS = COUNT * LENGTH
BLOCK = 16
HALF = D // 2
PART = D // (NC * NY)
RUN = PART // NZ
PAD = 128
CUT = 2048
TILE = 256
VMEM_LIMIT = 62 * 1024 * 1024
SCALE = HD ** (-0.5)
ANY = pl.BlockSpec(memory_space=pl.ANY)
SMEM = pl.BlockSpec(memory_space=pltpu.SMEM)


def dot(left, right, precision=None):
    return jnp.dot(left, right, preferred_element_type=FULL, precision=precision)


def dot_nt(left, right):
    return lax.dot_general(left, right, (((1,), (1,)), ((), ())), preferred_element_type=FULL)


def dot_tn(left, right):
    return lax.dot_general(left, right, (((0,), (0,)), ((), ())), preferred_element_type=FULL)


def unit_rows(stream):
    inverse_rms = lax.rsqrt(jnp.mean(stream * stream, axis=-1, keepdims=True) + EPSILON)
    return stream * inverse_rms, inverse_rms


def turn(rows, cosine, sine):
    return rows * cosine + pltpu.roll(rows, HD // 2, 1) * sine


def span(start, size):
    return slice(start, start + size)


def attend_forward(x, gain, cosine, sine, w_qkv, qkv, plain):
    unit, _ = unit_rows(x[...])
    normed = (unit * gain[0:1, :]).astype(LOW)
    for start in range(0, 3 * D, TILE):
        joined = dot(normed, w_qkv[:, span(start, TILE)])
        for at in range(start, start + TILE, HD):
            head = joined[:, span(at - start, HD)]
            if at < 2 * D:
                qkv[:, span(at, HD)] = turn(head, cosine[...], sine[...]).astype(LOW)
            else:
                qkv[:, span(at, HD)] = head.astype(LOW)
            if plain is not None and at < D:
                plain[:, span(at, HD)] = head.astype(LOW)


def causal():
    return lax.broadcasted_iota(jnp.int32, (LENGTH, LENGTH), 0) >= lax.broadcasted_iota(jnp.int32, (LENGTH, LENGTH), 1)


def heads_forward(qkv, plain, picked, counts, near, far, attended):
    keep = causal()
    for seq in range(COUNT):
        rows = span(seq * LENGTH, LENGTH)
        if picked is not None:
            valid = lax.broadcasted_iota(jnp.int32, (LENGTH, LENGTH), 1) < counts[seq]
        for head in range(HEADS):
            at = head * HD
            scores = dot_nt(qkv[rows, span(at, HD)], qkv[rows, span(D + at, HD)]) * SCALE
            scores = jnp.where(keep, scores, MASKED)
            row_max = jnp.max(scores, axis=-1, keepdims=True)
            if picked is not None:
                memory = dot_nt(plain[rows, span(at, HD)], picked[0, seq, head]) * SCALE
                memory = jnp.where(valid, memory, MASKED)
                row_max = jnp.maximum(row_max, jnp.max(memory, axis=-1, keepdims=True))
            scores = jnp.exp(scores - row_max)
            totals = jnp.sum(scores, axis=-1, keepdims=True)
            if picked is not None:
                memory = jnp.exp(memory - row_max)
                totals = totals + jnp.sum(memory, axis=-1, keepdims=True)
                memory = memory / totals
                far[seq * HEADS + head] = memory
            scores = scores / totals
            near[seq * HEADS + head] = scores
            result = dot(scores.astype(LOW), qkv[rows, span(2 * D + at, HD)])
            if picked is not None:
                result = result + dot(memory.astype(LOW), picked[1, seq, head])
            attended[rows, span(at, HD)] = result.astype(LOW)


def out_forward(x, attended, place, w_out, attended_rel, middle):
    attended_rel[...] = dot(attended[...], place[...]).astype(LOW)
    for start in range(0, D, 2 * TILE):
        out = dot(attended_rel[...], w_out[:, span(start, 2 * TILE)])
        high = out.astype(LOW)
        low = (out - high.astype(FULL)).astype(LOW)
        shard = place[span(start, 2 * TILE), :]
        moved = dot(high, shard) + dot(low, shard)
        middle[...] = (x[...] if start == 0 else middle[...]) + moved


def ff_forward(middle, gain, w_gate_up, normed_two, gate_up, hidden):
    unit, _ = unit_rows(middle[...])
    normed_two[...] = (unit * gain[1:2, :]).astype(LOW)
    for start in range(0, FF, TILE):
        gate = dot(normed_two[...], w_gate_up[:, span(start, TILE)])
        up = dot(normed_two[...], w_gate_up[:, span(FF + start, TILE)])
        gate_up[:, span(start, TILE)] = gate
        gate_up[:, span(FF + start, TILE)] = up
        hidden[:, span(start, TILE)] = (gate * jax.nn.sigmoid(gate) * up).astype(LOW)


def down_forward(middle, hidden, w_down, result):
    for start in range(0, D, TILE):
        columns = span(start, TILE)
        result[:, columns] = (middle[:, columns] + dot_nt(hidden[...], w_down[columns, :])).astype(result.dtype)


def norm_back(grad, unit, inverse_rms, gain):
    weighted = grad * gain
    return inverse_rms * (weighted - unit * jnp.mean(weighted * unit, axis=-1, keepdims=True))


def gate_backward(upstream_low, w_down, gate_up, grad_ff):
    for start in range(0, FF, TILE):
        grad_hidden = dot(upstream_low[...], w_down[:, span(start, TILE)])
        gate, up = gate_up[:, span(start, TILE)], gate_up[:, span(FF + start, TILE)]
        sigmoid_gate = jax.nn.sigmoid(gate)
        grad_gate = grad_hidden * up * sigmoid_gate * (1.0 + gate * (1.0 - sigmoid_gate))
        grad_ff[:, span(start, TILE)] = grad_gate.astype(LOW)
        grad_ff[:, span(FF + start, TILE)] = (grad_hidden * (gate * sigmoid_gate)).astype(LOW)


def ff_backward(upstream, middle, gain, w_gate_up, grad_ff, grad_middle, gain_grad):
    for start in range(0, D, TILE):
        grad_middle[:, span(start, TILE)] = dot_nt(grad_ff[...], w_gate_up[span(start, TILE), :])
    unit, inverse_rms = unit_rows(middle[...])
    grad = grad_middle[...]
    gain_grad[1:2, :] = jnp.sum(grad * unit, axis=0, keepdims=True)
    grad_middle[...] = upstream[...].astype(FULL) + norm_back(grad, unit, inverse_rms, gain[1:2, :])


def out_backward(grad_middle, place, w_out, branch, grad_attended):
    branch[...] = dot_nt(grad_middle[...].astype(LOW), place[...]).astype(LOW)
    grad_rel = dot_nt(branch[...], w_out[...]).astype(LOW)
    grad_attended[...] = dot_nt(grad_rel, place[...]).astype(LOW)


def heads_backward(qkv, picked, near, far, grad_attended, cosine, sine, grad_joined):
    for seq in range(COUNT):
        rows = span(seq * LENGTH, LENGTH)
        cos, sin = cosine[rows, :], -sine[rows, :]
        for head in range(HEADS):
            at = head * HD
            grad_out = grad_attended[rows, span(at, HD)]
            probs = near[seq * HEADS + head]
            grad_near = dot_nt(grad_out, qkv[rows, span(2 * D + at, HD)])
            delta = jnp.sum(probs * grad_near, axis=-1, keepdims=True)
            if picked is not None:
                memory = far[seq * HEADS + head]
                grad_far = dot_nt(grad_out, picked[1, seq, head])
                delta = delta + jnp.sum(memory * grad_far, axis=-1, keepdims=True)
            grad_joined[rows, span(2 * D + at, HD)] = dot_tn(probs.astype(LOW), grad_out).astype(LOW)
            grad_scores = (probs * (grad_near - delta)).astype(LOW)
            grad_query = turn(dot(grad_scores, qkv[rows, span(D + at, HD)]) * SCALE, cos, sin)
            grad_key = turn(dot_tn(grad_scores, qkv[rows, span(at, HD)]) * SCALE, cos, sin)
            if picked is not None:
                grad_memory = (memory * (grad_far - delta)).astype(LOW)
                grad_query = grad_query + dot(grad_memory, picked[0, seq, head]) * SCALE
            grad_joined[rows, span(at, HD)] = grad_query.astype(LOW)
            grad_joined[rows, span(D + at, HD)] = grad_key.astype(LOW)


def attend_backward(x, gain, w_qkv, grad_joined, grad_middle, normed, result, gain_grad):
    for start in range(0, D, TILE):
        result[:, span(start, TILE)] = dot_nt(grad_joined[...], w_qkv[span(start, TILE), :])
    unit, inverse_rms = unit_rows(x[...])
    normed[...] = (unit * gain[0:1, :]).astype(LOW)
    grad = result[...]
    gain_grad[0:1, :] = jnp.sum(grad * unit, axis=0, keepdims=True)
    result[...] = grad_middle[...] + norm_back(grad, unit, inverse_rms, gain[0:1, :])


EARLY = HALF + FF
WIDE = 2 * FF + HALF
LATE = 4 * D + 2 * HALF
GAINS = span(ROWS, 16)
LOWER, UPPER = span(0, HALF), span(HALF, HALF)
OWN = {name: span(at * HALF, HALF) for at, name in enumerate(("h2", "e", "h1", "o"))}


class Copies:
    def __init__(self, semaphores):
        self.semaphores, self.used, self.groups = semaphores, 0, {}

    def copy(self, at, source, target):
        source, target = (view[0].at[view[1]] if isinstance(view, tuple) else view for view in (source, target))
        return pltpu.make_async_copy(source, target, self.semaphores.at[at])

    def start(self, name, source, target):
        self.copy(self.used, source, target).start()
        self.groups.setdefault(name, []).append((self.used, source, target))
        self.used += 1

    def wait(self, *names):
        for name in names:
            for copy in self.groups.pop(name):
                self.copy(*copy).wait()

    def finish(self):
        self.wait(*list(self.groups))


def y_runs(size):
    return [(0, (0, PART), 0), (1, (0, PART), PART), (2, (0, PART // 2), 2 * PART)] + [
        (3, (0, PART // 2), 2 * PART + PART // 2),
        (4, (0, PART), 3 * PART),
    ]


def z_runs():
    runs = []
    for piece, dz, low, high in ((0, 0, 0, 4), (1, 1, 0, 4), (2, 2, 0, 2), (3, 2, 2, 4), (4, 3, 0, 4)):
        runs += [(piece, ((dy - low) * RUN, RUN), dy * PART + dz * RUN) for dy in range(low, high)]
    return runs


def load(copies, name, pieces, runs, columns, target, target_columns):
    for core in range(NC):
        for piece, (low, size), row in runs:
            source = pieces[core * 5 + piece], (span(low, size), columns)
            copies.start(name, source, (target, (span(core * HALF + row, size), target_columns)))


def load_qkv(copies, second, target):
    load(copies, "qkv", second, z_runs(), span(0, 3 * D), target, span(0, 3 * D))


def load_out(copies, second, target):
    load(copies, "out", second, z_runs(), span(3 * D, D), target, span(0, D))


def load_gains(copies, second, target):
    load(copies, "gains", second, z_runs(), span(4 * D + CUT, PAD), target, span(0, PAD))


def load_gate(copies, first, target):
    load(copies, "gate", first, y_runs(0), span(0, 2 * FF), target, span(0, 2 * FF))


def load_down(copies, first, second, target):
    load(copies, "down", second, z_runs(), span(4 * D, CUT), target, span(0, CUT))
    load(copies, "down", first, y_runs(0), span(2 * FF, FF - CUT), target, span(CUT, FF - CUT))


def kernel_first(section, core, *refs):
    (x, spread, cosine, sine, place), refs = refs[:5], refs[5:]
    first, second, refs = refs[:10], refs[10:20], refs[20:]
    (sent_o, qkv_o, near_o, late_o, middle_o, early_o, gate_up_o, own_o, gain_o), refs = refs[:9], refs[9:]
    xs, gains, cos, sin, places, w_qkv, w_out, w_gate, w_down = refs[:9]
    qkv, near, attended, attended_rel, middle, normed_two, gate_up, hidden, sent, spreads, gain_rows, semaphores = refs[9:]

    copies = Copies(semaphores)
    load_gains(copies, second, gain_rows)
    copies.start("gains", spread, spreads)

    @pl.when(section[0] == 0)
    def _():
        for source, target in ((x, xs), (cosine, cos), (sine, sin)):
            copies.start("small", source, target)
        load_qkv(copies, second, w_qkv)
        copies.start("place", place, places)
        load_out(copies, second, w_out)
        load_gate(copies, first, w_gate)
        load_down(copies, first, second, w_down)

    copies.wait("gains")
    rows = gain_rows[...].astype(FULL).T[:8].astype(LOW)
    low = lax.broadcasted_iota(jnp.int32, (1, D), 1) < HALF
    straight = jnp.logical_xor(low, core[0] == 1)
    for at in range(2):
        picked = dot(rows, spreads[at])
        gains[at : at + 1, :] = jnp.where(straight, picked[0:1], picked[1:2])
    copies.start("gain", gains, gain_o)

    @pl.when(section[0] == 0)
    def _():
        copies.wait("small", "qkv")
        attend_forward(xs, gains, cos, sin, w_qkv, qkv, None)
        copies.start("done", qkv, qkv_o)
        heads_forward(qkv, None, None, None, near, None, attended)
        copies.start("done", near, near_o)
        copies.wait("place", "out")
        out_forward(xs, attended, places, w_out, attended_rel, middle)
        copies.start("done", attended_rel.at[:, LOWER], own_o.at[:, OWN["o"]])
        copies.start("done", attended_rel.at[:, UPPER], late_o.at[span(0, ROWS), span(4 * D + HALF, HALF)])
        copies.start("done", middle, middle_o)
        copies.wait("gate")
        ff_forward(middle, gains, w_gate, normed_two, gate_up, hidden)
        copies.start("done", normed_two.at[:, LOWER], own_o.at[:, OWN["h2"]])
        copies.start("done", normed_two.at[:, UPPER], early_o.at[:, LOWER])
        copies.start("done", gate_up, gate_up_o)
        copies.start("done", hidden, early_o.at[:, span(HALF, FF)])
        copies.wait("down")
        down_forward(middle, hidden, w_down, sent)
        copies.start("done", sent, sent_o)
        copies.wait("done")

    copies.wait("gain")


def two_parts(gain_grad):
    full = gain_grad[...]
    high = full.astype(LOW).astype(FULL)
    return jnp.concatenate([high, full - high, jnp.zeros((12, D), FULL)], axis=0).astype(LOW)


def kernel_last(section, counts, *refs):
    (x_low, upstream, gain, cosine, sine, place, picked), refs = refs[:7], refs[7:]
    first, second, refs = refs[:10], refs[10:20], refs[20:]
    refs = refs[3:]
    (early_o, late_o, own_o, result_o, sent_o, grad_ff_o), refs = refs[:6], refs[6:]
    xl, ups, up_low, gains, cos, sin, places, picks, w_qkv, w_out, w_gate, w_down = refs[:12]
    xs, qkv, plain, near, far, attended, attended_rel, middle, normed_two, gate_up, hidden, result = refs[12:24]
    grad_ff, grad_middle, branch, grad_joined, normed, gain_grad, gain_rows, semaphores = refs[24:]

    @pl.when(section[0] == 1)
    def _():
        copies = Copies(semaphores)
        for source, target in ((x_low, xl), (gain, gains), (cosine, cos), (sine, sin)):
            copies.start("small", source, target)
        load_qkv(copies, second, w_qkv)
        copies.start("picks", picked, picks)
        copies.start("place", place, places)
        load_out(copies, second, w_out)
        load_gate(copies, first, w_gate)
        load_down(copies, first, second, w_down)
        copies.start("up", upstream, ups)
        copies.wait("small", "qkv")
        xs[...] = xl[...].astype(FULL)
        attend_forward(xs, gains, cos, sin, w_qkv, qkv, plain)
        copies.wait("picks")
        heads_forward(qkv, plain, picks, counts, near, far, attended)
        copies.wait("place", "out")
        out_forward(xs, attended, places, w_out, attended_rel, middle)
        copies.start("done", attended_rel.at[:, LOWER], own_o.at[:, OWN["o"]])
        copies.start("done", attended_rel.at[:, UPPER], late_o.at[span(0, ROWS), span(4 * D + HALF, HALF)])
        copies.wait("gate")
        ff_forward(middle, gains, w_gate, normed_two, gate_up, hidden)
        copies.start("done", normed_two.at[:, LOWER], own_o.at[:, OWN["h2"]])
        copies.start("done", normed_two.at[:, UPPER], early_o.at[:, LOWER])
        copies.start("done", hidden, early_o.at[:, span(HALF, FF)])
        copies.wait("down", "up")
        up_low[...] = ups[...].astype(LOW)
        copies.start("done", up_low.at[:, LOWER], own_o.at[:, OWN["e"]])
        copies.start("done", up_low.at[:, UPPER], grad_ff_o.at[:, span(2 * FF, HALF)])
        down_forward(middle, hidden, w_down, result)
        copies.start("result", result, result_o)
        gate_backward(up_low, w_down, gate_up, grad_ff)
        copies.start("done", grad_ff, grad_ff_o.at[:, span(0, 2 * FF)])
        ff_backward(ups, middle, gains, w_gate, grad_ff, grad_middle, gain_grad)
        out_backward(grad_middle, places, w_out, branch, attended)
        copies.start("done", branch, late_o.at[span(0, ROWS), span(3 * D, D)])
        heads_backward(qkv, picks, near, far, attended, cos, sin, grad_joined)
        copies.start("done", grad_joined, late_o.at[span(0, ROWS), span(0, 3 * D)])
        copies.wait("result")
        attend_backward(xs, gains, w_qkv, grad_joined, grad_middle, normed, result, gain_grad)
        xl[...] = result[...].astype(LOW)
        copies.start("done", xl, sent_o)
        copies.start("done", normed.at[:, LOWER], own_o.at[:, OWN["h1"]])
        copies.start("done", normed.at[:, UPPER], late_o.at[span(0, ROWS), span(4 * D, HALF)])
        gain_rows[...] = two_parts(gain_grad)
        copies.start("done", gain_rows, late_o.at[GAINS, span(0, D)])
        copies.finish()


def kernel_back_gate(section, *refs):
    (upstream, gate_up), refs = refs[:2], refs[2:]
    first, second, refs = refs[:10], refs[10:20], refs[20:]
    refs = refs[3:]
    (grad_ff_o, own_o), refs = refs[:2], refs[2:]
    ups, gate_ups, w_down, grad_ff, semaphores = refs

    @pl.when(section[0] == 0)
    def _():
        copies = Copies(semaphores)
        copies.start("up", upstream, ups)
        load_down(copies, first, second, w_down)
        copies.start("saved", gate_up, gate_ups)
        copies.wait("up", "down", "saved")
        copies.start("done", ups.at[:, LOWER], own_o.at[:, OWN["e"]])
        copies.start("done", ups.at[:, UPPER], grad_ff_o.at[:, span(2 * FF, HALF)])
        gate_backward(ups, w_down, gate_ups, grad_ff)
        copies.start("done", grad_ff, grad_ff_o.at[:, span(0, 2 * FF)])
        copies.finish()


def kernel_back_ff(section, *refs):
    (upstream, gain, middle, grad_ff), refs = refs[:4], refs[4:]
    first, refs = refs[:10], refs[10:]
    (grad_middle_o, gain_grad_o), refs = refs[:2], refs[2:]
    ups, gains, mid, grad_ffs, w_gate, grad_middle, gain_grad, semaphores = refs

    @pl.when(section[0] == 0)
    def _():
        copies = Copies(semaphores)
        copies.start("first", grad_ff.at[:, span(0, 2 * FF)], grad_ffs)
        load_gate(copies, first, w_gate)
        copies.start("late", upstream, ups)
        copies.start("late", middle, mid)
        copies.start("late", gain, gains)
        copies.wait("first", "gate", "late")
        ff_backward(ups, mid, gains, w_gate, grad_ffs, grad_middle, gain_grad)
        copies.start("done", grad_middle, grad_middle_o)
        copies.start("done", gain_grad, gain_grad_o)
        copies.finish()


def kernel_back_attend(section, *refs):
    (x, gain, cosine, sine, place, qkv, near, grad_middle, gain_part), refs = refs[:9], refs[9:]
    second, refs = refs[:10], refs[11:]
    (late_o, own_o, result_o), refs = refs[3:6], refs[6:]
    xs, gains, cos, sin, places, qkvs, nears, grad_mid, w_qkv, w_out = refs[:10]
    grad_attended, branch, grad_joined, normed, result, gain_grad, gain_rows, semaphores = refs[10:]

    @pl.when(section[0] == 0)
    def _():
        copies = Copies(semaphores)
        copies.start("mid", grad_middle, grad_mid)
        copies.start("mid", place, places)
        load_out(copies, second, w_out)
        for source, target in ((qkv, qkvs), (near, nears), (cosine, cos), (sine, sin)):
            copies.start("saved", source, target)
        load_qkv(copies, second, w_qkv)
        for source, target in ((x, xs), (gain, gains), (gain_part, gain_grad)):
            copies.start("late", source, target)
        copies.wait("mid", "out")
        out_backward(grad_mid, places, w_out, branch, grad_attended)
        copies.start("done", branch, late_o.at[span(0, ROWS), span(3 * D, D)])
        copies.wait("saved")
        heads_backward(qkvs, None, nears, None, grad_attended, cos, sin, grad_joined)
        copies.start("done", grad_joined, late_o.at[span(0, ROWS), span(0, 3 * D)])
        copies.wait("qkv", "late")
        attend_backward(xs, gains, w_qkv, grad_joined, grad_mid, normed, result, gain_grad)
        copies.start("done", result, result_o)
        copies.start("done", normed.at[:, LOWER], own_o.at[:, OWN["h1"]])
        copies.start("done", normed.at[:, UPPER], late_o.at[span(0, ROWS), span(4 * D, HALF)])
        gain_rows[...] = two_parts(gain_grad)
        copies.start("done", gain_rows, late_o.at[GAINS, span(0, D)])
        copies.finish()


def shape(*dims, dtype=LOW):
    return jax.ShapeDtypeStruct(dims, dtype)


def vmem(*dims, dtype=LOW):
    return pltpu.VMEM(dims, dtype)


Y_COPIES, Z_COPIES = 2 * 5, 2 * 16
W_QKV, W_OUT, W_GATE, W_DOWN = vmem(D, 3 * D), vmem(D, D), vmem(D, 2 * FF), vmem(D, FF)


def call(kernel, operands, scalars, outs, scratch, copies, flops, aliases=None):
    return pl.pallas_call(
        kernel,
        out_shape=outs,
        in_specs=[SMEM] * scalars + [ANY] * (len(operands) - scalars),
        out_specs=[ANY] * len(outs),
        scratch_shapes=list(scratch) + [pltpu.SemaphoreType.DMA((copies,))],
        input_output_aliases=aliases or {},
        compiler_params=pltpu.CompilerParams(vmem_limit_bytes=VMEM_LIMIT),
        cost_estimate=pl.CostEstimate(flops=1000, bytes_accessed=1000, transcendentals=0),
    )(*operands)


def run_first(section, core, x, spread, cosine, sine, place, first, second):
    outs = [
        shape(ROWS, D), shape(ROWS, 3 * D), shape(COUNT * HEADS, LENGTH, LENGTH, dtype=FULL), shape(ROWS + 16, LATE),
        shape(ROWS, D, dtype=FULL), shape(ROWS, EARLY), shape(ROWS, 2 * FF, dtype=FULL), shape(ROWS, 4 * HALF),
        shape(2, D, dtype=FULL),
    ]
    scratch = [vmem(ROWS, D, dtype=FULL), vmem(2, D, dtype=FULL), vmem(ROWS, HD, dtype=FULL), vmem(ROWS, HD, dtype=FULL)]
    scratch += [vmem(D, D), W_QKV, W_OUT, W_GATE, W_DOWN]
    scratch += [vmem(ROWS, 3 * D), vmem(COUNT * HEADS, LENGTH, LENGTH, dtype=FULL), vmem(ROWS, D), vmem(ROWS, D)]
    scratch += [vmem(ROWS, D, dtype=FULL), vmem(ROWS, D), vmem(ROWS, 2 * FF, dtype=FULL), vmem(ROWS, FF), vmem(ROWS, D)]
    scratch += [vmem(2, D, D), vmem(D, PAD)]
    operands = [section, core, x, spread, cosine, sine, place, *first, *second]
    return call(kernel_first, operands, 2, outs, scratch, 24 + 2 * Y_COPIES + 4 * Z_COPIES, 6 * 10**9)


def run_last(section, counts, x_low, upstream, gain, cosine, sine, place, picked, first, second, kept):
    outs = [shape(ROWS, EARLY), shape(ROWS + 16, LATE), shape(ROWS, 4 * HALF), shape(ROWS, D, dtype=FULL)]
    outs += [shape(ROWS, D), shape(ROWS, WIDE)]
    scratch = [vmem(ROWS, D), vmem(ROWS, D, dtype=FULL), vmem(ROWS, D), vmem(2, D, dtype=FULL)]
    scratch += [vmem(ROWS, HD, dtype=FULL), vmem(ROWS, HD, dtype=FULL), vmem(D, D), vmem(2, COUNT, HEADS, LENGTH, HD)]
    scratch += [W_QKV, W_OUT, W_GATE, W_DOWN]
    scratch += [vmem(ROWS, D, dtype=FULL), vmem(ROWS, 3 * D), vmem(ROWS, D)]
    scratch += [vmem(COUNT * HEADS, LENGTH, LENGTH, dtype=FULL)] * 2
    scratch += [vmem(ROWS, D), vmem(ROWS, D), vmem(ROWS, D, dtype=FULL), vmem(ROWS, D), vmem(ROWS, 2 * FF, dtype=FULL)]
    scratch += [vmem(ROWS, FF), vmem(ROWS, D, dtype=FULL)]
    scratch += [vmem(ROWS, 2 * FF), vmem(ROWS, D, dtype=FULL), vmem(ROWS, D), vmem(ROWS, 3 * D), vmem(ROWS, D)]
    scratch += [vmem(2, D, dtype=FULL), vmem(16, D)]
    operands = [section, counts, x_low, upstream, gain, cosine, sine, place, picked, *first, *second, *kept]
    aliases = {len(operands) - 3 + i: i for i in range(3)}
    return call(kernel_last, operands, 2, outs, scratch, 24 + 2 * Y_COPIES + 3 * Z_COPIES, 14 * 10**9, aliases)


def run_back_gate(section, upstream, gate_up, first, second, early, grad_ff, own):
    outs = [shape(ROWS, WIDE), shape(ROWS, 4 * HALF)]
    scratch = [vmem(ROWS, D), vmem(ROWS, 2 * FF, dtype=FULL), W_DOWN, vmem(ROWS, 2 * FF)]
    operands = [section, upstream, gate_up, *first, *second, early, grad_ff, own]
    at = len(operands) - 2
    return call(
        kernel_back_gate, operands, 1, outs, scratch, 10 + Y_COPIES + Z_COPIES, 2 * 10**9, {at: 0, at + 1: 1}
    )


def run_back_ff(section, upstream, gain, middle, grad_ff, first):
    outs = [shape(ROWS, D, dtype=FULL), shape(2, D, dtype=FULL)]
    scratch = [vmem(ROWS, D), vmem(2, D, dtype=FULL), vmem(ROWS, D, dtype=FULL), vmem(ROWS, 2 * FF)]
    scratch += [W_GATE, vmem(ROWS, D, dtype=FULL), vmem(2, D, dtype=FULL)]
    operands = [section, upstream, gain, middle, grad_ff, *first]
    return call(kernel_back_ff, operands, 1, outs, scratch, 10 + Y_COPIES, 3 * 10**9)


def run_back_attend(section, x, gain, cosine, sine, place, qkv, near, grad_middle, gain_part, second, after, kept):
    outs = [shape(ROWS + 16, LATE), shape(ROWS, 4 * HALF), shape(ROWS, D, dtype=FULL)]
    scratch = [vmem(ROWS, D, dtype=FULL), vmem(2, D, dtype=FULL), vmem(ROWS, HD, dtype=FULL), vmem(ROWS, HD, dtype=FULL)]
    scratch += [vmem(D, D), vmem(ROWS, 3 * D), vmem(COUNT * HEADS, LENGTH, LENGTH, dtype=FULL), vmem(ROWS, D, dtype=FULL)]
    scratch += [W_QKV, W_OUT, vmem(ROWS, D), vmem(ROWS, D), vmem(ROWS, 3 * D), vmem(ROWS, D), vmem(ROWS, D, dtype=FULL)]
    scratch += [vmem(2, D, dtype=FULL), vmem(16, D)]
    operands = [section, x, gain, cosine, sine, place, qkv, near, grad_middle, gain_part, *second, after, *kept]
    at = len(operands) - 3
    return call(
        kernel_back_attend, operands, 1, outs, scratch, 20 + 2 * Z_COPIES, 3 * 10**9, {at + i: i for i in range(3)}
    )


def pick_kernel(memory, index, out):
    chosen = index[0, 0]
    hot = (lax.broadcasted_iota(jnp.int32, (memory.shape[2], LENGTH), 0) == chosen).astype(FULL).astype(LOW)
    for kind in range(2):
        out[kind, 0, 0] = dot_tn(hot, memory[0, kind]).astype(LOW)


def run_pick(memory, mem_index):
    slots = memory.shape[2]
    return pl.pallas_call(
        pick_kernel,
        grid=(COUNT, HEADS),
        in_specs=[
            pl.BlockSpec((1, 2, slots, HD), lambda n, h: (n, 0, 0, h)),
            pl.BlockSpec((1, 1, 1, LENGTH), lambda n, h: (n, h, 0, 0)),
        ],
        out_specs=pl.BlockSpec((2, 1, 1, LENGTH, HD), lambda n, h: (0, n, h, 0, 0)),
        out_shape=shape(2, COUNT, HEADS, LENGTH, HD),
    )(memory, mem_index.reshape(COUNT, HEADS, 1, LENGTH))


def z_first(rows):
    return jnp.concatenate([rows[span(dy * PART + dz * RUN, RUN), :] for dz in range(NZ) for dy in range(NY)], axis=0)


def put(copies, staged, columns, outs):
    half = PART // 2
    for target, at, source in (
        (1, 0, 4), (1, 1, 3), (2, 0, 5), (2, 1, 6), (3, 0, 2), (4, 0, 7), (0, 0, 0), (0, 1, 1)
    ):
        rows = staged.at[span(source * half, half), columns]
        copies.start("done", rows, outs[target].at[span(at * half, half), columns])


def products(copies, plan, sides, rights, stages, outs, extra=None):
    for z, stage in ((0, stages[0]), (1, stages[1])):
        at = 0
        for left, right, first, size in plan[z]:
            if left is None:
                stage[:, span(at, size)] = extra()
            else:
                own, other = sides(left)
                if z:
                    own, other = z_first(own), z_first(other)
                mine, theirs = rights(right)
                for start in range(0, size, TILE):
                    width = min(TILE, size - start)
                    columns = span(first + start, width)
                    stage[:, span(at + start, width)] = (dot(own, mine[:, columns]) + dot(other, theirs[:, columns])).astype(LOW)
            put(copies, stage, span(at, size), outs[5 * z : 5 * z + 5])
            at += size


def widths_of(plan):
    return [sum(size for *_, size in part) for part in plan]


def grad_outs(plan):
    return [shape(rows, width) for width in widths_of(plan) for rows in (PART, PART, PART, PART // 2, PART // 2)]


def kernel_grad_ff(early, other_early, wide, other_wide, own, after, *refs):
    outs, (er, oer, wi, owi, ow, stage_y, stage_z, semaphores) = refs[:10], refs[10:]
    copies = Copies(semaphores)
    for source, target in ((early, er), (other_early, oer), (own, ow)):
        copies.start("a", source, target)
    for source, target in ((wide, wi), (other_wide, owi)):
        copies.start("b", source, target)
    copies.wait("a")
    left = {"h2": (ow[:, OWN["h2"]].T, oer[:, LOWER].T)}

    def sides(name):
        if name not in left:
            left[name] = (ow[:, OWN["e"]].T, owi[:, span(2 * FF, HALF)].T)
        return left[name]

    def rights(name):
        return (wi, owi) if name == "wide" else (er, oer)

    copies.wait("b")
    products(copies, FF_PLAN, sides, rights, (stage_y, stage_z), outs)
    copies.finish()


def run_grad_ff(early, other_early, wide, other_wide, own, after):
    scratch = [vmem(ROWS, EARLY)] * 2 + [vmem(ROWS, WIDE)] * 2 + [vmem(ROWS, 4 * HALF)]
    scratch += [vmem(HALF, width) for width in widths_of(FF_PLAN)]
    operands = [early, other_early, wide, other_wide, own, after]
    outs = call(kernel_grad_ff, operands, 0, grad_outs(FF_PLAN), scratch, 5 + 8 * 4, 0)
    return outs[:5], outs[5:]


def kernel_grad_attend(late, other_late, own, pack, *refs):
    outs, (la, ola, ow, pa, stage_y, stage_z, semaphores) = refs[:10], refs[10:]
    copies = Copies(semaphores)
    for source, target in ((late, la), (other_late, ola), (own, ow), (pack, pa)):
        copies.start("a", source, target)
    copies.wait("a")
    left = {
        "h1": (ow[:, OWN["h1"]].T, ola[span(0, ROWS), span(4 * D, HALF)].T),
        "o": (ow[:, OWN["o"]].T, ola[span(0, ROWS), span(4 * D + HALF, HALF)].T),
    }

    def extra():
        mine, theirs = la[GAINS, span(0, D)], ola[GAINS, span(0, D)]
        theirs = jnp.concatenate([theirs[:, UPPER], theirs[:, LOWER]], axis=1)
        columns = []
        for at in range(2):
            matrix = pa[at]
            first = dot(mine, matrix[:D]) + dot(theirs, matrix[:D])
            second = dot(mine, matrix[D:]) + dot(theirs, matrix[D:])
            columns.append(first[0:1] + first[2:3] + second[1:2] + second[3:4])
        rows = jnp.concatenate(columns + [jnp.zeros((PAD - 2, HALF), FULL)], axis=0)
        return z_first(rows.T).astype(LOW)

    la_rows, ola_rows = la.at[span(0, ROWS), :], ola.at[span(0, ROWS), :]
    products(copies, QKV_PLAN, left.get, lambda name: (la_rows, ola_rows), (stage_y, stage_z), outs, extra)
    copies.finish()


def run_grad_attend(late, other_late, own, pack):
    scratch = [vmem(ROWS + 16, LATE)] * 2 + [vmem(ROWS, 4 * HALF), vmem(2, 2 * D, HALF)]
    scratch += [vmem(HALF, width) for width in widths_of(QKV_PLAN)]
    operands = [late, other_late, own, pack]
    outs = call(kernel_grad_attend, operands, 0, grad_outs(QKV_PLAN), scratch, 5 + 8 * 4, 0)
    return outs[:5], outs[5:]


def hop(block, axis, step):
    count = lax.axis_size(axis)
    return lax.ppermute(block, axis, [(at, (at + step) % count) for at in range(count)])


def gather_near(block, axis):
    pair = jnp.concatenate([block, hop(block, "xh", 1)])
    ahead = hop(pair, axis, -1)
    behind = hop(pair, axis, 1)
    across = hop(pair, axis, 2)
    return jnp.concatenate([pair, ahead, across, behind])


def gather_far(whole, behind, ahead, axis):
    low = hop(behind[: PART // 2], axis, 1)
    high = hop(ahead[PART // 2 :], axis, -1)
    own = [whole, ahead, low, high, behind]
    return own + [hop(piece, "core", 1) for piece in own]


def total(*terms):
    result = terms[0].astype(FULL)
    for term in terms[1:]:
        result = result + term.astype(FULL)
    return result


def scatter_begin(blocks, axis):
    return hop(blocks[1], axis, 1), hop(blocks[2], axis, -1)


def scatter_sums(blocks, begun):
    half = PART // 2
    return total(blocks[3], begun[0][:half]).astype(LOW), total(blocks[4], begun[1][:half]).astype(LOW)


def scatter_main(sums, axis):
    return hop(sums[0], axis, 1), hop(sums[1], axis, -1)


def scatter_halves(blocks, begun, main):
    half = PART // 2
    low, high = [], []
    for block, (ahead, behind), (main_low, main_high) in zip(blocks, begun, main):
        low.append(total(block[0][:half], behind[half:], main_low))
        high.append(total(block[0][half:], ahead[half:], main_high))
    return jnp.concatenate(low, axis=1), jnp.concatenate(high, axis=1)


def scatter_end(low, high, axis):
    one = hop(low[RUN:].astype(LOW), axis, 1)
    two = hop(high[:RUN].astype(LOW), axis, 2)
    three = hop(high[RUN:].astype(LOW), axis, -1)
    low = low[:RUN].astype(LOW)
    other = hop(total(low[BLOCK:], one[BLOCK:], two[BLOCK:], three[BLOCK:]).astype(LOW), "xh", 1)
    return total(low[:BLOCK], one[:BLOCK], two[:BLOCK], three[:BLOCK], other)


def natural_of(rel, run, at):
    lane = rel % run
    rel = rel // run
    xx = (rel % NX + at[2]) % NX
    zz = (rel // NX % NZ + at[1]) % NZ
    yy = (rel // (NX * NZ) % NY + at[0]) % NY
    cc = (rel // (NX * NZ * NY) + at[3]) % NC
    return (((yy * NZ + zz) * NX + xx) * NC + cc) * run + lane


def place_matrix(at):
    natural = natural_of(jnp.arange(D), BLOCK, at)
    return (jnp.arange(D)[:, None] == natural[None, :]).astype(LOW)


def spread_matrix(at):
    natural = natural_of(jnp.arange(D), BLOCK, at)
    wanted = natural // (2 * BLOCK) * BLOCK + natural % BLOCK + jnp.arange(2)[:, None] * HALF
    return (natural[None, :, None] == wanted[:, None, :]).astype(LOW)


def pack_matrix(at):
    row = natural_of(jnp.arange(HALF), BLOCK, at)
    wanted = (row // BLOCK * (2 * BLOCK) + row % BLOCK)[None, :] + jnp.arange(2)[:, None] * BLOCK
    source = (jnp.arange(2)[:, None] * D + natural_of(jnp.arange(D), BLOCK, at)[None, :]).reshape(-1)
    return (wanted[:, None, :] == source[None, :, None]).astype(LOW)


def rotary_tables():
    half_dim = HD // 2
    rate_list = 10000.0 ** (-jnp.arange(half_dim, dtype=FULL) / half_dim)
    angles = jnp.arange(LENGTH, dtype=FULL)[:, None] * rate_list[None, :]
    cosine, sine = jnp.cos(angles), jnp.sin(angles)
    cosine = jnp.concatenate([cosine, cosine], axis=1)
    sine = jnp.concatenate([-sine, sine], axis=1)
    return jnp.tile(cosine, (COUNT, 1)), jnp.tile(sine, (COUNT, 1))


FF_PLAN = (
    (("h2", "wide", 0, FF), ("e", "early", HALF, FF // 2)),
    (("h2", "wide", FF, FF), ("e", "early", HALF + FF // 2, FF // 2)),
)
QKV_CUT = 17 * 128
QKV_PLAN = (
    (("h1", "late", 0, QKV_CUT),),
    (("h1", "late", QKV_CUT, 3 * D - QKV_CUT), ("o", "late", 3 * D, D), (None, None, 0, PAD)),
)


def local(boundary, w_qkv, w_out, w_gate_up, w_down_t, gains, memory, mem_index, mem_counts):
    section = lax.axis_index("section").astype(jnp.int32).reshape(1)
    core = lax.axis_index("core").astype(jnp.int32).reshape(1)
    gain_block = jnp.pad(gains.reshape(2, BLOCK).T.astype(LOW), ((0, 0), (0, PAD - 2)))
    first = jnp.concatenate([w_gate_up[0].astype(LOW), w_down_t[0, :, CUT:].astype(LOW)], axis=1)
    second = jnp.concatenate(
        [w_qkv[0].astype(LOW), w_out[0].astype(LOW), w_down_t[0, :, :CUT].astype(LOW), gain_block], axis=1
    )
    first = gather_near(first, "z")
    second = gather_near(second, "y")
    at = tuple(lax.axis_index(name) for name in DP)
    at, boundary, first, second = lax.optimization_barrier((at, boundary, first, second))
    first_behind, first_ahead = hop(first, "y", 1), hop(first, "y", -1)
    second_behind, second_ahead = hop(second, "z", 1), hop(second, "z", -1)
    place = place_matrix(at)
    pack = pack_matrix(at)
    spread = spread_matrix(at)
    cosine, sine = rotary_tables()
    edge = dot(boundary.reshape(ROWS, D), place, lax.Precision.HIGHEST)
    moved, prepared = lax.optimization_barrier(
        ((first_behind, first_ahead, second_behind, second_ahead), (place, pack, spread, cosine, sine, edge))
    )
    first_behind, first_ahead, second_behind, second_ahead = moved
    place, pack, spread, cosine, sine, edge = prepared
    first = gather_far(first, first_behind, first_ahead, "y")
    second = gather_far(second, second_behind, second_ahead, "z")
    picked = run_pick(memory, mem_index)

    sent, qkv, near, late, middle, early, gate_up, own, gain = run_first(
        section, core, edge, spread, cosine, sine, place, first, second
    )
    moved = lax.ppermute(sent, "section", [(0, 1)])
    early, late, own, result, sent, wide = run_last(
        section, mem_counts, moved, edge, gain, cosine, sine, place, picked, first, second, (early, late, own)
    )
    upstream = lax.ppermute(sent, "section", [(1, 0)])
    other_early = hop(early, "core", 1)
    wide, own = run_back_gate(section, upstream, gate_up, first, second, other_early, wide, own)
    other_wide = hop(wide, "core", 1)
    grad_middle, gain_part = run_back_ff(section, upstream, gain, middle, wide, first)
    gate_y, gate_z = run_grad_ff(early, other_early, wide, other_wide, own, grad_middle)
    begun_gate_y = scatter_begin(gate_y, "y")
    begun_gate_z = scatter_begin(gate_z, "z")
    late, own, result = run_back_attend(
        section, edge, gain, cosine, sine, place, qkv, near, grad_middle, gain_part, second, gate_z[0],
        (late, own, result),
    )
    other_late = hop(late, "core", 1)
    sums_y, sums_z = scatter_sums(gate_y, begun_gate_y), scatter_sums(gate_z, begun_gate_z)
    other_late, sums_y, sums_z = lax.optimization_barrier((other_late, sums_y, sums_z))
    main_gate_y, main_gate_z = scatter_main(sums_y, "y"), scatter_main(sums_z, "z")
    qkv_y, qkv_z = run_grad_attend(late, other_late, own, pack)
    begun_qkv_y = scatter_begin(qkv_y, "y")
    begun_qkv_z = scatter_begin(qkv_z, "z")
    result, main_gate_y, main_gate_z = lax.optimization_barrier((result, main_gate_y, main_gate_z))
    finals = dot(result, place.T, lax.Precision.HIGHEST).reshape(1, COUNT, LENGTH, D)
    main_qkv_y = scatter_main(scatter_sums(qkv_y, begun_qkv_y), "y")
    main_qkv_z = scatter_main(scatter_sums(qkv_z, begun_qkv_z), "z")
    low_y, high_y = scatter_halves((gate_y, qkv_y), (begun_gate_y, begun_qkv_y), (main_gate_y, main_qkv_y))
    low_z, high_z = scatter_halves((gate_z, qkv_z), (begun_gate_z, begun_qkv_z), (main_gate_z, main_qkv_z))
    y, z = scatter_end(low_y, high_y, "z"), scatter_end(low_z, high_z, "y")
    wide = widths_of(FF_PLAN)[0]
    gate_y, qkv_y, gate_z, qkv_z = y[:, :wide], y[:, wide:], z[:, :wide], z[:, wide:]
    cut = 3 * D - QKV_CUT
    return (
        finals,
        jnp.concatenate([qkv_y, qkv_z[:, :cut]], axis=1)[None],
        qkv_z[None, :, cut : cut + D],
        jnp.concatenate([gate_y[:, :FF], gate_z[:, :FF]], axis=1)[None],
        jnp.concatenate([gate_y[:, FF:], gate_z[:, FF:]], axis=1)[None],
        qkv_z[:, cut + D : cut + D + 2].T.reshape(1, -1),
    )


def solution(mesh):
    mesh = Mesh(mesh.devices.reshape(2, NY, NZ, NX, NC), ("section",) + DP)
    in_specs = (
        P("section", DP, None, None),
        P("section", DP, None),
        P("section", DP, None),
        P("section", DP, None),
        P("section", DP, None),
        P("section", DP),
        P(DP, None, None, None),
        P(DP, None, None),
        P(DP),
    )
    return jax.shard_map(local, mesh=mesh, in_specs=in_specs, out_specs=in_specs[:6], check_vma=False)
```

```python
import functools

import jax
import jax.numpy as jnp
from jax import lax
from jax.experimental import pallas as pl
from jax.experimental.pallas import tpu as pltpu
from jax.sharding import Mesh
from jax.sharding import PartitionSpec as P

MASKED = -1e30
EPSILON = 1e-06
LOW = jnp.bfloat16
FULL = jnp.float32
NY, NZ, NX, NC = 4, 4, 2, 2
DP = ("y", "z", "xh", "core")
D, HEADS, HD, FF = 1024, 8, 128, 2816
COUNT, LENGTH = 2, 128
ROWS = COUNT * LENGTH
BLOCK = 16
HALF = D // 2
PART = D // (NC * NY)
RUN = PART // NZ
PAD = 128
CUT = 2048
TILE = 256
VMEM_LIMIT = 62 * 1024 * 1024
SCALE = HD ** (-0.5)
HBM = pl.BlockSpec(memory_space=pltpu.HBM)
SMEM = pl.BlockSpec(memory_space=pltpu.SMEM)


def dot(left, right, precision=None):
    return jnp.dot(left, right, preferred_element_type=FULL, precision=precision)


def dot_nt(left, right):
    return lax.dot_general(left, right, (((1,), (1,)), ((), ())), preferred_element_type=FULL)


def dot_tn(left, right):
    return lax.dot_general(left, right, (((0,), (0,)), ((), ())), preferred_element_type=FULL)


def unit_rows(stream):
    inverse_rms = lax.rsqrt(jnp.mean(stream * stream, axis=-1, keepdims=True) + EPSILON)
    return stream * inverse_rms, inverse_rms


def turn(rows, cosine, sine):
    return rows * cosine + pltpu.roll(rows, HD // 2, 1) * sine


def span(start, size):
    return slice(start, start + size)


def no_wait(start):
    pass


def attend_forward(x, gain, cosine, sine, w_qkv, qkv, plain, wait):
    unit, _ = unit_rows(x[...])
    normed = (unit * gain[0:1, :]).astype(LOW)
    for start in range(0, 3 * D, TILE):
        wait(start)
        joined = dot(normed, w_qkv[:, span(start, TILE)])
        for at in range(start, start + TILE, HD):
            head = joined[:, span(at - start, HD)]
            if at < 2 * D:
                qkv[:, span(at, HD)] = turn(head, cosine[...], sine[...]).astype(LOW)
            else:
                qkv[:, span(at, HD)] = head.astype(LOW)
            if plain is not None and at < D:
                plain[:, span(at, HD)] = head.astype(LOW)


def causal():
    return lax.broadcasted_iota(jnp.int32, (LENGTH, LENGTH), 0) >= lax.broadcasted_iota(jnp.int32, (LENGTH, LENGTH), 1)


def heads_forward(qkv, plain, picked, counts, near, far, attended):
    keep = causal()
    every = range(HEADS)
    for seq in range(COUNT):
        rows = span(seq * LENGTH, LENGTH)
        at = [span(head * HD, HD) for head in every]
        scores = [dot_nt(qkv[rows, at[h]], qkv[rows, span(D + h * HD, HD)]) for h in every]
        scores = [jnp.where(keep, score * SCALE, MASKED) for score in scores]
        tops = [jnp.max(score, axis=-1, keepdims=True) for score in scores]
        if picked is not None:
            valid = lax.broadcasted_iota(jnp.int32, (LENGTH, LENGTH), 1) < counts[seq]
            memory = [dot_nt(plain[rows, at[h]], picked[0, seq, h]) for h in every]
            memory = [jnp.where(valid, score * SCALE, MASKED) for score in memory]
            tops = [jnp.maximum(top, jnp.max(score, axis=-1, keepdims=True)) for top, score in zip(tops, memory)]
        scores = [jnp.exp(score - top) for score, top in zip(scores, tops)]
        totals = [jnp.sum(score, axis=-1, keepdims=True) for score in scores]
        if picked is not None:
            memory = [jnp.exp(score - top) for score, top in zip(memory, tops)]
            totals = [part + jnp.sum(score, axis=-1, keepdims=True) for part, score in zip(totals, memory)]
        scales = [1.0 / part for part in totals]
        scores = [(score * scale).astype(LOW) for score, scale in zip(scores, scales)]
        values = [qkv[rows, span(2 * D + h * HD, HD)] for h in every]
        for h in every:
            near[seq * HEADS + h] = scores[h]
        if picked is not None:
            memory = [(score * scale).astype(LOW) for score, scale in zip(memory, scales)]
            for h in every:
                far[seq * HEADS + h] = memory[h]
            scores = [jnp.concatenate(both, axis=1) for both in zip(scores, memory)]
            values = [jnp.concatenate([values[h], picked[1, seq, h]], axis=0) for h in every]
        results = [dot(score, value) for score, value in zip(scores, values)]
        for h in every:
            attended[rows, at[h]] = results[h].astype(LOW)


def out_forward(x, attended, place, w_out, attended_rel, middle):
    attended_rel[...] = dot(attended[...], place[...]).astype(LOW)
    for start in range(0, D, 2 * TILE):
        out = dot(attended_rel[...], w_out[:, span(start, 2 * TILE)])
        high = out.astype(LOW)
        low = (out - high.astype(FULL)).astype(LOW)
        shard = place[span(start, 2 * TILE), :]
        moved = dot(high, shard) + dot(low, shard)
        middle[...] = (x[...] if start == 0 else middle[...]) + moved


def ff_forward(middle, gain, w_gate_up, normed_two, gate_up, hidden):
    unit, _ = unit_rows(middle[...])
    normed_two[...] = (unit * gain[1:2, :]).astype(LOW)
    for start in range(0, FF, TILE):
        gate = dot(normed_two[...], w_gate_up[:, span(start, TILE)])
        up = dot(normed_two[...], w_gate_up[:, span(FF + start, TILE)])
        gate_up[:, span(start, TILE)] = gate.astype(LOW)
        gate_up[:, span(FF + start, TILE)] = up.astype(LOW)
        hidden[:, span(start, TILE)] = (gate * jax.nn.sigmoid(gate) * up).astype(LOW)


def down_forward(middle, hidden, w_down, result):
    for start in range(0, D, TILE):
        columns = span(start, TILE)
        result[:, columns] = (middle[:, columns] + dot_nt(hidden[...], w_down[columns, :])).astype(result.dtype)


def norm_back(grad, unit, inverse_rms, gain):
    weighted = grad * gain
    return inverse_rms * (weighted - unit * jnp.mean(weighted * unit, axis=-1, keepdims=True))


def gate_backward(upstream_low, w_down, gate_up, grad_ff, wait=no_wait):
    for start in range(0, FF, TILE):
        wait(start)
        grad_hidden = dot(upstream_low[...], w_down[:, span(start, TILE)])
        gate, up = gate_up[:, span(start, TILE)].astype(FULL), gate_up[:, span(FF + start, TILE)].astype(FULL)
        sigmoid_gate = jax.nn.sigmoid(gate)
        grad_gate = grad_hidden * up * sigmoid_gate * (1.0 + gate * (1.0 - sigmoid_gate))
        grad_ff[:, span(start, TILE)] = grad_gate.astype(LOW)
        grad_ff[:, span(FF + start, TILE)] = (grad_hidden * (gate * sigmoid_gate)).astype(LOW)


def ff_backward(upstream, middle, gain, w_gate_up, grad_ff, grad_middle, gain_grad, wait=no_wait):
    for start in range(0, D, TILE):
        wait(start)
        grad_middle[:, span(start, TILE)] = dot_nt(grad_ff[...], w_gate_up[span(start, TILE), :])
    unit, inverse_rms = unit_rows(middle[...])
    grad = grad_middle[...]
    gain_grad[1:2, :] = jnp.sum(grad * unit, axis=0, keepdims=True)
    grad_middle[...] = upstream[...].astype(FULL) + norm_back(grad, unit, inverse_rms, gain[1:2, :])


def out_backward(grad_middle, place, w_out, branch, grad_attended):
    branch[...] = dot_nt(grad_middle[...].astype(LOW), place[...]).astype(LOW)
    grad_rel = dot_nt(branch[...], w_out[...]).astype(LOW)
    grad_attended[...] = dot_nt(grad_rel, place[...]).astype(LOW)


def heads_backward(qkv, picked, near, far, grad_attended, cosine, sine, grad_joined):
    every = range(HEADS)
    for seq in range(COUNT):
        rows = span(seq * LENGTH, LENGTH)
        cos, sin = cosine[rows, :], -sine[rows, :]
        at = [span(head * HD, HD) for head in every]
        grad_outs = [grad_attended[rows, at[h]] for h in every]
        probs = [near[seq * HEADS + h] for h in every]
        values = [qkv[rows, span(2 * D + h * HD, HD)] for h in every]
        grad_values = [dot_tn(prob, grad_out) for prob, grad_out in zip(probs, grad_outs)]
        if picked is not None:
            probs = [jnp.concatenate([probs[h], far[seq * HEADS + h]], axis=1) for h in every]
            values = [jnp.concatenate([values[h], picked[1, seq, h]], axis=0) for h in every]
        probs = [prob.astype(FULL) for prob in probs]
        grads = [dot_nt(grad_out, value) for grad_out, value in zip(grad_outs, values)]
        deltas = [jnp.sum(prob * grad, axis=-1, keepdims=True) for prob, grad in zip(probs, grads)]
        grads = [(prob * (grad - delta)).astype(LOW) for prob, grad, delta in zip(probs, grads, deltas)]
        for h in every:
            grad_joined[rows, span(2 * D + h * HD, HD)] = grad_values[h].astype(LOW)
        queries = [dot(grads[h][:, :LENGTH], qkv[rows, span(D + h * HD, HD)]) * SCALE for h in every]
        keys = [dot_tn(grads[h][:, :LENGTH], qkv[rows, at[h]]) * SCALE for h in every]
        queries = [turn(query, cos, sin) for query in queries]
        keys = [turn(key, cos, sin) for key in keys]
        if picked is not None:
            queries = [queries[h] + dot(grads[h][:, LENGTH:], picked[0, seq, h]) * SCALE for h in every]
        for h in every:
            grad_joined[rows, at[h]] = queries[h].astype(LOW)
            grad_joined[rows, span(D + h * HD, HD)] = keys[h].astype(LOW)


def attend_backward(x, gain, w_qkv, grad_joined, grad_middle, normed, result, gain_grad):
    for start in range(0, D, TILE):
        result[:, span(start, TILE)] = dot_nt(grad_joined[...], w_qkv[span(start, TILE), :])
    unit, inverse_rms = unit_rows(x[...])
    normed[...] = (unit * gain[0:1, :]).astype(LOW)
    grad = result[...]
    gain_grad[0:1, :] = jnp.sum(grad * unit, axis=0, keepdims=True)
    result[...] = grad_middle[...] + norm_back(grad, unit, inverse_rms, gain[0:1, :])


EARLY = HALF + FF
WIDE = 2 * FF + HALF
LATE = 4 * D + 2 * HALF
GAINS = span(ROWS, 16)
LOWER, UPPER = span(0, HALF), span(HALF, HALF)
OWN = {name: span(at * HALF, HALF) for at, name in enumerate(("h2", "e", "h1", "o"))}


class Copies:
    def __init__(self, semaphores):
        self.semaphores, self.used, self.groups = semaphores, 0, {}

    def copy(self, at, source, target):
        source, target = (view[0].at[view[1]] if isinstance(view, tuple) else view for view in (source, target))
        return pltpu.make_async_copy(source, target, self.semaphores.at[at])

    def start(self, name, source, target):
        self.copy(self.used, source, target).start()
        self.groups.setdefault(name, []).append((self.used, source, target))
        self.used += 1

    def wait(self, *names):
        for name in names:
            for copy in self.groups.pop(name):
                self.copy(*copy).wait()

    def finish(self):
        self.wait(*list(self.groups))


def y_runs():
    return [(0, (0, PART), 0), (1, (0, PART), PART), (2, (0, PART // 2), 2 * PART)] + [
        (3, (0, PART // 2), 2 * PART + PART // 2),
        (4, (0, PART), 3 * PART),
    ]


def z_runs():
    runs = []
    for piece, dz, low, high in ((0, 0, 0, 4), (1, 1, 0, 4), (2, 2, 0, 2), (3, 2, 2, 4), (4, 3, 0, 4)):
        runs += [(piece, ((dy - low) * RUN, RUN), dy * PART + dz * RUN) for dy in range(low, high)]
    return runs


def load(copies, name, pieces, runs, columns, target, target_columns):
    for core in range(NC):
        for piece, (low, size), row in runs:
            source = pieces[core * 5 + piece], (span(low, size), columns)
            copies.start(name, source, (target, (span(core * HALF + row, size), target_columns)))


def load_qkv(copies, second, target):
    for at in range(3):
        columns = span(at * D, D)
        load(copies, f"qkv{at * D}", second, z_runs(), columns, target, columns)


def wait_qkv(copies):
    return lambda start: copies.wait(f"qkv{start}") if start % D == 0 else None


def load_out(copies, second, target):
    load(copies, "out", second, z_runs(), span(3 * D, D), target, span(0, D))


def load_gains(copies, second, target):
    load(copies, "gains", second, z_runs(), span(4 * D + CUT, PAD), target, span(0, PAD))


def load_gate(copies, first, target):
    for core in range(NC):
        for piece, (low, size), row in y_runs():
            row += core * HALF
            source = first[core * 5 + piece], (span(low, size), span(0, 2 * FF))
            copies.start(f"gate{row // TILE * TILE}", source, (target, (span(row, size), span(0, 2 * FF))))


GATE = tuple(f"gate{at}" for at in range(0, D, TILE))
DOWN = tuple(f"down{at}" for at in range(0, FF, D))


def load_down(copies, first, second, target, also=None):
    for start in range(0, FF, D):
        name = f"down{start}"
        if start < CUT:
            load(copies, name, second, z_runs(), span(4 * D + start, D), target, span(start, D))
        else:
            load(copies, name, first, y_runs(), span(2 * FF, FF - CUT), target, span(CUT, FF - CUT))
        if also:
            also(name, start, min(D, FF - start))


def kernel_first(section, core, *refs):
    (x, spread, cosine, sine, place), refs = refs[:5], refs[5:]
    first, second, refs = refs[:10], refs[10:20], refs[20:]
    (sent_o, qkv_o, near_o, late_o, middle_o, early_o, gate_up_o, own_o, gain_o), refs = refs[:9], refs[9:]
    xs, gains, cos, sin, places, w_qkv, w_out, w_gate, w_down = refs[:9]
    qkv, near, attended, attended_rel, middle, normed_two, gate_up, hidden, sent, spreads, gain_rows, semaphores = refs[9:]

    copies = Copies(semaphores)
    load_gains(copies, second, gain_rows)
    copies.start("gains", spread, spreads)

    @pl.when(section[0] == 0)
    def _():
        for source, target in ((x, xs), (cosine, cos), (sine, sin)):
            copies.start("small", source, target)
        load_qkv(copies, second, w_qkv)
        copies.start("place", place, places)
        load_out(copies, second, w_out)
        load_gate(copies, first, w_gate)
        load_down(copies, first, second, w_down)

    copies.wait("gains")
    rows = gain_rows[...].astype(FULL).T[:8].astype(LOW)
    low = lax.broadcasted_iota(jnp.int32, (1, D), 1) < HALF
    straight = jnp.logical_xor(low, core[0] == 1)
    for at in range(2):
        picked = dot(rows, spreads[at])
        gains[at : at + 1, :] = jnp.where(straight, picked[0:1], picked[1:2])
    copies.start("gain", gains, gain_o)

    @pl.when(section[0] == 0)
    def _():
        copies.wait("small")
        attend_forward(xs, gains, cos, sin, w_qkv, qkv, None, wait_qkv(copies))
        copies.start("done", qkv, qkv_o)
        heads_forward(qkv, None, None, None, near, None, attended)
        copies.start("done", near, near_o)
        copies.wait("place", "out")
        out_forward(xs, attended, places, w_out, attended_rel, middle)
        copies.start("done", attended_rel.at[:, LOWER], own_o.at[:, OWN["o"]])
        copies.start("done", attended_rel.at[:, UPPER], late_o.at[span(0, ROWS), span(4 * D + HALF, HALF)])
        copies.start("done", middle, middle_o)
        copies.wait(*GATE)
        ff_forward(middle, gains, w_gate, normed_two, gate_up, hidden)
        copies.start("done", normed_two.at[:, LOWER], own_o.at[:, OWN["h2"]])
        copies.start("done", normed_two.at[:, UPPER], early_o.at[:, LOWER])
        copies.start("done", gate_up, gate_up_o)
        copies.start("done", hidden, early_o.at[:, span(HALF, FF)])
        copies.wait(*DOWN)
        down_forward(middle, hidden, w_down, sent)
        copies.start("done", sent, sent_o)
        copies.wait("done")

    copies.wait("gain")


def two_parts(gain_grad):
    full = gain_grad[...]
    high = full.astype(LOW).astype(FULL)
    return jnp.concatenate([high, full - high, jnp.zeros((12, D), FULL)], axis=0).astype(LOW)


def kernel_last(section, counts, *refs):
    (x_low, upstream, gain, cosine, sine, place, picked), refs = refs[:7], refs[7:]
    first, second, refs = refs[:10], refs[10:20], refs[20:]
    refs = refs[3:]
    (early_o, late_o, own_o, result_o, sent_o, grad_ff_o), refs = refs[:6], refs[6:]
    xl, ups, up_low, gains, cos, sin, places, picks, w_qkv, w_out, w_gate, w_down = refs[:12]
    xs, qkv, plain, near, far, attended, attended_rel, middle, normed_two, gate_up, hidden, result = refs[12:24]
    grad_ff, grad_middle, branch, grad_joined, normed, gain_grad, gain_rows, semaphores = refs[24:]

    @pl.when(section[0] == 1)
    def _():
        copies = Copies(semaphores)
        for source, target in ((x_low, xl), (gain, gains), (cosine, cos), (sine, sin)):
            copies.start("small", source, target)
        load_qkv(copies, second, w_qkv)
        copies.start("picks", picked, picks)
        copies.start("place", place, places)
        load_out(copies, second, w_out)
        load_gate(copies, first, w_gate)
        load_down(copies, first, second, w_down)
        copies.start("up", upstream, ups)
        copies.wait("small")
        xs[...] = xl[...].astype(FULL)
        attend_forward(xs, gains, cos, sin, w_qkv, qkv, plain, wait_qkv(copies))
        copies.wait("picks")
        heads_forward(qkv, plain, picks, counts, near, far, attended)
        copies.wait("place", "out")
        out_forward(xs, attended, places, w_out, attended_rel, middle)
        copies.start("done", attended_rel.at[:, LOWER], own_o.at[:, OWN["o"]])
        copies.start("done", attended_rel.at[:, UPPER], late_o.at[span(0, ROWS), span(4 * D + HALF, HALF)])
        copies.wait(*GATE)
        ff_forward(middle, gains, w_gate, normed_two, gate_up, hidden)
        copies.start("done", normed_two.at[:, LOWER], own_o.at[:, OWN["h2"]])
        copies.start("done", normed_two.at[:, UPPER], early_o.at[:, LOWER])
        copies.start("done", hidden, early_o.at[:, span(HALF, FF)])
        copies.wait(*DOWN, "up")
        up_low[...] = ups[...].astype(LOW)
        copies.start("done", up_low.at[:, LOWER], own_o.at[:, OWN["e"]])
        copies.start("done", up_low.at[:, UPPER], grad_ff_o.at[:, span(2 * FF, HALF)])
        down_forward(middle, hidden, w_down, result)
        copies.start("result", result, result_o)
        gate_backward(up_low, w_down, gate_up, grad_ff)
        copies.start("done", grad_ff, grad_ff_o.at[:, span(0, 2 * FF)])
        ff_backward(ups, middle, gains, w_gate, grad_ff, grad_middle, gain_grad)
        out_backward(grad_middle, places, w_out, branch, attended)
        copies.start("done", branch, late_o.at[span(0, ROWS), span(3 * D, D)])
        heads_backward(qkv, picks, near, far, attended, cos, sin, grad_joined)
        copies.start("done", grad_joined, late_o.at[span(0, ROWS), span(0, 3 * D)])
        copies.wait("result")
        attend_backward(xs, gains, w_qkv, grad_joined, grad_middle, normed, result, gain_grad)
        xl[...] = result[...].astype(LOW)
        copies.start("done", xl, sent_o)
        copies.start("done", normed.at[:, LOWER], own_o.at[:, OWN["h1"]])
        copies.start("done", normed.at[:, UPPER], late_o.at[span(0, ROWS), span(4 * D, HALF)])
        gain_rows[...] = two_parts(gain_grad)
        copies.start("done", gain_rows, late_o.at[GAINS, span(0, D)])
        copies.finish()


def kernel_back_gate(section, *refs):
    (upstream, gate_up), refs = refs[:2], refs[2:]
    first, second, refs = refs[:10], refs[10:20], refs[20:]
    refs = refs[3:]
    (grad_ff_o, own_o), refs = refs[:2], refs[2:]
    ups, gate_ups, w_down, grad_ff, semaphores = refs

    @pl.when(section[0] == 0)
    def _():
        copies = Copies(semaphores)
        copies.start("up", upstream, ups)

        def saved(name, start, size):
            for columns in (span(start, size), span(FF + start, size)):
                copies.start(name, gate_up.at[:, columns], gate_ups.at[:, columns])

        load_down(copies, first, second, w_down, saved)
        copies.wait("up")
        copies.start("done", ups.at[:, LOWER], own_o.at[:, OWN["e"]])
        copies.start("done", ups.at[:, UPPER], grad_ff_o.at[:, span(2 * FF, HALF)])
        gate_backward(
            ups, w_down, gate_ups, grad_ff, lambda start: copies.wait(f"down{start}") if start % D == 0 else None
        )
        copies.start("done", grad_ff, grad_ff_o.at[:, span(0, 2 * FF)])
        copies.finish()


def kernel_back_ff(section, *refs):
    (upstream, gain, middle, grad_ff), refs = refs[:4], refs[4:]
    first, refs = refs[:10], refs[10:]
    (grad_middle_o, gain_grad_o), refs = refs[:2], refs[2:]
    ups, gains, mid, grad_ffs, w_gate, grad_middle, gain_grad, semaphores = refs

    @pl.when(section[0] == 0)
    def _():
        copies = Copies(semaphores)
        copies.start("first", grad_ff.at[:, span(0, 2 * FF)], grad_ffs)
        load_gate(copies, first, w_gate)
        copies.start("late", upstream, ups)
        copies.start("late", middle, mid)
        copies.start("late", gain, gains)
        copies.wait("first")

        def wait(start):
            copies.wait(f"gate{start}")
            if start == D - TILE:
                copies.wait("late")

        ff_backward(ups, mid, gains, w_gate, grad_ffs, grad_middle, gain_grad, wait)
        copies.start("done", grad_middle, grad_middle_o)
        copies.start("done", gain_grad, gain_grad_o)
        copies.finish()


def kernel_back_attend(section, *refs):
    (x, gain, cosine, sine, place, qkv, near, grad_middle, gain_part), refs = refs[:9], refs[9:]
    second, refs = refs[:10], refs[11:]
    (late_o, own_o, result_o), refs = refs[3:6], refs[6:]
    xs, gains, cos, sin, places, qkvs, nears, grad_mid, w_qkv, w_out = refs[:10]
    grad_attended, branch, grad_joined, normed, result, gain_grad, gain_rows, semaphores = refs[10:]

    @pl.when(section[0] == 0)
    def _():
        copies = Copies(semaphores)
        copies.start("mid", grad_middle, grad_mid)
        copies.start("mid", place, places)
        load_out(copies, second, w_out)
        for source, target in ((qkv, qkvs), (near, nears), (cosine, cos), (sine, sin)):
            copies.start("saved", source, target)
        load_qkv(copies, second, w_qkv)
        for source, target in ((x, xs), (gain, gains), (gain_part, gain_grad)):
            copies.start("late", source, target)
        copies.wait("mid", "out")
        out_backward(grad_mid, places, w_out, branch, grad_attended)
        copies.start("done", branch, late_o.at[span(0, ROWS), span(3 * D, D)])
        copies.wait("saved")
        heads_backward(qkvs, None, nears, None, grad_attended, cos, sin, grad_joined)
        copies.start("done", grad_joined, late_o.at[span(0, ROWS), span(0, 3 * D)])
        copies.wait("qkv0", f"qkv{D}", f"qkv{2 * D}", "late")
        attend_backward(xs, gains, w_qkv, grad_joined, grad_mid, normed, result, gain_grad)
        copies.start("done", result, result_o)
        copies.start("done", normed.at[:, LOWER], own_o.at[:, OWN["h1"]])
        copies.start("done", normed.at[:, UPPER], late_o.at[span(0, ROWS), span(4 * D, HALF)])
        gain_rows[...] = two_parts(gain_grad)
        copies.start("done", gain_rows, late_o.at[GAINS, span(0, D)])
        copies.finish()


def shape(*dims, dtype=LOW):
    return jax.ShapeDtypeStruct(dims, dtype)


def vmem(*dims, dtype=LOW):
    return pltpu.VMEM(dims, dtype)


Y_COPIES, Z_COPIES = 2 * 5, 2 * 16
QKV_COPIES, DOWN_COPIES = 3 * Z_COPIES, 2 * Z_COPIES + Y_COPIES
W_QKV, W_OUT, W_GATE, W_DOWN = vmem(D, 3 * D), vmem(D, D), vmem(D, 2 * FF), vmem(D, FF)


def call(kernel, operands, scalars, outs, scratch, copies, aliases=None, cost=1000):
    return pl.pallas_call(
        kernel,
        out_shape=outs,
        in_specs=[SMEM] * scalars + [HBM] * (len(operands) - scalars),
        out_specs=[HBM] * len(outs),
        scratch_shapes=list(scratch) + [pltpu.SemaphoreType.DMA((copies,))],
        input_output_aliases=aliases or {},
        compiler_params=pltpu.CompilerParams(vmem_limit_bytes=VMEM_LIMIT),
        cost_estimate=pl.CostEstimate(flops=cost, bytes_accessed=cost, transcendentals=0),
    )(*operands)


def run_first(section, core, x, spread, cosine, sine, place, first, second):
    outs = [
        shape(ROWS, D), shape(ROWS, 3 * D), shape(COUNT * HEADS, LENGTH, LENGTH), shape(ROWS + 16, LATE),
        shape(ROWS, D, dtype=FULL), shape(ROWS, EARLY), shape(ROWS, 2 * FF), shape(ROWS, 4 * HALF),
        shape(2, D, dtype=FULL),
    ]
    scratch = [vmem(ROWS, D, dtype=FULL), vmem(2, D, dtype=FULL), vmem(ROWS, HD, dtype=FULL), vmem(ROWS, HD, dtype=FULL)]
    scratch += [vmem(D, D), W_QKV, W_OUT, W_GATE, W_DOWN]
    scratch += [vmem(ROWS, 3 * D), vmem(COUNT * HEADS, LENGTH, LENGTH), vmem(ROWS, D), vmem(ROWS, D)]
    scratch += [vmem(ROWS, D, dtype=FULL), vmem(ROWS, D), vmem(ROWS, 2 * FF), vmem(ROWS, FF), vmem(ROWS, D)]
    scratch += [vmem(2, D, D), vmem(D, PAD)]
    operands = [section, core, x, spread, cosine, sine, place, *first, *second]
    return call(kernel_first, operands, 2, outs, scratch, 24 + Y_COPIES + 2 * Z_COPIES + QKV_COPIES + DOWN_COPIES)


def run_last(section, counts, x_low, upstream, gain, cosine, sine, place, picked, first, second, kept):
    outs = [shape(ROWS, EARLY), shape(ROWS + 16, LATE), shape(ROWS, 4 * HALF), shape(ROWS, D, dtype=FULL)]
    outs += [shape(ROWS, D), shape(ROWS, WIDE)]
    scratch = [vmem(ROWS, D), vmem(ROWS, D, dtype=FULL), vmem(ROWS, D), vmem(2, D, dtype=FULL)]
    scratch += [vmem(ROWS, HD, dtype=FULL), vmem(ROWS, HD, dtype=FULL), vmem(D, D), vmem(2, COUNT, HEADS, LENGTH, HD)]
    scratch += [W_QKV, W_OUT, W_GATE, W_DOWN]
    scratch += [vmem(ROWS, D, dtype=FULL), vmem(ROWS, 3 * D), vmem(ROWS, D)]
    scratch += [vmem(COUNT * HEADS, LENGTH, LENGTH)] * 2
    scratch += [vmem(ROWS, D), vmem(ROWS, D), vmem(ROWS, D, dtype=FULL), vmem(ROWS, D), vmem(ROWS, 2 * FF)]
    scratch += [vmem(ROWS, FF), vmem(ROWS, D, dtype=FULL)]
    scratch += [vmem(ROWS, 2 * FF), vmem(ROWS, D, dtype=FULL), vmem(ROWS, D), vmem(ROWS, 3 * D), vmem(ROWS, D)]
    scratch += [vmem(2, D, dtype=FULL), vmem(16, D)]
    operands = [section, counts, x_low, upstream, gain, cosine, sine, place, picked, *first, *second, *kept]
    aliases = {len(operands) - 3 + i: i for i in range(3)}
    return call(kernel_last, operands, 2, outs, scratch, 24 + Y_COPIES + Z_COPIES + QKV_COPIES + DOWN_COPIES, aliases)


def run_back_gate(section, upstream, gate_up, first, second, early, grad_ff, own):
    outs = [shape(ROWS, WIDE), shape(ROWS, 4 * HALF)]
    scratch = [vmem(ROWS, D), vmem(ROWS, 2 * FF), W_DOWN, vmem(ROWS, 2 * FF)]
    operands = [section, upstream, gate_up, *first, *second, early, grad_ff, own]
    at = len(operands) - 2
    return call(
        kernel_back_gate, operands, 1, outs, scratch, 16 + DOWN_COPIES, {at: 0, at + 1: 1}
    )


def run_back_ff(section, upstream, gain, middle, grad_ff, first):
    outs = [shape(ROWS, D, dtype=FULL), shape(2, D, dtype=FULL)]
    scratch = [vmem(ROWS, D), vmem(2, D, dtype=FULL), vmem(ROWS, D, dtype=FULL), vmem(ROWS, 2 * FF)]
    scratch += [W_GATE, vmem(ROWS, D, dtype=FULL), vmem(2, D, dtype=FULL)]
    operands = [section, upstream, gain, middle, grad_ff, *first]
    return call(kernel_back_ff, operands, 1, outs, scratch, 10 + Y_COPIES)


def run_back_attend(section, x, gain, cosine, sine, place, qkv, near, grad_middle, gain_part, second, after, kept):
    outs = [shape(ROWS + 16, LATE), shape(ROWS, 4 * HALF), shape(ROWS, D, dtype=FULL)]
    scratch = [vmem(ROWS, D, dtype=FULL), vmem(2, D, dtype=FULL), vmem(ROWS, HD, dtype=FULL), vmem(ROWS, HD, dtype=FULL)]
    scratch += [vmem(D, D), vmem(ROWS, 3 * D), vmem(COUNT * HEADS, LENGTH, LENGTH), vmem(ROWS, D, dtype=FULL)]
    scratch += [W_QKV, W_OUT, vmem(ROWS, D), vmem(ROWS, D), vmem(ROWS, 3 * D), vmem(ROWS, D), vmem(ROWS, D, dtype=FULL)]
    scratch += [vmem(2, D, dtype=FULL), vmem(16, D)]
    operands = [section, x, gain, cosine, sine, place, qkv, near, grad_middle, gain_part, *second, after, *kept]
    at = len(operands) - 3
    return call(
        kernel_back_attend, operands, 1, outs, scratch, 20 + Z_COPIES + QKV_COPIES, {at + i: i for i in range(3)}
    )


def pick_kernel(memory, index, out):
    chosen = index[0, 0]
    hot = (lax.broadcasted_iota(jnp.int32, (memory.shape[2], LENGTH), 0) == chosen).astype(FULL).astype(LOW)
    for kind in range(2):
        out[kind, 0, 0] = dot_tn(hot, memory[0, kind]).astype(LOW)


def run_pick(memory, mem_index):
    slots = memory.shape[2]
    return pl.pallas_call(
        pick_kernel,
        grid=(COUNT, HEADS),
        in_specs=[
            pl.BlockSpec((1, 2, slots, HD), lambda n, h: (n, 0, 0, h)),
            pl.BlockSpec((1, 1, 1, LENGTH), lambda n, h: (n, h, 0, 0)),
        ],
        out_specs=pl.BlockSpec((2, 1, 1, LENGTH, HD), lambda n, h: (0, n, h, 0, 0)),
        out_shape=shape(2, COUNT, HEADS, LENGTH, HD),
    )(memory, mem_index.reshape(COUNT, HEADS, 1, LENGTH))


def z_first(rows):
    return jnp.concatenate([rows[span(dy * PART + dz * RUN, RUN), :] for dz in range(NZ) for dy in range(NY)], axis=0)


HALVES = PART // 2
QKV_CUT = 17 * 128
N_FF, N_Y, N_Z = FF + FF // 2, QKV_CUT, 3 * D - QKV_CUT + D + PAD
FF_PARTS = (
    (0, "e", "early", HALF, FF // 2, FF), (1, "e", "early", HALF + FF // 2, FF // 2, FF),
    (0, "h2", "wide", 0, FF, 0), (1, "h2", "wide", FF, FF, 0),
)
QKV_PARTS = (
    (1, "o", "late", 3 * D, D, 3 * D - QKV_CUT), (0, "h1", "late", 0, QKV_CUT, 0),
    (1, "h1", "late", QKV_CUT, 3 * D - QKV_CUT, 0), (1, None, None, 0, PAD, 3 * D - QKV_CUT + D),
)


def put(copies, staged, columns, targets):
    for source, (ref, rows, shift) in targets.items():
        at = span(columns.start + shift, columns.stop - columns.start)
        copies.start("done", staged.at[span(source * HALVES, HALVES), columns], ref.at[rows, at])


def products(copies, parts, sides, rights, stages, targets, extra=None):
    for z, left, right, first, size, at in parts:
        stage = stages[z]
        if left is None:
            stage[:, span(at, size)] = extra()
        else:
            own, other = sides(left)
            if z:
                own, other = z_first(own), z_first(other)
            mine, theirs = rights(right, first)
            for start in range(0, size, TILE):
                width = min(TILE, size - start)
                columns = span(first + start, width)
                product = dot(own, mine[:, columns]) + dot(other, theirs[:, columns])
                stage[:, span(at + start, width)] = product.astype(LOW)
        put(copies, stage, span(at, size), targets[z])


def ff_targets(own, ahead, behind, low, high):
    upper, lower = span(0, HALVES), span(HALVES, HALVES)
    return {
        4: (ahead, upper, 0), 3: (ahead, lower, 0), 5: (behind, upper, 0), 6: (behind, lower, 0),
        2: (low, upper, 0), 7: (high, upper, 0), 0: (own, upper, 0), 1: (own, lower, 0),
    }


def kernel_grad_ff(early, other_early, wide, other_wide, own, after, *refs):
    outs, (er, oer, wi, owi, ow, stage_y, stage_z, semaphores) = refs[:10], refs[10:]
    copies = Copies(semaphores)
    tail = span(2 * FF, HALF)
    copies.start("a", other_wide.at[:, tail], owi.at[:, tail])
    for source, target in ((early, er), (other_early, oer), (own, ow)):
        copies.start("a", source, target)
    for at in range(2):
        for source, target in ((wide, wi), (other_wide, owi)):
            copies.start(f"b{at * FF}", source.at[:, span(at * FF, FF)], target.at[:, span(at * FF, FF)])
    copies.wait("a")
    left = {"e": (ow[:, OWN["e"]].T, owi[:, tail].T), "h2": (ow[:, OWN["h2"]].T, oer[:, LOWER].T)}

    def rights(name, first):
        if name == "wide":
            copies.wait(f"b{first}")
        return (wi, owi) if name == "wide" else (er, oer)

    targets = ff_targets(*outs[:5]), ff_targets(*outs[5:])
    products(copies, FF_PARTS, left.get, rights, (stage_y, stage_z), targets)
    copies.finish()


def run_grad_ff(early, other_early, wide, other_wide, own, after):
    scratch = [vmem(ROWS, EARLY)] * 2 + [vmem(ROWS, WIDE)] * 2 + [vmem(ROWS, 4 * HALF)] + [vmem(HALF, N_FF)] * 2
    outs = [shape(rows, N_FF) for rows in (PART, PART, PART, HALVES, HALVES)] * 2
    operands = [early, other_early, wide, other_wide, own, after]
    outs = call(kernel_grad_ff, operands, 0, outs, scratch, 8 + 8 * 4)
    return outs[:5], outs[5:]


def kernel_grad_attend(late, other_late, own, pack, *refs):
    outs, (la, ola, ow, pa, stage_y, stage_z, semaphores) = refs[:10], refs[10:]
    copies = Copies(semaphores)
    copies.start("a", own, ow)
    tail = span(3 * D, LATE - 3 * D)
    for name, columns in (("a", tail), ("b0", span(0, QKV_CUT)), (f"b{QKV_CUT}", span(QKV_CUT, 3 * D - QKV_CUT))):
        for source, target in ((late, la), (other_late, ola)):
            copies.start(name, source.at[:, columns], target.at[:, columns])
    copies.start("pack", pack, pa)
    copies.wait("a")
    left = {
        "h1": (ow[:, OWN["h1"]].T, ola[span(0, ROWS), span(4 * D, HALF)].T),
        "o": (ow[:, OWN["o"]].T, ola[span(0, ROWS), span(4 * D + HALF, HALF)].T),
    }

    def extra():
        copies.wait("pack")
        mine, theirs = la[GAINS, span(0, D)], ola[GAINS, span(0, D)]
        theirs = jnp.concatenate([theirs[:, UPPER], theirs[:, LOWER]], axis=1)
        columns = []
        for at in range(2):
            matrix = pa[at]
            first = dot(mine, matrix[:D]) + dot(theirs, matrix[:D])
            second = dot(mine, matrix[D:]) + dot(theirs, matrix[D:])
            columns.append(first[0:1] + first[2:3] + second[1:2] + second[3:4])
        rows = jnp.concatenate(columns + [jnp.zeros((PAD - 2, HALF), FULL)], axis=0)
        return z_first(rows.T).astype(LOW)

    mine, theirs = la.at[span(0, ROWS), :], ola.at[span(0, ROWS), :]

    def rights(name, first):
        if first < 3 * D:
            copies.wait(f"b{first}")
        return mine, theirs

    targets = ff_targets(*outs[:5]), ff_targets(*outs[5:])
    products(copies, QKV_PARTS, left.get, rights, (stage_y, stage_z), targets, extra)
    copies.finish()


def run_grad_attend(late, other_late, own, pack):
    scratch = [vmem(ROWS + 16, LATE)] * 2 + [vmem(ROWS, 4 * HALF), vmem(2, 2 * D, HALF), vmem(HALF, N_Y), vmem(HALF, N_Z)]
    outs = [shape(rows, width) for width in (N_Y, N_Z) for rows in (PART, PART, PART, HALVES, HALVES)]
    operands = [late, other_late, own, pack]
    outs = call(kernel_grad_attend, operands, 0, outs, scratch, 10 + 8 * 4)
    return outs[:5], outs[5:]


def hop(block, axis, step):
    count = lax.axis_size(axis)
    return lax.ppermute(block, axis, [(at, (at + step) % count) for at in range(count)])


def gather_near(block, axis):
    pair = jnp.concatenate([block, hop(block, "xh", 1)])
    ahead = hop(pair, axis, -1)
    behind = hop(pair, axis, 1)
    across = hop(pair, axis, 2)
    return jnp.concatenate([pair, ahead, across, behind])


def gather_far(whole, behind, ahead, axis):
    low = hop(behind[: PART // 2], axis, 1)
    high = hop(ahead[PART // 2 :], axis, -1)
    own = [whole, ahead, low, high, behind]
    return own + [hop(piece, "core", 1) for piece in own]


def total(*terms):
    result = terms[0].astype(FULL)
    for term in terms[1:]:
        result = result + term.astype(FULL)
    return result


def scatter_begin(blocks, axis):
    return hop(blocks[1], axis, 1), hop(blocks[2], axis, -1)


def scatter_sums(blocks, begun):
    return total(blocks[3], begun[0][:HALVES]).astype(LOW), total(blocks[4], begun[1][:HALVES]).astype(LOW)


def scatter_main(sums, axis):
    return hop(sums[0], axis, 1), hop(sums[1], axis, -1)


def scatter_halves(blocks, begun, main):
    low, high = [], []
    for block, (ahead, behind), (main_low, main_high) in zip(blocks, begun, main):
        low.append(total(block[0][:HALVES], behind[HALVES:], main_low))
        high.append(total(block[0][HALVES:], ahead[HALVES:], main_high))
    return jnp.concatenate(low, axis=1), jnp.concatenate(high, axis=1)


def scatter_end(low, high, axis):
    one = hop(low[RUN:].astype(LOW), axis, 1)
    two = hop(high[:RUN].astype(LOW), axis, 2)
    three = hop(high[RUN:].astype(LOW), axis, -1)
    low = low[:RUN].astype(LOW)
    other = hop(total(low[BLOCK:], one[BLOCK:], two[BLOCK:], three[BLOCK:]).astype(LOW), "xh", 1)
    return total(low[:BLOCK], one[:BLOCK], two[:BLOCK], three[:BLOCK], other)


def natural_of(rel, run, at):
    lane = rel % run
    rel = rel // run
    xx = (rel % NX + at[2]) % NX
    zz = (rel // NX % NZ + at[1]) % NZ
    yy = (rel // (NX * NZ) % NY + at[0]) % NY
    cc = (rel // (NX * NZ * NY) + at[3]) % NC
    return (((yy * NZ + zz) * NX + xx) * NC + cc) * run + lane


def place_matrix(at):
    natural = natural_of(jnp.arange(D), BLOCK, at)
    return (jnp.arange(D)[:, None] == natural[None, :]).astype(LOW)


def spread_matrix(at):
    natural = natural_of(jnp.arange(D), BLOCK, at)
    wanted = natural // (2 * BLOCK) * BLOCK + natural % BLOCK + jnp.arange(2)[:, None] * HALF
    return (natural[None, :, None] == wanted[:, None, :]).astype(LOW)


def pack_matrix(at):
    row = natural_of(jnp.arange(HALF), BLOCK, at)
    wanted = (row // BLOCK * (2 * BLOCK) + row % BLOCK)[None, :] + jnp.arange(2)[:, None] * BLOCK
    source = (jnp.arange(2)[:, None] * D + natural_of(jnp.arange(D), BLOCK, at)[None, :]).reshape(-1)
    return (wanted[:, None, :] == source[None, :, None]).astype(LOW)


def rotary_tables():
    half_dim = HD // 2
    rate_list = 10000.0 ** (-jnp.arange(half_dim, dtype=FULL) / half_dim)
    angles = jnp.arange(LENGTH, dtype=FULL)[:, None] * rate_list[None, :]
    cosine, sine = jnp.cos(angles), jnp.sin(angles)
    cosine = jnp.concatenate([cosine, cosine], axis=1)
    sine = jnp.concatenate([-sine, sine], axis=1)
    return jnp.tile(cosine, (COUNT, 1)), jnp.tile(sine, (COUNT, 1))


def local(boundary, w_qkv, w_out, w_gate_up, w_down_t, gains, memory, mem_index, mem_counts):
    section = lax.axis_index("section").astype(jnp.int32).reshape(1)
    core = lax.axis_index("core").astype(jnp.int32).reshape(1)
    gain_block = jnp.pad(gains.reshape(2, BLOCK).T.astype(LOW), ((0, 0), (0, PAD - 2)))
    first = jnp.concatenate([w_gate_up[0].astype(LOW), w_down_t[0, :, CUT:].astype(LOW)], axis=1)
    second = jnp.concatenate(
        [w_qkv[0].astype(LOW), w_out[0].astype(LOW), w_down_t[0, :, :CUT].astype(LOW), gain_block], axis=1
    )
    first = gather_near(first, "z")
    second = gather_near(second, "y")
    at = tuple(lax.axis_index(name) for name in DP)
    at, boundary, first, second = lax.optimization_barrier((at, boundary, first, second))
    first_behind, first_ahead = hop(first, "y", 1), hop(first, "y", -1)
    second_behind, second_ahead = hop(second, "z", 1), hop(second, "z", -1)
    place = place_matrix(at)
    pack = pack_matrix(at)
    spread = spread_matrix(at)
    cosine, sine = rotary_tables()
    edge = dot(boundary.reshape(ROWS, D), place, lax.Precision.HIGHEST)
    moved, prepared = lax.optimization_barrier(
        ((first_behind, first_ahead, second_behind, second_ahead), (place, pack, spread, cosine, sine, edge))
    )
    first_behind, first_ahead, second_behind, second_ahead = moved
    place, pack, spread, cosine, sine, edge = prepared
    first = gather_far(first, first_behind, first_ahead, "y")
    second = gather_far(second, second_behind, second_ahead, "z")
    picked = run_pick(memory, mem_index)

    sent, qkv, near, late, middle, early, gate_up, own, gain = run_first(
        section, core, edge, spread, cosine, sine, place, first, second
    )
    moved = lax.ppermute(sent, "section", [(0, 1)])
    early, late, own, result, sent, wide = run_last(
        section, mem_counts, moved, edge, gain, cosine, sine, place, picked, first, second, (early, late, own)
    )
    upstream = lax.ppermute(sent, "section", [(1, 0)])
    other_early = hop(early, "core", 1)
    wide, own = run_back_gate(section, upstream, gate_up, first, second, other_early, wide, own)
    other_wide = hop(wide, "core", 1)
    grad_middle, gain_part = run_back_ff(section, upstream, gain, middle, wide, first)
    gate_y, gate_z = run_grad_ff(early, other_early, wide, other_wide, own, grad_middle)
    begun_gate_y = scatter_begin(gate_y, "y")
    begun_gate_z = scatter_begin(gate_z, "z")
    late, own, result = run_back_attend(
        section, edge, gain, cosine, sine, place, qkv, near, grad_middle, gain_part, second, gate_z[0],
        (late, own, result),
    )
    other_late = hop(late, "core", 1)
    sums_y, sums_z = scatter_sums(gate_y, begun_gate_y), scatter_sums(gate_z, begun_gate_z)
    other_late, sums_y, sums_z = lax.optimization_barrier((other_late, sums_y, sums_z))
    main_gate_y, main_gate_z = scatter_main(sums_y, "y"), scatter_main(sums_z, "z")
    qkv_y, qkv_z = run_grad_attend(late, other_late, own, pack)
    begun_qkv_y = scatter_begin(qkv_y, "y")
    begun_qkv_z = scatter_begin(qkv_z, "z")
    result, main_gate_y, main_gate_z = lax.optimization_barrier((result, main_gate_y, main_gate_z))
    finals = dot(result, place.T, lax.Precision.HIGHEST).reshape(1, COUNT, LENGTH, D)
    main_qkv_y = scatter_main(scatter_sums(qkv_y, begun_qkv_y), "y")
    main_qkv_z = scatter_main(scatter_sums(qkv_z, begun_qkv_z), "z")
    low_y, high_y = scatter_halves((gate_y, qkv_y), (begun_gate_y, begun_qkv_y), (main_gate_y, main_qkv_y))
    low_z, high_z = scatter_halves((gate_z, qkv_z), (begun_gate_z, begun_qkv_z), (main_gate_z, main_qkv_z))
    y, z = scatter_end(low_y, high_y, "z"), scatter_end(low_z, high_z, "y")
    wide = N_FF
    gate_y, qkv_y, gate_z, qkv_z = y[:, :wide], y[:, wide:], z[:, :wide], z[:, wide:]
    cut = 3 * D - QKV_CUT
    return (
        finals,
        jnp.concatenate([qkv_y, qkv_z[:, :cut]], axis=1)[None],
        qkv_z[None, :, cut : cut + D],
        jnp.concatenate([gate_y[:, :FF], gate_z[:, :FF]], axis=1)[None],
        jnp.concatenate([gate_y[:, FF:], gate_z[:, FF:]], axis=1)[None],
        qkv_z[:, cut + D : cut + D + 2].T.reshape(1, -1),
    )


def solution(mesh):
    mesh = Mesh(mesh.devices.reshape(2, NY, NZ, NX, NC), ("section",) + DP)
    in_specs = (
        P("section", DP, None, None),
        P("section", DP, None),
        P("section", DP, None),
        P("section", DP, None),
        P("section", DP, None),
        P("section", DP),
        P(DP, None, None, None),
        P(DP, None, None),
        P(DP),
    )
    return jax.shard_map(local, mesh=mesh, in_specs=in_specs, out_specs=in_specs[:6], check_vma=False)
```

```python
import functools

import jax
import jax.numpy as jnp
from jax import lax
from jax.experimental import pallas as pl
from jax.experimental.pallas import tpu as pltpu
from jax.sharding import Mesh
from jax.sharding import PartitionSpec as P

MASKED = -1e30
EPSILON = 1e-06
LOW = jnp.bfloat16
FULL = jnp.float32
NY, NZ, NX, NC = 4, 4, 2, 2
DP = ("y", "z", "xh", "core")
D, HEADS, HD, FF = 1024, 8, 128, 2816
COUNT, LENGTH = 2, 128
ROWS = COUNT * LENGTH
BLOCK = 16
HALF = D // 2
PART = D // (NC * NY)
RUN = PART // NZ
PAD = 128
CUT = 2048
TILE = 256
MIB = 1024 * 1024
SCALE = HD ** (-0.5)
HBM = pl.BlockSpec(memory_space=pltpu.HBM)
SMEM = pl.BlockSpec(memory_space=pltpu.SMEM)


def dot(left, right, precision=None):
    return jnp.dot(left, right, preferred_element_type=FULL, precision=precision)


def dot_nt(left, right):
    return lax.dot_general(left, right, (((1,), (1,)), ((), ())), preferred_element_type=FULL)


def dot_tn(left, right):
    return lax.dot_general(left, right, (((0,), (0,)), ((), ())), preferred_element_type=FULL)


def unit_rows(stream):
    inverse_rms = lax.rsqrt(jnp.mean(stream * stream, axis=-1, keepdims=True) + EPSILON)
    return stream * inverse_rms, inverse_rms


def turn(rows, cosine, sine):
    return rows * cosine + pltpu.roll(rows, HD // 2, 1) * sine


def span(start, size):
    return slice(start, start + size)


def no_wait(start):
    pass


def attend_forward(x, gain, cosine, sine, w_qkv, qkv, plain, wait):
    unit, _ = unit_rows(x[...])
    normed = (unit * gain[0:1, :]).astype(LOW)
    for start in range(0, 3 * D, TILE):
        wait(start)
        joined = dot(normed, w_qkv[:, span(start, TILE)])
        for at in range(start, start + TILE, HD):
            head = joined[:, span(at - start, HD)]
            if at < 2 * D:
                qkv[:, span(at, HD)] = turn(head, cosine[...], sine[...]).astype(LOW)
            else:
                qkv[:, span(at, HD)] = head.astype(LOW)
            if plain is not None and at < D:
                plain[:, span(at, HD)] = head.astype(LOW)


def causal():
    return lax.broadcasted_iota(jnp.int32, (LENGTH, LENGTH), 0) >= lax.broadcasted_iota(jnp.int32, (LENGTH, LENGTH), 1)


def heads_forward(qkv, plain, picked, counts, near, far, attended):
    keep = causal()
    every = range(HEADS)
    for seq in range(COUNT):
        rows = span(seq * LENGTH, LENGTH)
        at = [span(head * HD, HD) for head in every]
        scores = [dot_nt(qkv[rows, at[h]], qkv[rows, span(D + h * HD, HD)]) for h in every]
        scores = [jnp.where(keep, score * SCALE, MASKED) for score in scores]
        tops = [jnp.max(score, axis=-1, keepdims=True) for score in scores]
        if picked is not None:
            valid = lax.broadcasted_iota(jnp.int32, (LENGTH, LENGTH), 1) < counts[seq]
            memory = [dot_nt(plain[rows, at[h]], picked[0, seq, h]) for h in every]
            memory = [jnp.where(valid, score * SCALE, MASKED) for score in memory]
            tops = [jnp.maximum(top, jnp.max(score, axis=-1, keepdims=True)) for top, score in zip(tops, memory)]
        scores = [jnp.exp(score - top) for score, top in zip(scores, tops)]
        totals = [jnp.sum(score, axis=-1, keepdims=True) for score in scores]
        if picked is not None:
            memory = [jnp.exp(score - top) for score, top in zip(memory, tops)]
            totals = [part + jnp.sum(score, axis=-1, keepdims=True) for part, score in zip(totals, memory)]
        scales = [1.0 / part for part in totals]
        scores = [(score * scale).astype(LOW) for score, scale in zip(scores, scales)]
        values = [qkv[rows, span(2 * D + h * HD, HD)] for h in every]
        for h in every:
            near[seq * HEADS + h] = scores[h]
        if picked is not None:
            memory = [(score * scale).astype(LOW) for score, scale in zip(memory, scales)]
            for h in every:
                far[seq * HEADS + h] = memory[h]
            scores = [jnp.concatenate(both, axis=1) for both in zip(scores, memory)]
            values = [jnp.concatenate([values[h], picked[1, seq, h]], axis=0) for h in every]
        results = [dot(score, value) for score, value in zip(scores, values)]
        for h in every:
            attended[rows, at[h]] = results[h].astype(LOW)


def out_forward(x, attended, place, w_out, attended_rel, middle):
    attended_rel[...] = dot(attended[...], place[...]).astype(LOW)
    for start in range(0, D, 2 * TILE):
        out = dot(attended_rel[...], w_out[:, span(start, 2 * TILE)])
        high = out.astype(LOW)
        low = (out - high.astype(FULL)).astype(LOW)
        shard = place[span(start, 2 * TILE), :]
        moved = dot(high, shard) + dot(low, shard)
        middle[...] = (x[...] if start == 0 else middle[...]) + moved


def ff_forward(middle, gain, w_gate_up, normed_two, gate_up, hidden):
    unit, _ = unit_rows(middle[...])
    normed_two[...] = (unit * gain[1:2, :]).astype(LOW)
    for start in range(0, FF, TILE):
        gate = dot(normed_two[...], w_gate_up[:, span(start, TILE)])
        up = dot(normed_two[...], w_gate_up[:, span(FF + start, TILE)])
        gate_up[:, span(start, TILE)] = gate.astype(LOW)
        gate_up[:, span(FF + start, TILE)] = up.astype(LOW)
        hidden[:, span(start, TILE)] = (gate * jax.nn.sigmoid(gate) * up).astype(LOW)


def down_forward(middle, hidden, w_down, result):
    for start in range(0, D, TILE):
        columns = span(start, TILE)
        result[:, columns] = (middle[:, columns] + dot_nt(hidden[...], w_down[columns, :])).astype(result.dtype)


def norm_back(grad, unit, inverse_rms, gain):
    weighted = grad * gain
    return inverse_rms * (weighted - unit * jnp.mean(weighted * unit, axis=-1, keepdims=True))


def gate_backward(upstream_low, w_down, gate_up, grad_ff, wait=no_wait):
    for start in range(0, FF, TILE):
        wait(start)
        grad_hidden = dot(upstream_low[...], w_down[:, span(start, TILE)])
        gate, up = gate_up[:, span(start, TILE)].astype(FULL), gate_up[:, span(FF + start, TILE)].astype(FULL)
        sigmoid_gate = jax.nn.sigmoid(gate)
        grad_gate = grad_hidden * up * sigmoid_gate * (1.0 + gate * (1.0 - sigmoid_gate))
        grad_ff[:, span(start, TILE)] = grad_gate.astype(LOW)
        grad_ff[:, span(FF + start, TILE)] = (grad_hidden * (gate * sigmoid_gate)).astype(LOW)


def ff_backward(upstream, middle, gain, w_gate_up, grad_ff, grad_middle, gain_grad, wait=no_wait):
    for start in range(0, D, TILE):
        wait(start)
        grad_middle[:, span(start, TILE)] = dot_nt(grad_ff[...], w_gate_up[span(start, TILE), :])
    unit, inverse_rms = unit_rows(middle[...])
    grad = grad_middle[...]
    gain_grad[1:2, :] = jnp.sum(grad * unit, axis=0, keepdims=True)
    grad_middle[...] = upstream[...].astype(FULL) + norm_back(grad, unit, inverse_rms, gain[1:2, :])


def out_backward(grad_middle, place, w_out, branch, grad_attended):
    branch[...] = dot_nt(grad_middle[...].astype(LOW), place[...]).astype(LOW)
    grad_rel = dot_nt(branch[...], w_out[...]).astype(LOW)
    grad_attended[...] = dot_nt(grad_rel, place[...]).astype(LOW)


def heads_backward(qkv, picked, near, far, grad_attended, cosine, sine, grad_joined):
    every = range(HEADS)
    for seq in range(COUNT):
        rows = span(seq * LENGTH, LENGTH)
        cos, sin = cosine[rows, :], -sine[rows, :]
        at = [span(head * HD, HD) for head in every]
        grad_outs = [grad_attended[rows, at[h]] for h in every]
        probs = [near[seq * HEADS + h] for h in every]
        values = [qkv[rows, span(2 * D + h * HD, HD)] for h in every]
        grad_values = [dot_tn(prob, grad_out) for prob, grad_out in zip(probs, grad_outs)]
        if picked is not None:
            probs = [jnp.concatenate([probs[h], far[seq * HEADS + h]], axis=1) for h in every]
            values = [jnp.concatenate([values[h], picked[1, seq, h]], axis=0) for h in every]
        probs = [prob.astype(FULL) for prob in probs]
        grads = [dot_nt(grad_out, value) for grad_out, value in zip(grad_outs, values)]
        deltas = [jnp.sum(prob * grad, axis=-1, keepdims=True) for prob, grad in zip(probs, grads)]
        grads = [(prob * (grad - delta)).astype(LOW) for prob, grad, delta in zip(probs, grads, deltas)]
        for h in every:
            grad_joined[rows, span(2 * D + h * HD, HD)] = grad_values[h].astype(LOW)
        queries = [dot(grads[h][:, :LENGTH], qkv[rows, span(D + h * HD, HD)]) * SCALE for h in every]
        keys = [dot_tn(grads[h][:, :LENGTH], qkv[rows, at[h]]) * SCALE for h in every]
        queries = [turn(query, cos, sin) for query in queries]
        keys = [turn(key, cos, sin) for key in keys]
        if picked is not None:
            queries = [queries[h] + dot(grads[h][:, LENGTH:], picked[0, seq, h]) * SCALE for h in every]
        for h in every:
            grad_joined[rows, at[h]] = queries[h].astype(LOW)
            grad_joined[rows, span(D + h * HD, HD)] = keys[h].astype(LOW)


def attend_backward(x, gain, w_qkv, grad_joined, grad_middle, normed, result, gain_grad):
    for start in range(0, D, TILE):
        result[:, span(start, TILE)] = dot_nt(grad_joined[...], w_qkv[span(start, TILE), :])
    unit, inverse_rms = unit_rows(x[...])
    normed[...] = (unit * gain[0:1, :]).astype(LOW)
    grad = result[...]
    gain_grad[0:1, :] = jnp.sum(grad * unit, axis=0, keepdims=True)
    result[...] = grad_middle[...] + norm_back(grad, unit, inverse_rms, gain[0:1, :])


EARLY = HALF + FF
WIDE = 2 * FF + HALF
LATE = 4 * D + 2 * HALF
GAINS = span(ROWS, 16)
LOWER, UPPER = span(0, HALF), span(HALF, HALF)
OWN = {name: span(at * HALF, HALF) for at, name in enumerate(("h2", "e", "h1", "o"))}


class Copies:
    def __init__(self, semaphores):
        self.semaphores, self.used, self.groups = semaphores, 0, {}

    def copy(self, at, source, target):
        source, target = (view[0].at[view[1]] if isinstance(view, tuple) else view for view in (source, target))
        return pltpu.make_async_copy(source, target, self.semaphores.at[at])

    def start(self, name, source, target):
        self.copy(self.used, source, target).start()
        self.groups.setdefault(name, []).append((self.used, source, target))
        self.used += 1

    def wait(self, *names):
        for name in names:
            for copy in self.groups.pop(name):
                self.copy(*copy).wait()

    def finish(self):
        self.wait(*list(self.groups))


def y_runs():
    return [(0, (0, PART), 0), (1, (0, PART), PART), (2, (0, PART // 2), 2 * PART)] + [
        (3, (0, PART // 2), 2 * PART + PART // 2),
        (4, (0, PART), 3 * PART),
    ]


def z_runs():
    runs = []
    for piece, dz, low, high in ((0, 0, 0, 4), (1, 1, 0, 4), (2, 2, 0, 2), (3, 2, 2, 4), (4, 3, 0, 4)):
        runs += [(piece, ((dy - low) * RUN, RUN), dy * PART + dz * RUN) for dy in range(low, high)]
    return runs


def load(copies, name, pieces, runs, columns, target, target_columns):
    for core in range(NC):
        for piece, (low, size), row in runs:
            source = pieces[core * 5 + piece], (span(low, size), columns)
            copies.start(name, source, (target, (span(core * HALF + row, size), target_columns)))


def load_qkv(copies, second, target):
    for at in range(3):
        columns = span(at * D, D)
        load(copies, f"qkv{at * D}", second, z_runs(), columns, target, columns)


def wait_qkv(copies):
    return lambda start: copies.wait(f"qkv{start}") if start % D == 0 else None


def load_out(copies, second, target):
    load(copies, "out", second, z_runs(), span(3 * D, D), target, span(0, D))


def load_gains(copies, second, target):
    load(copies, "gains", second, z_runs(), span(4 * D + CUT, PAD), target, span(0, PAD))


def load_gate(copies, first, target):
    for core in range(NC):
        for piece, (low, size), row in y_runs():
            row += core * HALF
            source = first[core * 5 + piece], (span(low, size), span(0, 2 * FF))
            copies.start(f"gate{row // TILE * TILE}", source, (target, (span(row, size), span(0, 2 * FF))))


GATE = tuple(f"gate{at}" for at in range(0, D, TILE))
DOWN = tuple(f"down{at}" for at in range(0, FF, D))


def load_down(copies, first, second, target, also=None):
    for start in range(0, FF, D):
        name = f"down{start}"
        if start < CUT:
            load(copies, name, second, z_runs(), span(4 * D + start, D), target, span(start, D))
        else:
            load(copies, name, first, y_runs(), span(2 * FF, FF - CUT), target, span(CUT, FF - CUT))
        if also:
            also(name, start, min(D, FF - start))


def kernel_first(section, core, *refs):
    (x, spread, cosine, sine, place), refs = refs[:5], refs[5:]
    first, second, refs = refs[:10], refs[10:20], refs[20:]
    (sent_o, qkv_o, near_o, late_o, middle_o, early_o, gate_up_o, own_o, gain_o), refs = refs[:9], refs[9:]
    xs, gains, cos, sin, places, w_qkv, w_out, w_gate, w_down = refs[:9]
    qkv, near, attended, attended_rel, middle, normed_two, gate_up, hidden, sent, spreads, gain_rows, semaphores = refs[9:]

    copies = Copies(semaphores)
    load_gains(copies, second, gain_rows)
    copies.start("gains", spread, spreads)

    @pl.when(section[0] == 0)
    def _():
        for source, target in ((x, xs), (cosine, cos), (sine, sin)):
            copies.start("small", source, target)
        load_qkv(copies, second, w_qkv)
        copies.start("place", place, places)
        load_out(copies, second, w_out)
        load_gate(copies, first, w_gate)
        load_down(copies, first, second, w_down)

    copies.wait("gains")
    rows = gain_rows[...].astype(FULL).T[:8].astype(LOW)
    low = lax.broadcasted_iota(jnp.int32, (1, D), 1) < HALF
    straight = jnp.logical_xor(low, core[0] == 1)
    for at in range(2):
        picked = dot(rows, spreads[at])
        gains[at : at + 1, :] = jnp.where(straight, picked[0:1], picked[1:2])
    copies.start("gain", gains, gain_o)

    @pl.when(section[0] == 0)
    def _():
        copies.wait("small")
        attend_forward(xs, gains, cos, sin, w_qkv, qkv, None, wait_qkv(copies))
        copies.start("done", qkv, qkv_o)
        heads_forward(qkv, None, None, None, near, None, attended)
        copies.start("done", near, near_o)
        copies.wait("place", "out")
        out_forward(xs, attended, places, w_out, attended_rel, middle)
        copies.start("done", attended_rel.at[:, LOWER], own_o.at[:, OWN["o"]])
        copies.start("done", attended_rel.at[:, UPPER], late_o.at[span(0, ROWS), span(4 * D + HALF, HALF)])
        copies.start("done", middle, middle_o)
        copies.wait(*GATE)
        ff_forward(middle, gains, w_gate, normed_two, gate_up, hidden)
        copies.start("done", normed_two.at[:, LOWER], own_o.at[:, OWN["h2"]])
        copies.start("done", normed_two.at[:, UPPER], early_o.at[:, LOWER])
        copies.start("done", gate_up, gate_up_o)
        copies.start("done", hidden, early_o.at[:, span(HALF, FF)])
        copies.wait(*DOWN)
        down_forward(middle, hidden, w_down, sent)
        copies.start("done", sent, sent_o)
        copies.wait("done")

    copies.wait("gain")


def two_parts(gain_grad):
    full = gain_grad[...]
    high = full.astype(LOW).astype(FULL)
    return jnp.concatenate([high, full - high, jnp.zeros((12, D), FULL)], axis=0).astype(LOW)


def kernel_last(section, counts, *refs):
    (x_low, upstream, gain, cosine, sine, place, picked), refs = refs[:7], refs[7:]
    first, second, refs = refs[:10], refs[10:20], refs[20:]
    refs = refs[3:]
    (early_o, late_o, own_o, result_o, sent_o, grad_ff_o), refs = refs[:6], refs[6:]
    xl, ups, up_low, gains, cos, sin, places, picks, w_qkv, w_out, w_gate, w_down = refs[:12]
    xs, qkv, plain, near, far, attended, attended_rel, middle, normed_two, gate_up, hidden, result = refs[12:24]
    grad_ff, grad_middle, branch, grad_joined, normed, gain_grad, gain_rows, semaphores = refs[24:]

    @pl.when(section[0] == 1)
    def _():
        copies = Copies(semaphores)
        for source, target in ((x_low, xl), (gain, gains), (cosine, cos), (sine, sin)):
            copies.start("small", source, target)
        load_qkv(copies, second, w_qkv)
        copies.start("picks", picked, picks)
        copies.start("place", place, places)
        load_out(copies, second, w_out)
        load_gate(copies, first, w_gate)
        load_down(copies, first, second, w_down)
        copies.start("up", upstream, ups)
        copies.wait("small")
        xs[...] = xl[...].astype(FULL)
        attend_forward(xs, gains, cos, sin, w_qkv, qkv, plain, wait_qkv(copies))
        copies.wait("picks")
        heads_forward(qkv, plain, picks, counts, near, far, attended)
        copies.wait("place", "out")
        out_forward(xs, attended, places, w_out, attended_rel, middle)
        copies.start("done", attended_rel.at[:, LOWER], own_o.at[:, OWN["o"]])
        copies.start("done", attended_rel.at[:, UPPER], late_o.at[span(0, ROWS), span(4 * D + HALF, HALF)])
        copies.wait(*GATE)
        ff_forward(middle, gains, w_gate, normed_two, gate_up, hidden)
        copies.start("done", normed_two.at[:, LOWER], own_o.at[:, OWN["h2"]])
        copies.start("done", normed_two.at[:, UPPER], early_o.at[:, LOWER])
        copies.start("done", hidden, early_o.at[:, span(HALF, FF)])
        copies.wait(*DOWN, "up")
        up_low[...] = ups[...].astype(LOW)
        copies.start("done", up_low.at[:, LOWER], own_o.at[:, OWN["e"]])
        copies.start("done", up_low.at[:, UPPER], grad_ff_o.at[:, span(2 * FF, HALF)])
        down_forward(middle, hidden, w_down, result)
        copies.start("result", result, result_o)
        gate_backward(up_low, w_down, gate_up, grad_ff)
        copies.start("done", grad_ff, grad_ff_o.at[:, span(0, 2 * FF)])
        ff_backward(ups, middle, gains, w_gate, grad_ff, grad_middle, gain_grad)
        out_backward(grad_middle, places, w_out, branch, attended)
        copies.start("done", branch, late_o.at[span(0, ROWS), span(3 * D, D)])
        heads_backward(qkv, picks, near, far, attended, cos, sin, grad_joined)
        copies.start("done", grad_joined, late_o.at[span(0, ROWS), span(0, 3 * D)])
        copies.wait("result")
        attend_backward(xs, gains, w_qkv, grad_joined, grad_middle, normed, result, gain_grad)
        xl[...] = result[...].astype(LOW)
        copies.start("done", xl, sent_o)
        copies.start("done", normed.at[:, LOWER], own_o.at[:, OWN["h1"]])
        copies.start("done", normed.at[:, UPPER], late_o.at[span(0, ROWS), span(4 * D, HALF)])
        gain_rows[...] = two_parts(gain_grad)
        copies.start("done", gain_rows, late_o.at[GAINS, span(0, D)])
        copies.finish()


def kernel_back_gate(section, *refs):
    (upstream, gate_up), refs = refs[:2], refs[2:]
    first, second, refs = refs[:10], refs[10:20], refs[20:]
    refs = refs[3:]
    (grad_ff_o, own_o), refs = refs[:2], refs[2:]
    ups, gate_ups, w_down, grad_ff, semaphores = refs

    @pl.when(section[0] == 0)
    def _():
        copies = Copies(semaphores)
        copies.start("up", upstream, ups)

        def saved(name, start, size):
            for columns in (span(start, size), span(FF + start, size)):
                copies.start(name, gate_up.at[:, columns], gate_ups.at[:, columns])

        load_down(copies, first, second, w_down, saved)
        copies.wait("up")
        copies.start("done", ups.at[:, LOWER], own_o.at[:, OWN["e"]])
        copies.start("done", ups.at[:, UPPER], grad_ff_o.at[:, span(2 * FF, HALF)])
        gate_backward(
            ups, w_down, gate_ups, grad_ff, lambda start: copies.wait(f"down{start}") if start % D == 0 else None
        )
        copies.start("done", grad_ff, grad_ff_o.at[:, span(0, 2 * FF)])
        copies.finish()


def kernel_back_ff(section, *refs):
    (upstream, gain, middle, grad_ff), refs = refs[:4], refs[4:]
    first, refs = refs[:10], refs[10:]
    (grad_middle_o, gain_grad_o), refs = refs[:2], refs[2:]
    ups, gains, mid, grad_ffs, w_gate, grad_middle, gain_grad, semaphores = refs

    @pl.when(section[0] == 0)
    def _():
        copies = Copies(semaphores)
        copies.start("first", grad_ff.at[:, span(0, 2 * FF)], grad_ffs)
        load_gate(copies, first, w_gate)
        copies.start("late", upstream, ups)
        copies.start("late", middle, mid)
        copies.start("late", gain, gains)
        copies.wait("first")

        def wait(start):
            copies.wait(f"gate{start}")
            if start == D - TILE:
                copies.wait("late")

        ff_backward(ups, mid, gains, w_gate, grad_ffs, grad_middle, gain_grad, wait)
        copies.start("done", grad_middle, grad_middle_o)
        copies.start("done", gain_grad, gain_grad_o)
        copies.finish()


def kernel_back_attend(section, *refs):
    (x, gain, cosine, sine, place, qkv, near, grad_middle, gain_part), refs = refs[:9], refs[9:]
    second, refs = refs[:10], refs[11:]
    (late_o, own_o, result_o), refs = refs[3:6], refs[6:]
    xs, gains, cos, sin, places, qkvs, nears, grad_mid, w_qkv, w_out = refs[:10]
    grad_attended, branch, grad_joined, normed, result, gain_grad, gain_rows, semaphores = refs[10:]

    @pl.when(section[0] == 0)
    def _():
        copies = Copies(semaphores)
        copies.start("mid", grad_middle, grad_mid)
        copies.start("mid", place, places)
        load_out(copies, second, w_out)
        for source, target in ((qkv, qkvs), (near, nears), (cosine, cos), (sine, sin)):
            copies.start("saved", source, target)
        load_qkv(copies, second, w_qkv)
        for source, target in ((x, xs), (gain, gains), (gain_part, gain_grad)):
            copies.start("late", source, target)
        copies.wait("mid", "out")
        out_backward(grad_mid, places, w_out, branch, grad_attended)
        copies.start("done", branch, late_o.at[span(0, ROWS), span(3 * D, D)])
        copies.wait("saved")
        heads_backward(qkvs, None, nears, None, grad_attended, cos, sin, grad_joined)
        copies.start("done", grad_joined, late_o.at[span(0, ROWS), span(0, 3 * D)])
        copies.wait("qkv0", f"qkv{D}", f"qkv{2 * D}", "late")
        attend_backward(xs, gains, w_qkv, grad_joined, grad_mid, normed, result, gain_grad)
        copies.start("done", result, result_o)
        copies.start("done", normed.at[:, LOWER], own_o.at[:, OWN["h1"]])
        copies.start("done", normed.at[:, UPPER], late_o.at[span(0, ROWS), span(4 * D, HALF)])
        gain_rows[...] = two_parts(gain_grad)
        copies.start("done", gain_rows, late_o.at[GAINS, span(0, D)])
        copies.finish()


def shape(*dims, dtype=LOW):
    return jax.ShapeDtypeStruct(dims, dtype)


def vmem(*dims, dtype=LOW):
    return pltpu.VMEM(dims, dtype)


Y_COPIES, Z_COPIES = 2 * 5, 2 * 16
QKV_COPIES, DOWN_COPIES = 3 * Z_COPIES, 2 * Z_COPIES + Y_COPIES
W_QKV, W_OUT, W_GATE, W_DOWN = vmem(D, 3 * D), vmem(D, D), vmem(D, 2 * FF), vmem(D, FF)


def call(kernel, operands, scalars, outs, scratch, copies, aliases=None):
    return pl.pallas_call(
        kernel,
        out_shape=outs,
        in_specs=[SMEM] * scalars + [HBM] * (len(operands) - scalars),
        out_specs=[HBM] * len(outs),
        scratch_shapes=list(scratch) + [pltpu.SemaphoreType.DMA((copies,))],
        input_output_aliases=aliases or {},
        compiler_params=pltpu.CompilerParams(vmem_limit_bytes=62 * MIB),
        cost_estimate=pl.CostEstimate(flops=1000, bytes_accessed=1000, transcendentals=0),
    )(*operands)


def run_first(section, core, x, spread, cosine, sine, place, first, second):
    outs = [
        shape(ROWS, D), shape(ROWS, 3 * D), shape(COUNT * HEADS, LENGTH, LENGTH), shape(ROWS + 16, LATE),
        shape(ROWS, D, dtype=FULL), shape(ROWS, EARLY), shape(ROWS, 2 * FF), shape(ROWS, 4 * HALF),
        shape(2, D, dtype=FULL),
    ]
    scratch = [vmem(ROWS, D, dtype=FULL), vmem(2, D, dtype=FULL), vmem(ROWS, HD, dtype=FULL), vmem(ROWS, HD, dtype=FULL)]
    scratch += [vmem(D, D), W_QKV, W_OUT, W_GATE, W_DOWN]
    scratch += [vmem(ROWS, 3 * D), vmem(COUNT * HEADS, LENGTH, LENGTH), vmem(ROWS, D), vmem(ROWS, D)]
    scratch += [vmem(ROWS, D, dtype=FULL), vmem(ROWS, D), vmem(ROWS, 2 * FF), vmem(ROWS, FF), vmem(ROWS, D)]
    scratch += [vmem(2, D, D), vmem(D, PAD)]
    operands = [section, core, x, spread, cosine, sine, place, *first, *second]
    return call(kernel_first, operands, 2, outs, scratch, 24 + Y_COPIES + 2 * Z_COPIES + QKV_COPIES + DOWN_COPIES)


def run_last(section, counts, x_low, upstream, gain, cosine, sine, place, picked, first, second, kept):
    outs = [shape(ROWS, EARLY), shape(ROWS + 16, LATE), shape(ROWS, 4 * HALF), shape(ROWS, D, dtype=FULL)]
    outs += [shape(ROWS, D), shape(ROWS, WIDE)]
    scratch = [vmem(ROWS, D), vmem(ROWS, D, dtype=FULL), vmem(ROWS, D), vmem(2, D, dtype=FULL)]
    scratch += [vmem(ROWS, HD, dtype=FULL), vmem(ROWS, HD, dtype=FULL), vmem(D, D), vmem(2, COUNT, HEADS, LENGTH, HD)]
    scratch += [W_QKV, W_OUT, W_GATE, W_DOWN]
    scratch += [vmem(ROWS, D, dtype=FULL), vmem(ROWS, 3 * D), vmem(ROWS, D)]
    scratch += [vmem(COUNT * HEADS, LENGTH, LENGTH)] * 2
    scratch += [vmem(ROWS, D), vmem(ROWS, D), vmem(ROWS, D, dtype=FULL), vmem(ROWS, D), vmem(ROWS, 2 * FF)]
    scratch += [vmem(ROWS, FF), vmem(ROWS, D, dtype=FULL)]
    scratch += [vmem(ROWS, 2 * FF), vmem(ROWS, D, dtype=FULL), vmem(ROWS, D), vmem(ROWS, 3 * D), vmem(ROWS, D)]
    scratch += [vmem(2, D, dtype=FULL), vmem(16, D)]
    operands = [section, counts, x_low, upstream, gain, cosine, sine, place, picked, *first, *second, *kept]
    aliases = {len(operands) - 3 + i: i for i in range(3)}
    return call(kernel_last, operands, 2, outs, scratch, 24 + Y_COPIES + Z_COPIES + QKV_COPIES + DOWN_COPIES, aliases)


def run_back_gate(section, upstream, gate_up, first, second, early, grad_ff, own):
    outs = [shape(ROWS, WIDE), shape(ROWS, 4 * HALF)]
    scratch = [vmem(ROWS, D), vmem(ROWS, 2 * FF), W_DOWN, vmem(ROWS, 2 * FF)]
    operands = [section, upstream, gate_up, *first, *second, early, grad_ff, own]
    at = len(operands) - 2
    return call(
        kernel_back_gate, operands, 1, outs, scratch, 16 + DOWN_COPIES, {at: 0, at + 1: 1}
    )


def run_back_ff(section, upstream, gain, middle, grad_ff, first):
    outs = [shape(ROWS, D, dtype=FULL), shape(2, D, dtype=FULL)]
    scratch = [vmem(ROWS, D), vmem(2, D, dtype=FULL), vmem(ROWS, D, dtype=FULL), vmem(ROWS, 2 * FF)]
    scratch += [W_GATE, vmem(ROWS, D, dtype=FULL), vmem(2, D, dtype=FULL)]
    operands = [section, upstream, gain, middle, grad_ff, *first]
    return call(kernel_back_ff, operands, 1, outs, scratch, 10 + Y_COPIES)


def run_back_attend(section, x, gain, cosine, sine, place, qkv, near, grad_middle, gain_part, second, after, kept):
    outs = [shape(ROWS + 16, LATE), shape(ROWS, 4 * HALF), shape(ROWS, D, dtype=FULL)]
    scratch = [vmem(ROWS, D, dtype=FULL), vmem(2, D, dtype=FULL), vmem(ROWS, HD, dtype=FULL), vmem(ROWS, HD, dtype=FULL)]
    scratch += [vmem(D, D), vmem(ROWS, 3 * D), vmem(COUNT * HEADS, LENGTH, LENGTH), vmem(ROWS, D, dtype=FULL)]
    scratch += [W_QKV, W_OUT, vmem(ROWS, D), vmem(ROWS, D), vmem(ROWS, 3 * D), vmem(ROWS, D), vmem(ROWS, D, dtype=FULL)]
    scratch += [vmem(2, D, dtype=FULL), vmem(16, D)]
    operands = [section, x, gain, cosine, sine, place, qkv, near, grad_middle, gain_part, *second, after, *kept]
    at = len(operands) - 3
    return call(
        kernel_back_attend, operands, 1, outs, scratch, 20 + Z_COPIES + QKV_COPIES, {at + i: i for i in range(3)}
    )


def pick_kernel(memory, index, out):
    chosen = index[0, 0]
    hot = (lax.broadcasted_iota(jnp.int32, (memory.shape[2], LENGTH), 0) == chosen).astype(FULL).astype(LOW)
    for kind in range(2):
        out[kind, 0, 0] = dot_tn(hot, memory[0, kind]).astype(LOW)


def run_pick(memory, mem_index):
    slots = memory.shape[2]
    return pl.pallas_call(
        pick_kernel,
        grid=(COUNT, HEADS),
        in_specs=[
            pl.BlockSpec((1, 2, slots, HD), lambda n, h: (n, 0, 0, h)),
            pl.BlockSpec((1, 1, 1, LENGTH), lambda n, h: (n, h, 0, 0)),
        ],
        out_specs=pl.BlockSpec((2, 1, 1, LENGTH, HD), lambda n, h: (0, n, h, 0, 0)),
        out_shape=shape(2, COUNT, HEADS, LENGTH, HD),
    )(memory, mem_index.reshape(COUNT, HEADS, 1, LENGTH))


def z_first(rows):
    return jnp.concatenate([rows[span(dy * PART + dz * RUN, RUN), :] for dz in range(NZ) for dy in range(NY)], axis=0)


HALVES = PART // 2
QKV_CUT = 17 * 128
N_FF, N_Y, N_Z = FF + FF // 2, QKV_CUT, 3 * D - QKV_CUT + D + PAD
FF_PARTS = (
    (0, "e", "early", HALF, FF // 2, FF), (1, "e", "early", HALF + FF // 2, FF // 2, FF),
    (0, "h2", "wide", 0, FF, 0), (1, "h2", "wide", FF, FF, 0),
)
QKV_PARTS = (
    (1, "o", "late", 3 * D, D, 3 * D - QKV_CUT), (0, "h1", "late", 0, QKV_CUT, 0),
    (1, "h1", "late", QKV_CUT, 3 * D - QKV_CUT, 0), (1, None, None, 0, PAD, 3 * D - QKV_CUT + D),
)


def put(copies, staged, columns, targets):
    for source, (ref, rows, shift) in targets.items():
        at = span(columns.start + shift, columns.stop - columns.start)
        copies.start("done", staged.at[span(source * HALVES, HALVES), columns], ref.at[rows, at])


def products(copies, parts, sides, rights, stages, targets, extra=None):
    for z, left, right, first, size, at in parts:
        stage = stages[z]
        if left is None:
            stage[:, span(at, size)] = extra()
        else:
            own, other = sides(left)
            if z:
                own, other = z_first(own), z_first(other)
            mine, theirs = rights(right, first)
            for start in range(0, size, TILE):
                width = min(TILE, size - start)
                columns = span(first + start, width)
                product = dot(own, mine[:, columns]) + dot(other, theirs[:, columns])
                stage[:, span(at + start, width)] = product.astype(LOW)
        put(copies, stage, span(at, size), targets[z])


def ff_targets(own, ahead, behind, low, high):
    upper, lower = span(0, HALVES), span(HALVES, HALVES)
    return {
        4: (ahead, upper, 0), 3: (ahead, lower, 0), 5: (behind, upper, 0), 6: (behind, lower, 0),
        2: (low, upper, 0), 7: (high, upper, 0), 0: (own, upper, 0), 1: (own, lower, 0),
    }


def kernel_grad_ff(early, other_early, wide, other_wide, own, after, *refs):
    outs, (er, oer, wi, owi, ow, stage_y, stage_z, semaphores) = refs[:10], refs[10:]
    copies = Copies(semaphores)
    tail = span(2 * FF, HALF)
    copies.start("a", other_wide.at[:, tail], owi.at[:, tail])
    for source, target in ((early, er), (other_early, oer), (own, ow)):
        copies.start("a", source, target)
    for at in range(2):
        for source, target in ((wide, wi), (other_wide, owi)):
            copies.start(f"b{at * FF}", source.at[:, span(at * FF, FF)], target.at[:, span(at * FF, FF)])
    copies.wait("a")
    left = {"e": (ow[:, OWN["e"]].T, owi[:, tail].T), "h2": (ow[:, OWN["h2"]].T, oer[:, LOWER].T)}

    def rights(name, first):
        if name == "wide":
            copies.wait(f"b{first}")
        return (wi, owi) if name == "wide" else (er, oer)

    targets = ff_targets(*outs[:5]), ff_targets(*outs[5:])
    products(copies, FF_PARTS, left.get, rights, (stage_y, stage_z), targets)
    copies.finish()


def run_grad_ff(early, other_early, wide, other_wide, own, after):
    scratch = [vmem(ROWS, EARLY)] * 2 + [vmem(ROWS, WIDE)] * 2 + [vmem(ROWS, 4 * HALF)] + [vmem(HALF, N_FF)] * 2
    outs = [shape(rows, N_FF) for rows in (PART, PART, PART, HALVES, HALVES)] * 2
    operands = [early, other_early, wide, other_wide, own, after]
    outs = call(kernel_grad_ff, operands, 0, outs, scratch, 8 + 8 * 4)
    return outs[:5], outs[5:]


def kernel_grad_attend(late, other_late, own, pack, *refs):
    outs, (la, ola, ow, pa, stage_y, stage_z, semaphores) = refs[:10], refs[10:]
    copies = Copies(semaphores)
    copies.start("a", own, ow)
    tail = span(3 * D, LATE - 3 * D)
    for name, columns in (("a", tail), ("b0", span(0, QKV_CUT)), (f"b{QKV_CUT}", span(QKV_CUT, 3 * D - QKV_CUT))):
        for source, target in ((late, la), (other_late, ola)):
            copies.start(name, source.at[:, columns], target.at[:, columns])
    copies.start("pack", pack, pa)
    copies.wait("a")
    left = {
        "h1": (ow[:, OWN["h1"]].T, ola[span(0, ROWS), span(4 * D, HALF)].T),
        "o": (ow[:, OWN["o"]].T, ola[span(0, ROWS), span(4 * D + HALF, HALF)].T),
    }

    def extra():
        copies.wait("pack")
        mine, theirs = la[GAINS, span(0, D)], ola[GAINS, span(0, D)]
        theirs = jnp.concatenate([theirs[:, UPPER], theirs[:, LOWER]], axis=1)
        columns = []
        for at in range(2):
            matrix = pa[at]
            first = dot(mine, matrix[:D]) + dot(theirs, matrix[:D])
            second = dot(mine, matrix[D:]) + dot(theirs, matrix[D:])
            columns.append(first[0:1] + first[2:3] + second[1:2] + second[3:4])
        rows = jnp.concatenate(columns + [jnp.zeros((PAD - 2, HALF), FULL)], axis=0)
        return z_first(rows.T).astype(LOW)

    mine, theirs = la.at[span(0, ROWS), :], ola.at[span(0, ROWS), :]

    def rights(name, first):
        if first < 3 * D:
            copies.wait(f"b{first}")
        return mine, theirs

    targets = ff_targets(*outs[:5]), ff_targets(*outs[5:])
    products(copies, QKV_PARTS, left.get, rights, (stage_y, stage_z), targets, extra)
    copies.finish()


def run_grad_attend(late, other_late, own, pack):
    scratch = [vmem(ROWS + 16, LATE)] * 2 + [vmem(ROWS, 4 * HALF), vmem(2, 2 * D, HALF), vmem(HALF, N_Y), vmem(HALF, N_Z)]
    outs = [shape(rows, width) for width in (N_Y, N_Z) for rows in (PART, PART, PART, HALVES, HALVES)]
    operands = [late, other_late, own, pack]
    outs = call(kernel_grad_attend, operands, 0, outs, scratch, 10 + 8 * 4)
    return outs[:5], outs[5:]


def hop(block, axis, step):
    count = lax.axis_size(axis)
    return lax.ppermute(block, axis, [(at, (at + step) % count) for at in range(count)])


def gather_near(block, axis):
    pair = jnp.concatenate([block, hop(block, "xh", 1)])
    ahead = hop(pair, axis, -1)
    behind = hop(pair, axis, 1)
    across = hop(ahead, axis, -1)
    return jnp.concatenate([pair, ahead, across, behind])


def gather_far(whole, behind, ahead, axis):
    low = hop(behind[: PART // 2], axis, 1)
    high = hop(ahead[PART // 2 :], axis, -1)
    own = [whole, ahead, low, high, behind]
    return own + [hop(piece, "core", 1) for piece in own]


def total(*terms):
    result = terms[0].astype(FULL)
    for term in terms[1:]:
        result = result + term.astype(FULL)
    return result


def scatter_begin(blocks, axis):
    return hop(blocks[1], axis, 1), hop(blocks[2], axis, -1)


def scatter_sums(blocks, begun):
    return total(blocks[3], begun[0][:HALVES]).astype(LOW), total(blocks[4], begun[1][:HALVES]).astype(LOW)


def scatter_main(sums, axis):
    return hop(sums[0], axis, 1), hop(sums[1], axis, -1)


def scatter_halves(blocks, begun, main):
    low, high = [], []
    for block, (ahead, behind), (main_low, main_high) in zip(blocks, begun, main):
        low.append(total(block[0][:HALVES], behind[HALVES:], main_low))
        high.append(total(block[0][HALVES:], ahead[HALVES:], main_high))
    return jnp.concatenate(low, axis=1), jnp.concatenate(high, axis=1)


def scatter_end(low, high, axis):
    one = hop(low[RUN:].astype(LOW), axis, 1)
    two = hop(high[:RUN].astype(LOW), axis, 2)
    three = hop(high[RUN:].astype(LOW), axis, -1)
    low = low[:RUN].astype(LOW)
    other = hop(total(low[BLOCK:], one[BLOCK:], two[BLOCK:], three[BLOCK:]).astype(LOW), "xh", 1)
    return total(low[:BLOCK], one[:BLOCK], two[:BLOCK], three[:BLOCK], other)


def natural_of(rel, run, at):
    lane = rel % run
    rel = rel // run
    xx = (rel % NX + at[2]) % NX
    zz = (rel // NX % NZ + at[1]) % NZ
    yy = (rel // (NX * NZ) % NY + at[0]) % NY
    cc = (rel // (NX * NZ * NY) + at[3]) % NC
    return (((yy * NZ + zz) * NX + xx) * NC + cc) * run + lane


def place_matrix(at):
    natural = natural_of(jnp.arange(D), BLOCK, at)
    return (jnp.arange(D)[:, None] == natural[None, :]).astype(LOW)


def spread_matrix(at):
    natural = natural_of(jnp.arange(D), BLOCK, at)
    wanted = natural // (2 * BLOCK) * BLOCK + natural % BLOCK + jnp.arange(2)[:, None] * HALF
    return (natural[None, :, None] == wanted[:, None, :]).astype(LOW)


def pack_matrix(at):
    row = natural_of(jnp.arange(HALF), BLOCK, at)
    wanted = (row // BLOCK * (2 * BLOCK) + row % BLOCK)[None, :] + jnp.arange(2)[:, None] * BLOCK
    source = (jnp.arange(2)[:, None] * D + natural_of(jnp.arange(D), BLOCK, at)[None, :]).reshape(-1)
    return (wanted[:, None, :] == source[None, :, None]).astype(LOW)


def rotary_tables():
    half_dim = HD // 2
    rate_list = 10000.0 ** (-jnp.arange(half_dim, dtype=FULL) / half_dim)
    angles = jnp.arange(LENGTH, dtype=FULL)[:, None] * rate_list[None, :]
    cosine, sine = jnp.cos(angles), jnp.sin(angles)
    cosine = jnp.concatenate([cosine, cosine], axis=1)
    sine = jnp.concatenate([-sine, sine], axis=1)
    return jnp.tile(cosine, (COUNT, 1)), jnp.tile(sine, (COUNT, 1))


def local(boundary, w_qkv, w_out, w_gate_up, w_down_t, gains, memory, mem_index, mem_counts):
    section = lax.axis_index("section").astype(jnp.int32).reshape(1)
    core = lax.axis_index("core").astype(jnp.int32).reshape(1)
    gain_block = jnp.pad(gains.reshape(2, BLOCK).T.astype(LOW), ((0, 0), (0, PAD - 2)))
    first = jnp.concatenate([w_gate_up[0].astype(LOW), w_down_t[0, :, CUT:].astype(LOW)], axis=1)
    second = jnp.concatenate(
        [w_qkv[0].astype(LOW), w_out[0].astype(LOW), w_down_t[0, :, :CUT].astype(LOW), gain_block], axis=1
    )
    first = gather_near(first, "z")
    second = gather_near(second, "y")
    at = tuple(lax.axis_index(name) for name in DP)
    at, boundary, first, second = lax.optimization_barrier((at, boundary, first, second))
    first_behind, first_ahead = hop(first, "y", 1), hop(first, "y", -1)
    second_behind, second_ahead = hop(second, "z", 1), hop(second, "z", -1)
    place = place_matrix(at)
    pack = pack_matrix(at)
    spread = spread_matrix(at)
    cosine, sine = rotary_tables()
    edge = dot(boundary.reshape(ROWS, D), place, lax.Precision.HIGHEST)
    moved, prepared = lax.optimization_barrier(
        ((first_behind, first_ahead, second_behind, second_ahead), (place, pack, spread, cosine, sine, edge))
    )
    first_behind, first_ahead, second_behind, second_ahead = moved
    place, pack, spread, cosine, sine, edge = prepared
    first = gather_far(first, first_behind, first_ahead, "y")
    second = gather_far(second, second_behind, second_ahead, "z")
    picked = run_pick(memory, mem_index)

    sent, qkv, near, late, middle, early, gate_up, own, gain = run_first(
        section, core, edge, spread, cosine, sine, place, first, second
    )
    moved = lax.ppermute(sent, "section", [(0, 1)])
    early, late, own, result, sent, wide = run_last(
        section, mem_counts, moved, edge, gain, cosine, sine, place, picked, first, second, (early, late, own)
    )
    upstream = lax.ppermute(sent, "section", [(1, 0)])
    other_early = hop(early, "core", 1)
    wide, own = run_back_gate(section, upstream, gate_up, first, second, other_early, wide, own)
    other_wide = hop(wide, "core", 1)
    grad_middle, gain_part = run_back_ff(section, upstream, gain, middle, wide, first)
    gate_y, gate_z = run_grad_ff(early, other_early, wide, other_wide, own, grad_middle)
    begun_gate_y = scatter_begin(gate_y, "y")
    begun_gate_z = scatter_begin(gate_z, "z")
    late, own, result = run_back_attend(
        section, edge, gain, cosine, sine, place, qkv, near, grad_middle, gain_part, second, gate_z[0],
        (late, own, result),
    )
    other_late = hop(late, "core", 1)
    sums_y, sums_z = scatter_sums(gate_y, begun_gate_y), scatter_sums(gate_z, begun_gate_z)
    other_late, sums_y, sums_z = lax.optimization_barrier((other_late, sums_y, sums_z))
    main_gate_y, main_gate_z = scatter_main(sums_y, "y"), scatter_main(sums_z, "z")
    qkv_y, qkv_z = run_grad_attend(late, other_late, own, pack)
    qkv_y, qkv_z, main_gate_y, main_gate_z = lax.optimization_barrier((qkv_y, qkv_z, main_gate_y, main_gate_z))
    begun_qkv_y = scatter_begin(qkv_y, "y")
    begun_qkv_z = scatter_begin(qkv_z, "z")
    finals = dot(result, place.T, lax.Precision.HIGHEST).reshape(1, COUNT, LENGTH, D)
    begun_qkv_y, begun_qkv_z, finals = lax.optimization_barrier((begun_qkv_y, begun_qkv_z, finals))
    main_qkv_y = scatter_main(scatter_sums(qkv_y, begun_qkv_y), "y")
    main_qkv_z = scatter_main(scatter_sums(qkv_z, begun_qkv_z), "z")
    low_y, high_y = scatter_halves((gate_y, qkv_y), (begun_gate_y, begun_qkv_y), (main_gate_y, main_qkv_y))
    low_z, high_z = scatter_halves((gate_z, qkv_z), (begun_gate_z, begun_qkv_z), (main_gate_z, main_qkv_z))
    y, z = scatter_end(low_y, high_y, "z"), scatter_end(low_z, high_z, "y")
    wide = N_FF
    gate_y, qkv_y, gate_z, qkv_z = y[:, :wide], y[:, wide:], z[:, :wide], z[:, wide:]
    cut = 3 * D - QKV_CUT
    return (
        finals,
        jnp.concatenate([qkv_y, qkv_z[:, :cut]], axis=1)[None],
        qkv_z[None, :, cut : cut + D],
        jnp.concatenate([gate_y[:, :FF], gate_z[:, :FF]], axis=1)[None],
        jnp.concatenate([gate_y[:, FF:], gate_z[:, FF:]], axis=1)[None],
        qkv_z[:, cut + D : cut + D + 2].T.reshape(1, -1),
    )


def solution(mesh):
    mesh = Mesh(mesh.devices.reshape(2, NY, NZ, NX, NC), ("section",) + DP)
    in_specs = (
        P("section", DP, None, None),
        P("section", DP, None),
        P("section", DP, None),
        P("section", DP, None),
        P("section", DP, None),
        P("section", DP),
        P(DP, None, None, None),
        P(DP, None, None),
        P(DP),
    )
    return jax.shard_map(local, mesh=mesh, in_specs=in_specs, out_specs=in_specs[:6], check_vma=False)
```

```python
import functools

import jax
import jax.numpy as jnp
from jax import lax
from jax.experimental import pallas as pl
from jax.experimental.pallas import tpu as pltpu
from jax.sharding import Mesh
from jax.sharding import PartitionSpec as P

MASKED = -1e30
EPSILON = 1e-06
LOW = jnp.bfloat16
FULL = jnp.float32
NY, NZ, NX, NC = 4, 4, 2, 2
DP = ("y", "z", "xh", "core")
D, HEADS, HD, FF = 1024, 8, 128, 2816
COUNT, LENGTH = 2, 128
ROWS = COUNT * LENGTH
BLOCK = 16
HALF = D // 2
PART = D // (NC * NY)
RUN = PART // NZ
PAD = 128
CUT = 2048
TILE = 256
MIB = 1024 * 1024
SCALE = HD ** (-0.5)
HBM = pl.BlockSpec(memory_space=pltpu.HBM)
SMEM = pl.BlockSpec(memory_space=pltpu.SMEM)


def dot(left, right, precision=None):
    return jnp.dot(left, right, preferred_element_type=FULL, precision=precision)


def dot_nt(left, right):
    return lax.dot_general(left, right, (((1,), (1,)), ((), ())), preferred_element_type=FULL)


def dot_tn(left, right):
    return lax.dot_general(left, right, (((0,), (0,)), ((), ())), preferred_element_type=FULL)


def unit_rows(stream):
    inverse_rms = lax.rsqrt(jnp.mean(stream * stream, axis=-1, keepdims=True) + EPSILON)
    return stream * inverse_rms, inverse_rms


def turn(rows, cosine, sine):
    return rows * cosine + pltpu.roll(rows, HD // 2, 1) * sine


def span(start, size):
    return slice(start, start + size)


def no_wait(start):
    pass


def attend_forward(x, gain, cosine, sine, w_qkv, qkv, plain, wait):
    unit, _ = unit_rows(x[...])
    normed = (unit * gain[0:1, :]).astype(LOW)
    for start in range(0, 3 * D, TILE):
        wait(start)
        joined = dot(normed, w_qkv[:, span(start, TILE)])
        for at in range(start, start + TILE, HD):
            head = joined[:, span(at - start, HD)]
            if at < 2 * D:
                qkv[:, span(at, HD)] = turn(head, cosine[...], sine[...]).astype(LOW)
            else:
                qkv[:, span(at, HD)] = head.astype(LOW)
            if plain is not None and at < D:
                plain[:, span(at, HD)] = head.astype(LOW)


def causal():
    return lax.broadcasted_iota(jnp.int32, (LENGTH, LENGTH), 0) >= lax.broadcasted_iota(jnp.int32, (LENGTH, LENGTH), 1)


def heads_forward(qkv, plain, picked, counts, near, far, attended):
    keep = causal()
    every = range(HEADS)
    for seq in range(COUNT):
        rows = span(seq * LENGTH, LENGTH)
        at = [span(head * HD, HD) for head in every]
        scores = [dot_nt(qkv[rows, at[h]], qkv[rows, span(D + h * HD, HD)]) for h in every]
        scores = [jnp.where(keep, score * SCALE, MASKED) for score in scores]
        tops = [jnp.max(score, axis=-1, keepdims=True) for score in scores]
        if picked is not None:
            valid = lax.broadcasted_iota(jnp.int32, (LENGTH, LENGTH), 1) < counts[seq]
            memory = [dot_nt(plain[rows, at[h]], picked[0, seq, h]) for h in every]
            memory = [jnp.where(valid, score * SCALE, MASKED) for score in memory]
            tops = [jnp.maximum(top, jnp.max(score, axis=-1, keepdims=True)) for top, score in zip(tops, memory)]
        scores = [jnp.exp(score - top) for score, top in zip(scores, tops)]
        totals = [jnp.sum(score, axis=-1, keepdims=True) for score in scores]
        if picked is not None:
            memory = [jnp.exp(score - top) for score, top in zip(memory, tops)]
            totals = [part + jnp.sum(score, axis=-1, keepdims=True) for part, score in zip(totals, memory)]
        scales = [1.0 / part for part in totals]
        scores = [(score * scale).astype(LOW) for score, scale in zip(scores, scales)]
        values = [qkv[rows, span(2 * D + h * HD, HD)] for h in every]
        for h in every:
            near[seq * HEADS + h] = scores[h]
        if picked is not None:
            memory = [(score * scale).astype(LOW) for score, scale in zip(memory, scales)]
            for h in every:
                far[seq * HEADS + h] = memory[h]
            scores = [jnp.concatenate(both, axis=1) for both in zip(scores, memory)]
            values = [jnp.concatenate([values[h], picked[1, seq, h]], axis=0) for h in every]
        results = [dot(score, value) for score, value in zip(scores, values)]
        for h in every:
            attended[rows, at[h]] = results[h].astype(LOW)


def out_forward(x, attended, place, w_out, attended_rel, middle):
    attended_rel[...] = dot(attended[...], place[...]).astype(LOW)
    for start in range(0, D, 2 * TILE):
        out = dot(attended_rel[...], w_out[:, span(start, 2 * TILE)])
        high = out.astype(LOW)
        low = (out - high.astype(FULL)).astype(LOW)
        shard = place[span(start, 2 * TILE), :]
        moved = dot(high, shard) + dot(low, shard)
        middle[...] = (x[...] if start == 0 else middle[...]) + moved


def ff_forward(middle, gain, w_gate_up, normed_two, gate_up, hidden):
    unit, _ = unit_rows(middle[...])
    normed_two[...] = (unit * gain[1:2, :]).astype(LOW)
    for start in range(0, FF, TILE):
        gate = dot(normed_two[...], w_gate_up[:, span(start, TILE)])
        up = dot(normed_two[...], w_gate_up[:, span(FF + start, TILE)])
        gate_up[:, span(start, TILE)] = gate.astype(LOW)
        gate_up[:, span(FF + start, TILE)] = up.astype(LOW)
        hidden[:, span(start, TILE)] = (gate * jax.nn.sigmoid(gate) * up).astype(LOW)


def down_forward(middle, hidden, w_down, result):
    for start in range(0, D, TILE):
        columns = span(start, TILE)
        result[:, columns] = (middle[:, columns] + dot_nt(hidden[...], w_down[columns, :])).astype(result.dtype)


def norm_back(grad, unit, inverse_rms, gain):
    weighted = grad * gain
    return inverse_rms * (weighted - unit * jnp.mean(weighted * unit, axis=-1, keepdims=True))


def gate_backward(upstream_low, w_down, gate_up, grad_ff, wait=no_wait):
    for start in range(0, FF, TILE):
        wait(start)
        grad_hidden = dot(upstream_low[...], w_down[:, span(start, TILE)])
        gate, up = gate_up[:, span(start, TILE)].astype(FULL), gate_up[:, span(FF + start, TILE)].astype(FULL)
        sigmoid_gate = jax.nn.sigmoid(gate)
        grad_gate = grad_hidden * up * sigmoid_gate * (1.0 + gate * (1.0 - sigmoid_gate))
        grad_ff[:, span(start, TILE)] = grad_gate.astype(LOW)
        grad_ff[:, span(FF + start, TILE)] = (grad_hidden * (gate * sigmoid_gate)).astype(LOW)


def ff_backward(upstream, middle, gain, w_gate_up, grad_ff, grad_middle, gain_grad, wait=no_wait):
    for start in range(0, D, TILE):
        wait(start)
        grad_middle[:, span(start, TILE)] = dot_nt(grad_ff[...], w_gate_up[span(start, TILE), :])
    unit, inverse_rms = unit_rows(middle[...])
    grad = grad_middle[...]
    gain_grad[1:2, :] = jnp.sum(grad * unit, axis=0, keepdims=True)
    grad_middle[...] = upstream[...].astype(FULL) + norm_back(grad, unit, inverse_rms, gain[1:2, :])


def out_backward(grad_middle, place, w_out, branch, grad_attended):
    branch[...] = dot_nt(grad_middle[...].astype(LOW), place[...]).astype(LOW)
    grad_rel = dot_nt(branch[...], w_out[...]).astype(LOW)
    grad_attended[...] = dot_nt(grad_rel, place[...]).astype(LOW)


def heads_backward(qkv, picked, near, far, grad_attended, cosine, sine, grad_joined):
    every = range(HEADS)
    for seq in range(COUNT):
        rows = span(seq * LENGTH, LENGTH)
        cos, sin = cosine[rows, :], -sine[rows, :]
        at = [span(head * HD, HD) for head in every]
        grad_outs = [grad_attended[rows, at[h]] for h in every]
        probs = [near[seq * HEADS + h] for h in every]
        values = [qkv[rows, span(2 * D + h * HD, HD)] for h in every]
        grad_values = [dot_tn(prob, grad_out) for prob, grad_out in zip(probs, grad_outs)]
        if picked is not None:
            probs = [jnp.concatenate([probs[h], far[seq * HEADS + h]], axis=1) for h in every]
            values = [jnp.concatenate([values[h], picked[1, seq, h]], axis=0) for h in every]
        probs = [prob.astype(FULL) for prob in probs]
        grads = [dot_nt(grad_out, value) for grad_out, value in zip(grad_outs, values)]
        deltas = [jnp.sum(prob * grad, axis=-1, keepdims=True) for prob, grad in zip(probs, grads)]
        grads = [(prob * (grad - delta)).astype(LOW) for prob, grad, delta in zip(probs, grads, deltas)]
        for h in every:
            grad_joined[rows, span(2 * D + h * HD, HD)] = grad_values[h].astype(LOW)
        queries = [dot(grads[h][:, :LENGTH], qkv[rows, span(D + h * HD, HD)]) * SCALE for h in every]
        keys = [dot_tn(grads[h][:, :LENGTH], qkv[rows, at[h]]) * SCALE for h in every]
        queries = [turn(query, cos, sin) for query in queries]
        keys = [turn(key, cos, sin) for key in keys]
        if picked is not None:
            queries = [queries[h] + dot(grads[h][:, LENGTH:], picked[0, seq, h]) * SCALE for h in every]
        for h in every:
            grad_joined[rows, at[h]] = queries[h].astype(LOW)
            grad_joined[rows, span(D + h * HD, HD)] = keys[h].astype(LOW)


def attend_backward(x, gain, w_qkv, grad_joined, grad_middle, normed, result, gain_grad):
    for start in range(0, D, TILE):
        result[:, span(start, TILE)] = dot_nt(grad_joined[...], w_qkv[span(start, TILE), :])
    unit, inverse_rms = unit_rows(x[...])
    normed[...] = (unit * gain[0:1, :]).astype(LOW)
    grad = result[...]
    gain_grad[0:1, :] = jnp.sum(grad * unit, axis=0, keepdims=True)
    result[...] = grad_middle[...] + norm_back(grad, unit, inverse_rms, gain[0:1, :])


EARLY = HALF + FF
WIDE = 2 * FF + HALF
LATE = 4 * D + 2 * HALF
GAINS = span(ROWS, 16)
LOWER, UPPER = span(0, HALF), span(HALF, HALF)
OWN = {name: span(at * HALF, HALF) for at, name in enumerate(("h2", "e", "h1", "o"))}


class Copies:
    def __init__(self, semaphores):
        self.semaphores, self.used, self.groups = semaphores, 0, {}

    def copy(self, at, source, target):
        source, target = (view[0].at[view[1]] if isinstance(view, tuple) else view for view in (source, target))
        return pltpu.make_async_copy(source, target, self.semaphores.at[at])

    def start(self, name, source, target):
        self.copy(self.used, source, target).start()
        self.groups.setdefault(name, []).append((self.used, source, target))
        self.used += 1

    def wait(self, *names):
        for name in names:
            for copy in self.groups.pop(name):
                self.copy(*copy).wait()

    def finish(self):
        self.wait(*list(self.groups))


def y_runs():
    return [(0, (0, PART), 0), (1, (0, PART), PART), (2, (0, PART // 2), 2 * PART)] + [
        (3, (0, PART // 2), 2 * PART + PART // 2),
        (4, (0, PART), 3 * PART),
    ]


def z_runs():
    runs = []
    for piece, dz, low, high in ((0, 0, 0, 4), (1, 1, 0, 4), (2, 2, 0, 2), (3, 2, 2, 4), (4, 3, 0, 4)):
        runs += [(piece, ((dy - low) * RUN, RUN), dy * PART + dz * RUN) for dy in range(low, high)]
    return runs


def load(copies, name, pieces, runs, columns, target, target_columns):
    for core in range(NC):
        for piece, (low, size), row in runs:
            source = pieces[core * 5 + piece], (span(low, size), columns)
            copies.start(name, source, (target, (span(core * HALF + row, size), target_columns)))


def load_qkv(copies, second, target):
    for at in range(3):
        columns = span(at * D, D)
        load(copies, f"qkv{at * D}", second, z_runs(), columns, target, columns)


def wait_qkv(copies):
    return lambda start: copies.wait(f"qkv{start}") if start % D == 0 else None


def load_out(copies, second, target):
    load(copies, "out", second, z_runs(), span(3 * D, D), target, span(0, D))


def load_gains(copies, second, target):
    load(copies, "gains", second, z_runs(), span(4 * D + CUT, PAD), target, span(0, PAD))


def load_gate(copies, first, target):
    for core in range(NC):
        for piece, (low, size), row in y_runs():
            row += core * HALF
            source = first[core * 5 + piece], (span(low, size), span(0, 2 * FF))
            copies.start(f"gate{row // TILE * TILE}", source, (target, (span(row, size), span(0, 2 * FF))))


GATE = tuple(f"gate{at}" for at in range(0, D, TILE))
DOWN = tuple(f"down{at}" for at in range(0, FF, D))


def load_down(copies, first, second, target, also=None):
    for start in range(0, FF, D):
        name = f"down{start}"
        if start < CUT:
            load(copies, name, second, z_runs(), span(4 * D + start, D), target, span(start, D))
        else:
            load(copies, name, first, y_runs(), span(2 * FF, FF - CUT), target, span(CUT, FF - CUT))
        if also:
            also(name, start, min(D, FF - start))


def kernel_first(section, core, *refs):
    (x, spread, cosine, sine, place), refs = refs[:5], refs[5:]
    first, second, refs = refs[:10], refs[10:20], refs[20:]
    (sent_o, qkv_o, near_o, late_o, middle_o, early_o, gate_up_o, own_o, gain_o), refs = refs[:9], refs[9:]
    xs, gains, cos, sin, places, w_qkv, w_out, w_gate, w_down = refs[:9]
    qkv, near, attended, attended_rel, middle, normed_two, gate_up, hidden, sent, spreads, gain_rows, semaphores = refs[9:]

    copies = Copies(semaphores)
    load_gains(copies, second, gain_rows)
    copies.start("gains", spread, spreads)

    @pl.when(section[0] == 0)
    def _():
        for source, target in ((x, xs), (cosine, cos), (sine, sin)):
            copies.start("small", source, target)
        load_qkv(copies, second, w_qkv)
        copies.start("place", place, places)
        load_out(copies, second, w_out)
        load_gate(copies, first, w_gate)
        load_down(copies, first, second, w_down)

    copies.wait("gains")
    rows = gain_rows[...].astype(FULL).T[:8].astype(LOW)
    low = lax.broadcasted_iota(jnp.int32, (1, D), 1) < HALF
    straight = jnp.logical_xor(low, core[0] == 1)
    for at in range(2):
        picked = dot(rows, spreads[at])
        gains[at : at + 1, :] = jnp.where(straight, picked[0:1], picked[1:2])
    copies.start("gain", gains, gain_o)

    @pl.when(section[0] == 0)
    def _():
        copies.wait("small")
        attend_forward(xs, gains, cos, sin, w_qkv, qkv, None, wait_qkv(copies))
        copies.start("done", qkv, qkv_o)
        heads_forward(qkv, None, None, None, near, None, attended)
        copies.start("done", near, near_o)
        copies.wait("place", "out")
        out_forward(xs, attended, places, w_out, attended_rel, middle)
        copies.start("done", attended_rel.at[:, LOWER], own_o.at[:, OWN["o"]])
        copies.start("done", attended_rel.at[:, UPPER], late_o.at[span(0, ROWS), span(4 * D + HALF, HALF)])
        copies.start("done", middle, middle_o)
        copies.wait(*GATE)
        ff_forward(middle, gains, w_gate, normed_two, gate_up, hidden)
        copies.start("done", normed_two.at[:, LOWER], own_o.at[:, OWN["h2"]])
        copies.start("done", normed_two.at[:, UPPER], early_o.at[:, LOWER])
        copies.start("done", gate_up, gate_up_o)
        copies.start("done", hidden, early_o.at[:, span(HALF, FF)])
        copies.wait(*DOWN)
        down_forward(middle, hidden, w_down, sent)
        copies.start("done", sent, sent_o)
        copies.wait("done")

    copies.wait("gain")


def two_parts(gain_grad):
    full = gain_grad[...]
    high = full.astype(LOW).astype(FULL)
    return jnp.concatenate([high, full - high, jnp.zeros((12, D), FULL)], axis=0).astype(LOW)


def kernel_last(section, counts, *refs):
    (x_low, upstream, gain, cosine, sine, place, picked), refs = refs[:7], refs[7:]
    first, second, refs = refs[:10], refs[10:20], refs[20:]
    refs = refs[3:]
    (early_o, late_o, own_o, result_o, sent_o, grad_ff_o), refs = refs[:6], refs[6:]
    xl, ups, up_low, gains, cos, sin, places, picks, w_qkv, w_out, w_gate, w_down = refs[:12]
    xs, qkv, plain, near, far, attended, attended_rel, middle, normed_two, gate_up, hidden, result = refs[12:24]
    grad_ff, grad_middle, branch, grad_joined, normed, gain_grad, gain_rows, semaphores = refs[24:]

    @pl.when(section[0] == 1)
    def _():
        copies = Copies(semaphores)
        for source, target in ((x_low, xl), (gain, gains), (cosine, cos), (sine, sin)):
            copies.start("small", source, target)
        load_qkv(copies, second, w_qkv)
        copies.start("picks", picked, picks)
        copies.start("place", place, places)
        load_out(copies, second, w_out)
        load_gate(copies, first, w_gate)
        load_down(copies, first, second, w_down)
        copies.start("up", upstream, ups)
        copies.wait("small")
        xs[...] = xl[...].astype(FULL)
        attend_forward(xs, gains, cos, sin, w_qkv, qkv, plain, wait_qkv(copies))
        copies.wait("picks")
        heads_forward(qkv, plain, picks, counts, near, far, attended)
        copies.wait("place", "out")
        out_forward(xs, attended, places, w_out, attended_rel, middle)
        copies.start("done", attended_rel.at[:, LOWER], own_o.at[:, OWN["o"]])
        copies.start("done", attended_rel.at[:, UPPER], late_o.at[span(0, ROWS), span(4 * D + HALF, HALF)])
        copies.wait(*GATE)
        ff_forward(middle, gains, w_gate, normed_two, gate_up, hidden)
        copies.start("done", normed_two.at[:, LOWER], own_o.at[:, OWN["h2"]])
        copies.start("done", normed_two.at[:, UPPER], early_o.at[:, LOWER])
        copies.start("done", hidden, early_o.at[:, span(HALF, FF)])
        copies.wait(*DOWN, "up")
        up_low[...] = ups[...].astype(LOW)
        copies.start("done", up_low.at[:, LOWER], own_o.at[:, OWN["e"]])
        copies.start("done", up_low.at[:, UPPER], grad_ff_o.at[:, span(2 * FF, HALF)])
        down_forward(middle, hidden, w_down, result)
        copies.start("result", result, result_o)
        gate_backward(up_low, w_down, gate_up, grad_ff)
        copies.start("done", grad_ff, grad_ff_o.at[:, span(0, 2 * FF)])
        ff_backward(ups, middle, gains, w_gate, grad_ff, grad_middle, gain_grad)
        out_backward(grad_middle, places, w_out, branch, attended)
        copies.start("done", branch, late_o.at[span(0, ROWS), span(3 * D, D)])
        heads_backward(qkv, picks, near, far, attended, cos, sin, grad_joined)
        copies.start("done", grad_joined, late_o.at[span(0, ROWS), span(0, 3 * D)])
        copies.wait("result")
        attend_backward(xs, gains, w_qkv, grad_joined, grad_middle, normed, result, gain_grad)
        xl[...] = result[...].astype(LOW)
        copies.start("done", xl, sent_o)
        copies.start("done", normed.at[:, LOWER], own_o.at[:, OWN["h1"]])
        copies.start("done", normed.at[:, UPPER], late_o.at[span(0, ROWS), span(4 * D, HALF)])
        gain_rows[...] = two_parts(gain_grad)
        copies.start("done", gain_rows, late_o.at[GAINS, span(0, D)])
        copies.finish()


def kernel_back_gate(section, *refs):
    (upstream, gate_up), refs = refs[:2], refs[2:]
    first, second, refs = refs[:10], refs[10:20], refs[20:]
    refs = refs[3:]
    (grad_ff_o, own_o), refs = refs[:2], refs[2:]
    ups, gate_ups, w_down, grad_ff, semaphores = refs

    @pl.when(section[0] == 0)
    def _():
        copies = Copies(semaphores)
        copies.start("up", upstream, ups)

        def saved(name, start, size):
            for columns in (span(start, size), span(FF + start, size)):
                copies.start(name, gate_up.at[:, columns], gate_ups.at[:, columns])

        load_down(copies, first, second, w_down, saved)
        copies.wait("up")
        copies.start("done", ups.at[:, LOWER], own_o.at[:, OWN["e"]])
        copies.start("done", ups.at[:, UPPER], grad_ff_o.at[:, span(2 * FF, HALF)])
        gate_backward(
            ups, w_down, gate_ups, grad_ff, lambda start: copies.wait(f"down{start}") if start % D == 0 else None
        )
        copies.start("done", grad_ff, grad_ff_o.at[:, span(0, 2 * FF)])
        copies.finish()


def kernel_back_ff(section, *refs):
    (upstream, gain, middle, grad_ff), refs = refs[:4], refs[4:]
    first, refs = refs[:10], refs[11:]
    (grad_middle_o, gain_grad_o), refs = refs[:2], refs[2:]
    ups, gains, mid, grad_ffs, w_gate, grad_middle, gain_grad, semaphores = refs

    @pl.when(section[0] == 0)
    def _():
        copies = Copies(semaphores)
        copies.start("first", grad_ff.at[:, span(0, 2 * FF)], grad_ffs)
        load_gate(copies, first, w_gate)
        copies.start("late", upstream, ups)
        copies.start("late", middle, mid)
        copies.start("late", gain, gains)
        copies.wait("first")

        def wait(start):
            copies.wait(f"gate{start}")
            if start == D - TILE:
                copies.wait("late")

        ff_backward(ups, mid, gains, w_gate, grad_ffs, grad_middle, gain_grad, wait)
        copies.start("done", grad_middle, grad_middle_o)
        copies.start("done", gain_grad, gain_grad_o)
        copies.finish()


def kernel_back_attend(section, *refs):
    (x, gain, cosine, sine, place, qkv, near, grad_middle, gain_part), refs = refs[:9], refs[9:]
    second, refs = refs[:10], refs[11:]
    (late_o, own_o, result_o), refs = refs[3:6], refs[6:]
    xs, gains, cos, sin, places, qkvs, nears, grad_mid, w_qkv, w_out = refs[:10]
    grad_attended, branch, grad_joined, normed, result, gain_grad, gain_rows, semaphores = refs[10:]

    @pl.when(section[0] == 0)
    def _():
        copies = Copies(semaphores)
        copies.start("mid", grad_middle, grad_mid)
        copies.start("mid", place, places)
        load_out(copies, second, w_out)
        for source, target in ((qkv, qkvs), (near, nears), (cosine, cos), (sine, sin)):
            copies.start("saved", source, target)
        load_qkv(copies, second, w_qkv)
        for source, target in ((x, xs), (gain, gains), (gain_part, gain_grad)):
            copies.start("late", source, target)
        copies.wait("mid", "out")
        out_backward(grad_mid, places, w_out, branch, grad_attended)
        copies.start("done", branch, late_o.at[span(0, ROWS), span(3 * D, D)])
        copies.wait("saved")
        heads_backward(qkvs, None, nears, None, grad_attended, cos, sin, grad_joined)
        copies.start("done", grad_joined, late_o.at[span(0, ROWS), span(0, 3 * D)])
        copies.wait("qkv0", f"qkv{D}", f"qkv{2 * D}", "late")
        attend_backward(xs, gains, w_qkv, grad_joined, grad_mid, normed, result, gain_grad)
        copies.start("done", result, result_o)
        copies.start("done", normed.at[:, LOWER], own_o.at[:, OWN["h1"]])
        copies.start("done", normed.at[:, UPPER], late_o.at[span(0, ROWS), span(4 * D, HALF)])
        gain_rows[...] = two_parts(gain_grad)
        copies.start("done", gain_rows, late_o.at[GAINS, span(0, D)])
        copies.finish()


def shape(*dims, dtype=LOW):
    return jax.ShapeDtypeStruct(dims, dtype)


def vmem(*dims, dtype=LOW):
    return pltpu.VMEM(dims, dtype)


Y_COPIES, Z_COPIES = 2 * 5, 2 * 16
QKV_COPIES, DOWN_COPIES = 3 * Z_COPIES, 2 * Z_COPIES + Y_COPIES
W_QKV, W_OUT, W_GATE, W_DOWN = vmem(D, 3 * D), vmem(D, D), vmem(D, 2 * FF), vmem(D, FF)


def call(kernel, operands, scalars, outs, scratch, copies, aliases=None):
    return pl.pallas_call(
        kernel,
        out_shape=outs,
        in_specs=[SMEM] * scalars + [HBM] * (len(operands) - scalars),
        out_specs=[HBM] * len(outs),
        scratch_shapes=list(scratch) + [pltpu.SemaphoreType.DMA((copies,))],
        input_output_aliases=aliases or {},
        compiler_params=pltpu.CompilerParams(vmem_limit_bytes=62 * MIB),
        cost_estimate=pl.CostEstimate(flops=1000, bytes_accessed=1000, transcendentals=0),
    )(*operands)


def run_first(section, core, x, spread, cosine, sine, place, first, second):
    outs = [
        shape(ROWS, D), shape(ROWS, 3 * D), shape(COUNT * HEADS, LENGTH, LENGTH), shape(ROWS + 16, LATE),
        shape(ROWS, D, dtype=FULL), shape(ROWS, EARLY), shape(ROWS, 2 * FF), shape(ROWS, 4 * HALF),
        shape(2, D, dtype=FULL),
    ]
    scratch = [vmem(ROWS, D, dtype=FULL), vmem(2, D, dtype=FULL), vmem(ROWS, HD, dtype=FULL), vmem(ROWS, HD, dtype=FULL)]
    scratch += [vmem(D, D), W_QKV, W_OUT, W_GATE, W_DOWN]
    scratch += [vmem(ROWS, 3 * D), vmem(COUNT * HEADS, LENGTH, LENGTH), vmem(ROWS, D), vmem(ROWS, D)]
    scratch += [vmem(ROWS, D, dtype=FULL), vmem(ROWS, D), vmem(ROWS, 2 * FF), vmem(ROWS, FF), vmem(ROWS, D)]
    scratch += [vmem(2, D, D), vmem(D, PAD)]
    operands = [section, core, x, spread, cosine, sine, place, *first, *second]
    return call(kernel_first, operands, 2, outs, scratch, 24 + Y_COPIES + 2 * Z_COPIES + QKV_COPIES + DOWN_COPIES)


def run_last(section, counts, x_low, upstream, gain, cosine, sine, place, picked, first, second, kept):
    outs = [shape(ROWS, EARLY), shape(ROWS + 16, LATE), shape(ROWS, 4 * HALF), shape(ROWS, D, dtype=FULL)]
    outs += [shape(ROWS, D), shape(ROWS, WIDE)]
    scratch = [vmem(ROWS, D), vmem(ROWS, D, dtype=FULL), vmem(ROWS, D), vmem(2, D, dtype=FULL)]
    scratch += [vmem(ROWS, HD, dtype=FULL), vmem(ROWS, HD, dtype=FULL), vmem(D, D), vmem(2, COUNT, HEADS, LENGTH, HD)]
    scratch += [W_QKV, W_OUT, W_GATE, W_DOWN]
    scratch += [vmem(ROWS, D, dtype=FULL), vmem(ROWS, 3 * D), vmem(ROWS, D)]
    scratch += [vmem(COUNT * HEADS, LENGTH, LENGTH)] * 2
    scratch += [vmem(ROWS, D), vmem(ROWS, D), vmem(ROWS, D, dtype=FULL), vmem(ROWS, D), vmem(ROWS, 2 * FF)]
    scratch += [vmem(ROWS, FF), vmem(ROWS, D, dtype=FULL)]
    scratch += [vmem(ROWS, 2 * FF), vmem(ROWS, D, dtype=FULL), vmem(ROWS, D), vmem(ROWS, 3 * D), vmem(ROWS, D)]
    scratch += [vmem(2, D, dtype=FULL), vmem(16, D)]
    operands = [section, counts, x_low, upstream, gain, cosine, sine, place, picked, *first, *second, *kept]
    aliases = {len(operands) - 3 + i: i for i in range(3)}
    return call(kernel_last, operands, 2, outs, scratch, 24 + Y_COPIES + Z_COPIES + QKV_COPIES + DOWN_COPIES, aliases)


def run_back_gate(section, upstream, gate_up, first, second, early, grad_ff, own):
    outs = [shape(ROWS, WIDE), shape(ROWS, 4 * HALF)]
    scratch = [vmem(ROWS, D), vmem(ROWS, 2 * FF), W_DOWN, vmem(ROWS, 2 * FF)]
    operands = [section, upstream, gate_up, *first, *second, early, grad_ff, own]
    at = len(operands) - 2
    return call(
        kernel_back_gate, operands, 1, outs, scratch, 16 + DOWN_COPIES, {at: 0, at + 1: 1}
    )


def run_back_ff(section, upstream, gain, middle, grad_ff, first, after):
    outs = [shape(ROWS, D, dtype=FULL), shape(2, D, dtype=FULL)]
    scratch = [vmem(ROWS, D), vmem(2, D, dtype=FULL), vmem(ROWS, D, dtype=FULL), vmem(ROWS, 2 * FF)]
    scratch += [W_GATE, vmem(ROWS, D, dtype=FULL), vmem(2, D, dtype=FULL)]
    operands = [section, upstream, gain, middle, grad_ff, *first, after]
    return call(kernel_back_ff, operands, 1, outs, scratch, 10 + Y_COPIES)


def run_back_attend(section, x, gain, cosine, sine, place, qkv, near, grad_middle, gain_part, second, after, kept):
    outs = [shape(ROWS + 16, LATE), shape(ROWS, 4 * HALF), shape(ROWS, D, dtype=FULL)]
    scratch = [vmem(ROWS, D, dtype=FULL), vmem(2, D, dtype=FULL), vmem(ROWS, HD, dtype=FULL), vmem(ROWS, HD, dtype=FULL)]
    scratch += [vmem(D, D), vmem(ROWS, 3 * D), vmem(COUNT * HEADS, LENGTH, LENGTH), vmem(ROWS, D, dtype=FULL)]
    scratch += [W_QKV, W_OUT, vmem(ROWS, D), vmem(ROWS, D), vmem(ROWS, 3 * D), vmem(ROWS, D), vmem(ROWS, D, dtype=FULL)]
    scratch += [vmem(2, D, dtype=FULL), vmem(16, D)]
    operands = [section, x, gain, cosine, sine, place, qkv, near, grad_middle, gain_part, *second, after, *kept]
    at = len(operands) - 3
    return call(
        kernel_back_attend, operands, 1, outs, scratch, 20 + Z_COPIES + QKV_COPIES, {at + i: i for i in range(3)}
    )


def pick_kernel(memory, index, out):
    chosen = index[0, 0]
    hot = (lax.broadcasted_iota(jnp.int32, (memory.shape[2], LENGTH), 0) == chosen).astype(FULL).astype(LOW)
    for kind in range(2):
        out[kind, 0, 0] = dot_tn(hot, memory[0, kind]).astype(LOW)


def run_pick(memory, mem_index):
    slots = memory.shape[2]
    return pl.pallas_call(
        pick_kernel,
        grid=(COUNT, HEADS),
        in_specs=[
            pl.BlockSpec((1, 2, slots, HD), lambda n, h: (n, 0, 0, h)),
            pl.BlockSpec((1, 1, 1, LENGTH), lambda n, h: (n, h, 0, 0)),
        ],
        out_specs=pl.BlockSpec((2, 1, 1, LENGTH, HD), lambda n, h: (0, n, h, 0, 0)),
        out_shape=shape(2, COUNT, HEADS, LENGTH, HD),
    )(memory, mem_index.reshape(COUNT, HEADS, 1, LENGTH))


def z_first(rows):
    return jnp.concatenate([rows[span(dy * PART + dz * RUN, RUN), :] for dz in range(NZ) for dy in range(NY)], axis=0)


HALVES = PART // 2
QKV_CUT = 17 * 128
N_FF, N_Y, N_Z = FF + FF // 2, QKV_CUT, 3 * D - QKV_CUT + D + PAD
FF_PARTS = (
    (0, "e", "early", HALF, FF // 2, FF), (1, "e", "early", HALF + FF // 2, FF // 2, FF),
    (0, "h2", "wide", 0, FF, 0), (1, "h2", "wide", FF, FF, 0),
)
QKV_PARTS = (
    (1, "o", "late", 3 * D, D, 3 * D - QKV_CUT), (0, "h1", "late", 0, QKV_CUT, 0),
    (1, "h1", "late", QKV_CUT, 3 * D - QKV_CUT, 0), (1, None, None, 0, PAD, 3 * D - QKV_CUT + D),
)


def put(copies, staged, columns, targets):
    for source, (ref, rows, shift) in targets.items():
        at = span(columns.start + shift, columns.stop - columns.start)
        copies.start("done", staged.at[span(source * HALVES, HALVES), columns], ref.at[rows, at])


def products(copies, parts, sides, rights, stages, targets, extra=None):
    for z, left, right, first, size, at in parts:
        stage = stages[z]
        if left is None:
            stage[:, span(at, size)] = extra()
        else:
            own, other = sides(left)
            if z:
                own, other = z_first(own), z_first(other)
            mine, theirs = rights(right, first)
            for start in range(0, size, TILE):
                width = min(TILE, size - start)
                columns = span(first + start, width)
                product = dot(own, mine[:, columns]) + dot(other, theirs[:, columns])
                stage[:, span(at + start, width)] = product.astype(LOW)
        put(copies, stage, span(at, size), targets[z])


def ff_targets(own, ahead, behind, low, high):
    upper, lower = span(0, HALVES), span(HALVES, HALVES)
    return {
        4: (ahead, upper, 0), 3: (ahead, lower, 0), 5: (behind, upper, 0), 6: (behind, lower, 0),
        2: (low, upper, 0), 7: (high, upper, 0), 0: (own, upper, 0), 1: (own, lower, 0),
    }


def kernel_grad_ff(early, other_early, wide, other_wide, own, after, *refs):
    outs, (er, oer, wi, owi, ow, stage_y, stage_z, semaphores) = refs[:10], refs[10:]
    copies = Copies(semaphores)
    tail = span(2 * FF, HALF)
    copies.start("a", other_wide.at[:, tail], owi.at[:, tail])
    for source, target in ((early, er), (other_early, oer), (own, ow)):
        copies.start("a", source, target)
    for at in range(2):
        for source, target in ((wide, wi), (other_wide, owi)):
            copies.start(f"b{at * FF}", source.at[:, span(at * FF, FF)], target.at[:, span(at * FF, FF)])
    copies.wait("a")
    left = {"e": (ow[:, OWN["e"]].T, owi[:, tail].T), "h2": (ow[:, OWN["h2"]].T, oer[:, LOWER].T)}

    def rights(name, first):
        if name == "wide":
            copies.wait(f"b{first}")
        return (wi, owi) if name == "wide" else (er, oer)

    targets = ff_targets(*outs[:5]), ff_targets(*outs[5:])
    products(copies, FF_PARTS, left.get, rights, (stage_y, stage_z), targets)
    copies.finish()


def run_grad_ff(early, other_early, wide, other_wide, own, after):
    scratch = [vmem(ROWS, EARLY)] * 2 + [vmem(ROWS, WIDE)] * 2 + [vmem(ROWS, 4 * HALF)] + [vmem(HALF, N_FF)] * 2
    outs = [shape(rows, N_FF) for rows in (PART, PART, PART, HALVES, HALVES)] * 2
    operands = [early, other_early, wide, other_wide, own, after]
    outs = call(kernel_grad_ff, operands, 0, outs, scratch, 8 + 8 * 4)
    return outs[:5], outs[5:]


def kernel_grad_attend(late, other_late, own, pack, *refs):
    outs, (la, ola, ow, pa, stage_y, stage_z, semaphores) = refs[:10], refs[10:]
    copies = Copies(semaphores)
    copies.start("a", own, ow)
    tail = span(3 * D, LATE - 3 * D)
    for name, columns in (("a", tail), ("b0", span(0, QKV_CUT)), (f"b{QKV_CUT}", span(QKV_CUT, 3 * D - QKV_CUT))):
        for source, target in ((late, la), (other_late, ola)):
            copies.start(name, source.at[:, columns], target.at[:, columns])
    copies.start("pack", pack, pa)
    copies.wait("a")
    left = {
        "h1": (ow[:, OWN["h1"]].T, ola[span(0, ROWS), span(4 * D, HALF)].T),
        "o": (ow[:, OWN["o"]].T, ola[span(0, ROWS), span(4 * D + HALF, HALF)].T),
    }

    def extra():
        copies.wait("pack")
        mine, theirs = la[GAINS, span(0, D)], ola[GAINS, span(0, D)]
        theirs = jnp.concatenate([theirs[:, UPPER], theirs[:, LOWER]], axis=1)
        columns = []
        for at in range(2):
            matrix = pa[at]
            first = dot(mine, matrix[:D]) + dot(theirs, matrix[:D])
            second = dot(mine, matrix[D:]) + dot(theirs, matrix[D:])
            columns.append(first[0:1] + first[2:3] + second[1:2] + second[3:4])
        rows = jnp.concatenate(columns + [jnp.zeros((PAD - 2, HALF), FULL)], axis=0)
        return z_first(rows.T).astype(LOW)

    mine, theirs = la.at[span(0, ROWS), :], ola.at[span(0, ROWS), :]

    def rights(name, first):
        if first < 3 * D:
            copies.wait(f"b{first}")
        return mine, theirs

    targets = ff_targets(*outs[:5]), ff_targets(*outs[5:])
    products(copies, QKV_PARTS, left.get, rights, (stage_y, stage_z), targets, extra)
    copies.finish()


def run_grad_attend(late, other_late, own, pack):
    scratch = [vmem(ROWS + 16, LATE)] * 2 + [vmem(ROWS, 4 * HALF), vmem(2, 2 * D, HALF), vmem(HALF, N_Y), vmem(HALF, N_Z)]
    outs = [shape(rows, width) for width in (N_Y, N_Z) for rows in (PART, PART, PART, HALVES, HALVES)]
    operands = [late, other_late, own, pack]
    outs = call(kernel_grad_attend, operands, 0, outs, scratch, 10 + 8 * 4)
    return outs[:5], outs[5:]


def kernel_low(gate_up, down, qkv, out, gains, first, second):
    first[:, span(0, 2 * FF)] = gate_up[0].astype(LOW)
    first[:, span(2 * FF, FF - CUT)] = down[0, :, CUT:].astype(LOW)
    second[:, span(0, 3 * D)] = qkv[0].astype(LOW)
    second[:, span(3 * D, D)] = out[0].astype(LOW)
    second[:, span(4 * D, CUT)] = down[0, :, :CUT].astype(LOW)
    row = lax.broadcasted_iota(jnp.int32, (BLOCK, 2 * BLOCK), 0)
    lane = lax.broadcasted_iota(jnp.int32, (BLOCK, 2 * BLOCK), 1)
    column = lax.broadcasted_iota(jnp.int32, (BLOCK, PAD), 1)
    block = jnp.zeros((BLOCK, PAD), FULL)
    for at in range(2):
        own = jnp.sum(jnp.where(lane == row + at * BLOCK, gains[...], 0.0), axis=1, keepdims=True)
        block = block + jnp.where(column == at, own, 0.0)
    second[:, span(4 * D + CUT, PAD)] = block.astype(LOW)


def run_low(gate_up, down, qkv, out, gains):
    return pl.pallas_call(
        kernel_low, out_shape=[shape(BLOCK, 3 * FF - CUT), shape(BLOCK, 4 * D + CUT + PAD)]
    )(gate_up, down, qkv, out, gains)


def kernel_last_sums(y, z, *refs):
    blocks, (qkv, out, gate_up, down, gains) = refs[:8], refs[8:]
    rest = 3 * D - QKV_CUT
    total_y, total_z = y[:BLOCK].astype(FULL), z[:BLOCK].astype(FULL)
    for at in range(3):
        total_y = total_y + blocks[at][:BLOCK].astype(FULL)
        total_z = total_z + blocks[4 + at][:BLOCK].astype(FULL)
    total_y = total_y + blocks[3][...].astype(FULL)
    total_z = total_z + blocks[7][...].astype(FULL)
    gate_up[0, :, span(0, FF)] = total_y[:, :FF]
    gate_up[0, :, span(FF, FF)] = total_z[:, :FF]
    down[0, :, span(0, FF // 2)] = total_y[:, FF:N_FF]
    down[0, :, span(FF // 2, FF // 2)] = total_z[:, FF:N_FF]
    qkv[0, :, span(0, QKV_CUT)] = total_y[:, N_FF:]
    qkv[0, :, span(QKV_CUT, rest)] = total_z[:, N_FF : N_FF + rest]
    out[0] = total_z[:, N_FF + rest : N_FF + rest + D]
    gains[...] = total_z[:, N_FF + rest + D :]


def run_last_sums(y, z):
    outs = [shape(1, BLOCK, size, dtype=FULL) for size in (3 * D, D, 2 * FF, FF)] + [shape(BLOCK, PAD, dtype=FULL)]
    return pl.pallas_call(kernel_last_sums, out_shape=outs)(y[0], z[0], *y[1:], *z[1:])


def hop(block, axis, step):
    count = lax.axis_size(axis)
    return lax.ppermute(block, axis, [(at, (at + step) % count) for at in range(count)])


def gather_near(block, axis):
    pair = jnp.concatenate([block, hop(block, "xh", 1)])
    ahead = hop(pair, axis, -1)
    behind = hop(pair, axis, 1)
    across = hop(ahead, axis, -1)
    return jnp.concatenate([pair, ahead, across, behind])


def gather_far(whole, behind, ahead, axis):
    low = hop(behind[: PART // 2], axis, 1)
    high = hop(ahead[PART // 2 :], axis, -1)
    own = [whole, ahead, low, high, behind]
    return own + [hop(piece, "core", 1) for piece in own]


def total(*terms):
    result = terms[0].astype(FULL)
    for term in terms[1:]:
        result = result + term.astype(FULL)
    return result


def scatter_begin(blocks, axis):
    return hop(blocks[1], axis, 1), hop(blocks[2], axis, -1)


def scatter_sums(blocks, begun):
    return total(blocks[3], begun[0][:HALVES]).astype(LOW), total(blocks[4], begun[1][:HALVES]).astype(LOW)


def scatter_main(sums, axis):
    return hop(sums[0], axis, 1), hop(sums[1], axis, -1)


def scatter_halves(blocks, begun, main):
    low, high = [], []
    for block, (ahead, behind), (main_low, main_high) in zip(blocks, begun, main):
        low.append(total(block[0][:HALVES], behind[HALVES:], main_low))
        high.append(total(block[0][HALVES:], ahead[HALVES:], main_high))
    return jnp.concatenate(low, axis=1), jnp.concatenate(high, axis=1)


def scatter_end(low, high, axis):
    one = hop(low[RUN:].astype(LOW), axis, 1)
    two = hop(high[:RUN].astype(LOW), axis, 2)
    three = hop(high[RUN:].astype(LOW), axis, -1)
    low = low[:RUN].astype(LOW)
    other = hop(total(low[BLOCK:], one[BLOCK:], two[BLOCK:], three[BLOCK:]).astype(LOW), "xh", 1)
    return low, one, two, three, other


def natural_of(rel, run, at):
    lane = rel % run
    rel = rel // run
    xx = (rel % NX + at[2]) % NX
    zz = (rel // NX % NZ + at[1]) % NZ
    yy = (rel // (NX * NZ) % NY + at[0]) % NY
    cc = (rel // (NX * NZ * NY) + at[3]) % NC
    return (((yy * NZ + zz) * NX + xx) * NC + cc) * run + lane


def place_matrix(at):
    natural = natural_of(jnp.arange(D), BLOCK, at)
    return (jnp.arange(D)[:, None] == natural[None, :]).astype(LOW)


def spread_matrix(at):
    natural = natural_of(jnp.arange(D), BLOCK, at)
    wanted = natural // (2 * BLOCK) * BLOCK + natural % BLOCK + jnp.arange(2)[:, None] * HALF
    return (natural[None, :, None] == wanted[:, None, :]).astype(LOW)


def pack_matrix(at):
    row = natural_of(jnp.arange(HALF), BLOCK, at)
    wanted = (row // BLOCK * (2 * BLOCK) + row % BLOCK)[None, :] + jnp.arange(2)[:, None] * BLOCK
    source = (jnp.arange(2)[:, None] * D + natural_of(jnp.arange(D), BLOCK, at)[None, :]).reshape(-1)
    return (wanted[:, None, :] == source[None, :, None]).astype(LOW)


def rotary_tables():
    half_dim = HD // 2
    rate_list = 10000.0 ** (-jnp.arange(half_dim, dtype=FULL) / half_dim)
    angles = jnp.arange(LENGTH, dtype=FULL)[:, None] * rate_list[None, :]
    cosine, sine = jnp.cos(angles), jnp.sin(angles)
    cosine = jnp.concatenate([cosine, cosine], axis=1)
    sine = jnp.concatenate([-sine, sine], axis=1)
    return jnp.tile(cosine, (COUNT, 1)), jnp.tile(sine, (COUNT, 1))


def local(boundary, w_qkv, w_out, w_gate_up, w_down_t, gains, memory, mem_index, mem_counts):
    section = lax.axis_index("section").astype(jnp.int32).reshape(1)
    core = lax.axis_index("core").astype(jnp.int32).reshape(1)
    first, second = run_low(w_gate_up, w_down_t, w_qkv, w_out, gains)
    first = gather_near(first, "z")
    second = gather_near(second, "y")
    at = tuple(lax.axis_index(name) for name in DP)
    at, boundary, first, second = lax.optimization_barrier((at, boundary, first, second))
    first_behind, first_ahead = hop(first, "y", 1), hop(first, "y", -1)
    second_behind, second_ahead = hop(second, "z", 1), hop(second, "z", -1)
    place = place_matrix(at)
    pack = pack_matrix(at)
    spread = spread_matrix(at)
    cosine, sine = rotary_tables()
    edge = dot(boundary.reshape(ROWS, D), place, lax.Precision.HIGHEST)
    moved, prepared = lax.optimization_barrier(
        ((first_behind, first_ahead, second_behind, second_ahead), (place, pack, spread, cosine, sine, edge))
    )
    first_behind, first_ahead, second_behind, second_ahead = moved
    place, pack, spread, cosine, sine, edge = prepared
    first = gather_far(first, first_behind, first_ahead, "y")
    second = gather_far(second, second_behind, second_ahead, "z")
    picked = run_pick(memory, mem_index)

    sent, qkv, near, late, middle, early, gate_up, own, gain = run_first(
        section, core, edge, spread, cosine, sine, place, first, second
    )
    moved = lax.ppermute(sent, "section", [(0, 1)])
    early, late, own, result, sent, wide = run_last(
        section, mem_counts, moved, edge, gain, cosine, sine, place, picked, first, second, (early, late, own)
    )
    upstream = lax.ppermute(sent, "section", [(1, 0)])
    other_early = hop(early, "core", 1)
    wide, own = run_back_gate(section, upstream, gate_up, first, second, other_early, wide, own)
    other_wide = hop(wide, "core", 1)
    gate_y, gate_z = run_grad_ff(early, other_early, wide, other_wide, own, upstream)
    begun_gate_y = scatter_begin(gate_y, "y")
    begun_gate_z = scatter_begin(gate_z, "z")
    grad_middle, gain_part = run_back_ff(section, upstream, gain, middle, wide, first, gate_z[0])
    late, own, result = run_back_attend(
        section, edge, gain, cosine, sine, place, qkv, near, grad_middle, gain_part, second, gate_z[0],
        (late, own, result),
    )
    other_late = hop(late, "core", 1)
    sums_y, sums_z = scatter_sums(gate_y, begun_gate_y), scatter_sums(gate_z, begun_gate_z)
    other_late, sums_y, sums_z = lax.optimization_barrier((other_late, sums_y, sums_z))
    main_gate_y, main_gate_z = scatter_main(sums_y, "y"), scatter_main(sums_z, "z")
    qkv_y, qkv_z = run_grad_attend(late, other_late, own, pack)
    qkv_y, qkv_z, main_gate_y, main_gate_z = lax.optimization_barrier((qkv_y, qkv_z, main_gate_y, main_gate_z))
    begun_qkv_y = scatter_begin(qkv_y, "y")
    begun_qkv_z = scatter_begin(qkv_z, "z")
    finals = dot(result, place.T, lax.Precision.HIGHEST).reshape(1, COUNT, LENGTH, D)
    begun_qkv_y, begun_qkv_z, finals = lax.optimization_barrier((begun_qkv_y, begun_qkv_z, finals))
    main_qkv_y = scatter_main(scatter_sums(qkv_y, begun_qkv_y), "y")
    main_qkv_z = scatter_main(scatter_sums(qkv_z, begun_qkv_z), "z")
    low_y, high_y = scatter_halves((gate_y, qkv_y), (begun_gate_y, begun_qkv_y), (main_gate_y, main_qkv_y))
    low_z, high_z = scatter_halves((gate_z, qkv_z), (begun_gate_z, begun_qkv_z), (main_gate_z, main_qkv_z))
    y, z = scatter_end(low_y, high_y, "z"), scatter_end(low_z, high_z, "y")
    qkv_grad, out_grad, gate_grad, down_grad, gain_grad = run_last_sums(y, z)
    return finals, qkv_grad, out_grad, gate_grad, down_grad, gain_grad[:, :2].T.reshape(1, -1)


def solution(mesh):
    mesh = Mesh(mesh.devices.reshape(2, NY, NZ, NX, NC), ("section",) + DP)
    in_specs = (
        P("section", DP, None, None),
        P("section", DP, None),
        P("section", DP, None),
        P("section", DP, None),
        P("section", DP, None),
        P("section", DP),
        P(DP, None, None, None),
        P(DP, None, None),
        P(DP),
    )
    return jax.shard_map(local, mesh=mesh, in_specs=in_specs, out_specs=in_specs[:6], check_vma=False)
```

```python
import functools

import jax
import jax.numpy as jnp
from jax import lax
from jax.experimental import pallas as pl
from jax.experimental.pallas import tpu as pltpu
from jax.sharding import Mesh
from jax.sharding import PartitionSpec as P

MASKED = -1e30
EPSILON = 1e-06
LOW = jnp.bfloat16
FULL = jnp.float32
NY, NZ, NX, NC = 4, 4, 2, 2
DP = ("y", "z", "xh", "core")
D, HEADS, HD, FF = 1024, 8, 128, 2816
COUNT, LENGTH = 2, 128
ROWS = COUNT * LENGTH
BLOCK = 16
HALF = D // 2
PART = D // (NC * NY)
RUN = PART // NZ
PAD = 128
CUT = 2048
TILE = 256
MIB = 1024 * 1024
SCALE = HD ** (-0.5)
HBM = pl.BlockSpec(memory_space=pltpu.HBM)
SMEM = pl.BlockSpec(memory_space=pltpu.SMEM)


def dot(left, right, precision=None):
    return jnp.dot(left, right, preferred_element_type=FULL, precision=precision)


def dot_nt(left, right):
    return lax.dot_general(left, right, (((1,), (1,)), ((), ())), preferred_element_type=FULL)


def dot_tn(left, right):
    return lax.dot_general(left, right, (((0,), (0,)), ((), ())), preferred_element_type=FULL)


def unit_rows(stream):
    inverse_rms = lax.rsqrt(jnp.mean(stream * stream, axis=-1, keepdims=True) + EPSILON)
    return stream * inverse_rms, inverse_rms


def turn(rows, cosine, sine):
    return rows * cosine + pltpu.roll(rows, HD // 2, 1) * sine


def span(start, size):
    return slice(start, start + size)


def no_wait(start):
    pass


def attend_forward(x, gain, cosine, sine, w_qkv, qkv, plain, wait):
    unit, _ = unit_rows(x[...])
    normed = (unit * gain[0:1, :]).astype(LOW)
    for start in range(0, 3 * D, TILE):
        wait(start)
        joined = dot(normed, w_qkv[:, span(start, TILE)])
        for at in range(start, start + TILE, HD):
            head = joined[:, span(at - start, HD)]
            if at < 2 * D:
                qkv[:, span(at, HD)] = turn(head, cosine[...], sine[...]).astype(LOW)
            else:
                qkv[:, span(at, HD)] = head.astype(LOW)
            if plain is not None and at < D:
                plain[:, span(at, HD)] = head.astype(LOW)


def causal():
    return lax.broadcasted_iota(jnp.int32, (LENGTH, LENGTH), 0) >= lax.broadcasted_iota(jnp.int32, (LENGTH, LENGTH), 1)


def heads_forward(qkv, plain, picked, counts, near, far, attended):
    keep = causal()
    every = range(HEADS)
    for seq in range(COUNT):
        rows = span(seq * LENGTH, LENGTH)
        at = [span(head * HD, HD) for head in every]
        scores = [dot_nt(qkv[rows, at[h]], qkv[rows, span(D + h * HD, HD)]) for h in every]
        scores = [jnp.where(keep, score * SCALE, MASKED) for score in scores]
        tops = [jnp.max(score, axis=-1, keepdims=True) for score in scores]
        if picked is not None:
            valid = lax.broadcasted_iota(jnp.int32, (LENGTH, LENGTH), 1) < counts[seq]
            memory = [dot_nt(plain[rows, at[h]], picked[0, seq, h]) for h in every]
            memory = [jnp.where(valid, score * SCALE, MASKED) for score in memory]
            tops = [jnp.maximum(top, jnp.max(score, axis=-1, keepdims=True)) for top, score in zip(tops, memory)]
        scores = [jnp.exp(score - top) for score, top in zip(scores, tops)]
        totals = [jnp.sum(score, axis=-1, keepdims=True) for score in scores]
        if picked is not None:
            memory = [jnp.exp(score - top) for score, top in zip(memory, tops)]
            totals = [part + jnp.sum(score, axis=-1, keepdims=True) for part, score in zip(totals, memory)]
        scales = [1.0 / part for part in totals]
        scores = [(score * scale).astype(LOW) for score, scale in zip(scores, scales)]
        values = [qkv[rows, span(2 * D + h * HD, HD)] for h in every]
        for h in every:
            near[seq * HEADS + h] = scores[h]
        if picked is not None:
            memory = [(score * scale).astype(LOW) for score, scale in zip(memory, scales)]
            for h in every:
                far[seq * HEADS + h] = memory[h]
            scores = [jnp.concatenate(both, axis=1) for both in zip(scores, memory)]
            values = [jnp.concatenate([values[h], picked[1, seq, h]], axis=0) for h in every]
        results = [dot(score, value) for score, value in zip(scores, values)]
        for h in every:
            attended[rows, at[h]] = results[h].astype(LOW)


def out_forward(x, attended, place, w_out, attended_rel, middle):
    attended_rel[...] = dot(attended[...], place[...]).astype(LOW)
    for start in range(0, D, 2 * TILE):
        out = dot(attended_rel[...], w_out[:, span(start, 2 * TILE)])
        high = out.astype(LOW)
        low = (out - high.astype(FULL)).astype(LOW)
        shard = place[span(start, 2 * TILE), :]
        moved = dot(high, shard) + dot(low, shard)
        middle[...] = (x[...] if start == 0 else middle[...]) + moved


def ff_forward(middle, gain, w_gate_up, normed_two, gate_up, hidden):
    unit, _ = unit_rows(middle[...])
    normed_two[...] = (unit * gain[1:2, :]).astype(LOW)
    for start in range(0, FF, TILE):
        gate = dot(normed_two[...], w_gate_up[:, span(start, TILE)])
        up = dot(normed_two[...], w_gate_up[:, span(FF + start, TILE)])
        gate_up[:, span(start, TILE)] = gate.astype(LOW)
        gate_up[:, span(FF + start, TILE)] = up.astype(LOW)
        hidden[:, span(start, TILE)] = (gate * jax.nn.sigmoid(gate) * up).astype(LOW)


def down_forward(middle, hidden, w_down, result):
    for start in range(0, D, TILE):
        columns = span(start, TILE)
        result[:, columns] = (middle[:, columns] + dot_nt(hidden[...], w_down[columns, :])).astype(result.dtype)


def norm_back(grad, unit, inverse_rms, gain):
    weighted = grad * gain
    return inverse_rms * (weighted - unit * jnp.mean(weighted * unit, axis=-1, keepdims=True))


def gate_backward(upstream_low, w_down, gate_up, grad_ff, wait=no_wait):
    for start in range(0, FF, TILE):
        wait(start)
        grad_hidden = dot(upstream_low[...], w_down[:, span(start, TILE)])
        gate, up = gate_up[:, span(start, TILE)].astype(FULL), gate_up[:, span(FF + start, TILE)].astype(FULL)
        sigmoid_gate = jax.nn.sigmoid(gate)
        grad_gate = grad_hidden * up * sigmoid_gate * (1.0 + gate * (1.0 - sigmoid_gate))
        grad_ff[:, span(start, TILE)] = grad_gate.astype(LOW)
        grad_ff[:, span(FF + start, TILE)] = (grad_hidden * (gate * sigmoid_gate)).astype(LOW)


def ff_backward(upstream, middle, gain, w_gate_up, grad_ff, grad_middle, gain_grad, wait=no_wait):
    for start in range(0, D, TILE):
        wait(start)
        grad_middle[:, span(start, TILE)] = dot_nt(grad_ff[...], w_gate_up[span(start, TILE), :])
    unit, inverse_rms = unit_rows(middle[...])
    grad = grad_middle[...]
    gain_grad[1:2, :] = jnp.sum(grad * unit, axis=0, keepdims=True)
    grad_middle[...] = upstream[...].astype(FULL) + norm_back(grad, unit, inverse_rms, gain[1:2, :])


def out_backward(grad_middle, place, w_out, branch, grad_attended):
    branch[...] = dot_nt(grad_middle[...].astype(LOW), place[...]).astype(LOW)
    grad_rel = dot_nt(branch[...], w_out[...]).astype(LOW)
    grad_attended[...] = dot_nt(grad_rel, place[...]).astype(LOW)


def heads_backward(qkv, picked, near, far, grad_attended, cosine, sine, grad_joined):
    every = range(HEADS)
    for seq in range(COUNT):
        rows = span(seq * LENGTH, LENGTH)
        cos, sin = cosine[rows, :], -sine[rows, :]
        at = [span(head * HD, HD) for head in every]
        grad_outs = [grad_attended[rows, at[h]] for h in every]
        probs = [near[seq * HEADS + h] for h in every]
        values = [qkv[rows, span(2 * D + h * HD, HD)] for h in every]
        grad_values = [dot_tn(prob, grad_out) for prob, grad_out in zip(probs, grad_outs)]
        if picked is not None:
            probs = [jnp.concatenate([probs[h], far[seq * HEADS + h]], axis=1) for h in every]
            values = [jnp.concatenate([values[h], picked[1, seq, h]], axis=0) for h in every]
        probs = [prob.astype(FULL) for prob in probs]
        grads = [dot_nt(grad_out, value) for grad_out, value in zip(grad_outs, values)]
        deltas = [jnp.sum(prob * grad, axis=-1, keepdims=True) for prob, grad in zip(probs, grads)]
        grads = [(prob * (grad - delta)).astype(LOW) for prob, grad, delta in zip(probs, grads, deltas)]
        for h in every:
            grad_joined[rows, span(2 * D + h * HD, HD)] = grad_values[h].astype(LOW)
        queries = [dot(grads[h][:, :LENGTH], qkv[rows, span(D + h * HD, HD)]) * SCALE for h in every]
        keys = [dot_tn(grads[h][:, :LENGTH], qkv[rows, at[h]]) * SCALE for h in every]
        queries = [turn(query, cos, sin) for query in queries]
        keys = [turn(key, cos, sin) for key in keys]
        if picked is not None:
            queries = [queries[h] + dot(grads[h][:, LENGTH:], picked[0, seq, h]) * SCALE for h in every]
        for h in every:
            grad_joined[rows, at[h]] = queries[h].astype(LOW)
            grad_joined[rows, span(D + h * HD, HD)] = keys[h].astype(LOW)


def attend_backward(x, gain, w_qkv, grad_joined, grad_middle, normed, result, gain_grad):
    for start in range(0, D, TILE):
        result[:, span(start, TILE)] = dot_nt(grad_joined[...], w_qkv[span(start, TILE), :])
    unit, inverse_rms = unit_rows(x[...])
    normed[...] = (unit * gain[0:1, :]).astype(LOW)
    grad = result[...]
    gain_grad[0:1, :] = jnp.sum(grad * unit, axis=0, keepdims=True)
    result[...] = grad_middle[...] + norm_back(grad, unit, inverse_rms, gain[0:1, :])


EARLY = HALF + FF
WIDE = 2 * FF + HALF
LATE = 4 * D + 2 * HALF
GAINS = span(ROWS, 16)
LOWER, UPPER = span(0, HALF), span(HALF, HALF)
OWN = {name: span(at * HALF, HALF) for at, name in enumerate(("h2", "e", "h1", "o"))}


class Copies:
    def __init__(self, semaphores):
        self.semaphores, self.used, self.groups = semaphores, 0, {}

    def copy(self, at, source, target):
        source, target = (view[0].at[view[1]] if isinstance(view, tuple) else view for view in (source, target))
        return pltpu.make_async_copy(source, target, self.semaphores.at[at])

    def start(self, name, source, target):
        self.copy(self.used, source, target).start()
        self.groups.setdefault(name, []).append((self.used, source, target))
        self.used += 1

    def wait(self, *names):
        for name in names:
            for copy in self.groups.pop(name):
                self.copy(*copy).wait()

    def finish(self):
        self.wait(*list(self.groups))


def y_runs():
    return [(0, (0, PART), 0), (1, (0, PART), PART), (2, (0, PART // 2), 2 * PART)] + [
        (3, (0, PART // 2), 2 * PART + PART // 2),
        (4, (0, PART), 3 * PART),
    ]


def z_runs():
    runs = []
    for piece, dz, low, high in ((0, 0, 0, 4), (1, 1, 0, 4), (2, 2, 0, 2), (3, 2, 2, 4), (4, 3, 0, 4)):
        runs += [(piece, ((dy - low) * RUN, RUN), dy * PART + dz * RUN) for dy in range(low, high)]
    return runs


def load(copies, name, pieces, runs, columns, target, target_columns):
    for core in range(NC):
        for piece, (low, size), row in runs:
            source = pieces[core * 5 + piece], (span(low, size), columns)
            copies.start(name, source, (target, (span(core * HALF + row, size), target_columns)))


def load_qkv(copies, second, target):
    for at in range(3):
        columns = span(at * D, D)
        load(copies, f"qkv{at * D}", second, z_runs(), columns, target, columns)


def wait_qkv(copies):
    return lambda start: copies.wait(f"qkv{start}") if start % D == 0 else None


def load_out(copies, second, target):
    load(copies, "out", second, z_runs(), span(3 * D, D), target, span(0, D))


def load_gains(copies, second, target):
    load(copies, "gains", second, z_runs(), span(4 * D + CUT, PAD), target, span(0, PAD))


def load_gate(copies, first, target):
    for core in range(NC):
        for piece, (low, size), row in y_runs():
            row += core * HALF
            source = first[core * 5 + piece], (span(low, size), span(0, 2 * FF))
            copies.start(f"gate{row // TILE * TILE}", source, (target, (span(row, size), span(0, 2 * FF))))


GATE = tuple(f"gate{at}" for at in range(0, D, TILE))
DOWN = tuple(f"down{at}" for at in range(0, FF, D))


def load_down(copies, first, second, target, also=None):
    for start in range(0, FF, D):
        name = f"down{start}"
        if start < CUT:
            load(copies, name, second, z_runs(), span(4 * D + start, D), target, span(start, D))
        else:
            load(copies, name, first, y_runs(), span(2 * FF, FF - CUT), target, span(CUT, FF - CUT))
        if also:
            also(name, start, min(D, FF - start))


def kernel_first(section, core, *refs):
    (x, spread, cosine, sine, place), refs = refs[:5], refs[5:]
    first, second, refs = refs[:10], refs[10:20], refs[20:]
    (sent_o, qkv_o, near_o, late_o, middle_o, early_o, gate_up_o, own_o, gain_o), refs = refs[:9], refs[9:]
    xs, gains, cos, sin, places, w_qkv, w_out, w_gate, w_down = refs[:9]
    qkv, near, attended, attended_rel, middle, normed_two, gate_up, hidden, sent, spreads, gain_rows, semaphores = refs[9:]

    copies = Copies(semaphores)
    load_gains(copies, second, gain_rows)
    copies.start("gains", spread, spreads)

    @pl.when(section[0] == 0)
    def _():
        for source, target in ((x, xs), (cosine, cos), (sine, sin)):
            copies.start("small", source, target)
        load_qkv(copies, second, w_qkv)
        copies.start("place", place, places)
        load_out(copies, second, w_out)
        load_gate(copies, first, w_gate)
        load_down(copies, first, second, w_down)

    copies.wait("gains")
    rows = gain_rows[...].astype(FULL).T[:8].astype(LOW)
    low = lax.broadcasted_iota(jnp.int32, (1, D), 1) < HALF
    straight = jnp.logical_xor(low, core[0] == 1)
    for at in range(2):
        picked = dot(rows, spreads[at])
        gains[at : at + 1, :] = jnp.where(straight, picked[0:1], picked[1:2])
    copies.start("gain", gains, gain_o)

    @pl.when(section[0] == 0)
    def _():
        copies.wait("small")
        attend_forward(xs, gains, cos, sin, w_qkv, qkv, None, wait_qkv(copies))
        copies.start("done", qkv, qkv_o)
        heads_forward(qkv, None, None, None, near, None, attended)
        copies.start("done", near, near_o)
        copies.wait("place", "out")
        out_forward(xs, attended, places, w_out, attended_rel, middle)
        copies.start("done", attended_rel.at[:, LOWER], own_o.at[:, OWN["o"]])
        copies.start("done", attended_rel.at[:, UPPER], late_o.at[span(0, ROWS), span(4 * D + HALF, HALF)])
        copies.start("done", middle, middle_o)
        copies.wait(*GATE)
        ff_forward(middle, gains, w_gate, normed_two, gate_up, hidden)
        copies.start("done", normed_two.at[:, LOWER], own_o.at[:, OWN["h2"]])
        copies.start("done", normed_two.at[:, UPPER], early_o.at[:, LOWER])
        copies.start("done", gate_up, gate_up_o)
        copies.start("done", hidden, early_o.at[:, span(HALF, FF)])
        copies.wait(*DOWN)
        down_forward(middle, hidden, w_down, sent)
        copies.start("done", sent, sent_o)
        copies.wait("done")

    copies.wait("gain")


def two_parts(gain_grad):
    full = gain_grad[...]
    high = full.astype(LOW).astype(FULL)
    return jnp.concatenate([high, full - high, jnp.zeros((12, D), FULL)], axis=0).astype(LOW)


def kernel_last(section, counts, *refs):
    (x_low, upstream, gain, cosine, sine, place, picked), refs = refs[:7], refs[7:]
    first, second, refs = refs[:10], refs[10:20], refs[20:]
    refs = refs[3:]
    (early_o, late_o, own_o, result_o, sent_o, grad_ff_o), refs = refs[:6], refs[6:]
    xl, ups, up_low, gains, cos, sin, places, picks, w_qkv, w_out, w_gate, w_down = refs[:12]
    xs, qkv, plain, near, far, attended, attended_rel, middle, normed_two, gate_up, hidden, result = refs[12:24]
    grad_ff, grad_middle, branch, grad_joined, normed, gain_grad, gain_rows, semaphores = refs[24:]

    @pl.when(section[0] == 1)
    def _():
        copies = Copies(semaphores)
        for source, target in ((x_low, xl), (gain, gains), (cosine, cos), (sine, sin)):
            copies.start("small", source, target)
        load_qkv(copies, second, w_qkv)
        copies.start("picks", picked, picks)
        copies.start("place", place, places)
        load_out(copies, second, w_out)
        load_gate(copies, first, w_gate)
        load_down(copies, first, second, w_down)
        copies.start("up", upstream, ups)
        copies.wait("small")
        xs[...] = xl[...].astype(FULL)
        attend_forward(xs, gains, cos, sin, w_qkv, qkv, plain, wait_qkv(copies))
        copies.wait("picks")
        heads_forward(qkv, plain, picks, counts, near, far, attended)
        copies.wait("place", "out")
        out_forward(xs, attended, places, w_out, attended_rel, middle)
        copies.start("done", attended_rel.at[:, LOWER], own_o.at[:, OWN["o"]])
        copies.start("done", attended_rel.at[:, UPPER], late_o.at[span(0, ROWS), span(4 * D + HALF, HALF)])
        copies.wait(*GATE)
        ff_forward(middle, gains, w_gate, normed_two, gate_up, hidden)
        copies.start("done", normed_two.at[:, LOWER], own_o.at[:, OWN["h2"]])
        copies.start("done", normed_two.at[:, UPPER], early_o.at[:, LOWER])
        copies.start("done", hidden, early_o.at[:, span(HALF, FF)])
        copies.wait(*DOWN, "up")
        up_low[...] = ups[...].astype(LOW)
        copies.start("done", up_low.at[:, LOWER], own_o.at[:, OWN["e"]])
        copies.start("done", up_low.at[:, UPPER], grad_ff_o.at[:, span(2 * FF, HALF)])
        down_forward(middle, hidden, w_down, result)
        copies.start("result", result, result_o)
        gate_backward(up_low, w_down, gate_up, grad_ff)
        copies.start("done", grad_ff, grad_ff_o.at[:, span(0, 2 * FF)])
        ff_backward(ups, middle, gains, w_gate, grad_ff, grad_middle, gain_grad)
        out_backward(grad_middle, places, w_out, branch, attended)
        copies.start("done", branch, late_o.at[span(0, ROWS), span(3 * D, D)])
        heads_backward(qkv, picks, near, far, attended, cos, sin, grad_joined)
        copies.start("done", grad_joined, late_o.at[span(0, ROWS), span(0, 3 * D)])
        copies.wait("result")
        attend_backward(xs, gains, w_qkv, grad_joined, grad_middle, normed, result, gain_grad)
        xl[...] = result[...].astype(LOW)
        copies.start("done", xl, sent_o)
        copies.start("done", normed.at[:, LOWER], own_o.at[:, OWN["h1"]])
        copies.start("done", normed.at[:, UPPER], late_o.at[span(0, ROWS), span(4 * D, HALF)])
        gain_rows[...] = two_parts(gain_grad)
        copies.start("done", gain_rows, late_o.at[GAINS, span(0, D)])
        copies.finish()


def kernel_back_gate(section, *refs):
    (upstream, gate_up), refs = refs[:2], refs[2:]
    first, second, refs = refs[:10], refs[10:20], refs[20:]
    refs = refs[3:]
    (grad_ff_o, own_o), refs = refs[:2], refs[2:]
    ups, gate_ups, w_down, grad_ff, semaphores = refs

    @pl.when(section[0] == 0)
    def _():
        copies = Copies(semaphores)
        copies.start("up", upstream, ups)

        def saved(name, start, size):
            for columns in (span(start, size), span(FF + start, size)):
                copies.start(name, gate_up.at[:, columns], gate_ups.at[:, columns])

        load_down(copies, first, second, w_down, saved)
        copies.wait("up")
        copies.start("done", ups.at[:, LOWER], own_o.at[:, OWN["e"]])
        copies.start("done", ups.at[:, UPPER], grad_ff_o.at[:, span(2 * FF, HALF)])
        gate_backward(
            ups, w_down, gate_ups, grad_ff, lambda start: copies.wait(f"down{start}") if start % D == 0 else None
        )
        copies.start("done", grad_ff, grad_ff_o.at[:, span(0, 2 * FF)])
        copies.finish()


def kernel_back_ff(section, *refs):
    (upstream, gain, middle, grad_ff), refs = refs[:4], refs[4:]
    first, refs = refs[:10], refs[11:]
    (grad_middle_o, gain_grad_o), refs = refs[:2], refs[2:]
    ups, gains, mid, grad_ffs, w_gate, grad_middle, gain_grad, semaphores = refs

    @pl.when(section[0] == 0)
    def _():
        copies = Copies(semaphores)
        copies.start("first", grad_ff.at[:, span(0, 2 * FF)], grad_ffs)
        load_gate(copies, first, w_gate)
        copies.start("late", upstream, ups)
        copies.start("late", middle, mid)
        copies.start("late", gain, gains)
        copies.wait("first")

        def wait(start):
            copies.wait(f"gate{start}")
            if start == D - TILE:
                copies.wait("late")

        ff_backward(ups, mid, gains, w_gate, grad_ffs, grad_middle, gain_grad, wait)
        copies.start("done", grad_middle, grad_middle_o)
        copies.start("done", gain_grad, gain_grad_o)
        copies.finish()


def kernel_back_attend(section, *refs):
    (x, gain, cosine, sine, place, qkv, near, grad_middle, gain_part), refs = refs[:9], refs[9:]
    second, refs = refs[:10], refs[11:]
    (late_o, own_o, result_o), refs = refs[3:6], refs[6:]
    xs, gains, cos, sin, places, qkvs, nears, grad_mid, w_qkv, w_out = refs[:10]
    grad_attended, branch, grad_joined, normed, result, gain_grad, gain_rows, semaphores = refs[10:]

    @pl.when(section[0] == 0)
    def _():
        copies = Copies(semaphores)
        copies.start("mid", grad_middle, grad_mid)
        copies.start("mid", place, places)
        load_out(copies, second, w_out)
        for source, target in ((qkv, qkvs), (near, nears), (cosine, cos), (sine, sin)):
            copies.start("saved", source, target)
        load_qkv(copies, second, w_qkv)
        for source, target in ((x, xs), (gain, gains), (gain_part, gain_grad)):
            copies.start("late", source, target)
        copies.wait("mid", "out")
        out_backward(grad_mid, places, w_out, branch, grad_attended)
        copies.start("done", branch, late_o.at[span(0, ROWS), span(3 * D, D)])
        copies.wait("saved")
        heads_backward(qkvs, None, nears, None, grad_attended, cos, sin, grad_joined)
        copies.start("done", grad_joined, late_o.at[span(0, ROWS), span(0, 3 * D)])
        copies.wait("qkv0", f"qkv{D}", f"qkv{2 * D}", "late")
        attend_backward(xs, gains, w_qkv, grad_joined, grad_mid, normed, result, gain_grad)
        copies.start("done", result, result_o)
        copies.start("done", normed.at[:, LOWER], own_o.at[:, OWN["h1"]])
        copies.start("done", normed.at[:, UPPER], late_o.at[span(0, ROWS), span(4 * D, HALF)])
        gain_rows[...] = two_parts(gain_grad)
        copies.start("done", gain_rows, late_o.at[GAINS, span(0, D)])
        copies.finish()


def shape(*dims, dtype=LOW):
    return jax.ShapeDtypeStruct(dims, dtype)


def vmem(*dims, dtype=LOW):
    return pltpu.VMEM(dims, dtype)


Y_COPIES, Z_COPIES = 2 * 5, 2 * 16
QKV_COPIES, DOWN_COPIES = 3 * Z_COPIES, 2 * Z_COPIES + Y_COPIES
W_QKV, W_OUT, W_GATE, W_DOWN = vmem(D, 3 * D), vmem(D, D), vmem(D, 2 * FF), vmem(D, FF)


def call(kernel, operands, scalars, outs, scratch, copies, aliases=None):
    return pl.pallas_call(
        kernel,
        out_shape=outs,
        in_specs=[SMEM] * scalars + [HBM] * (len(operands) - scalars),
        out_specs=[HBM] * len(outs),
        scratch_shapes=list(scratch) + [pltpu.SemaphoreType.DMA((copies,))],
        input_output_aliases=aliases or {},
        compiler_params=pltpu.CompilerParams(vmem_limit_bytes=62 * MIB),
        cost_estimate=pl.CostEstimate(flops=1000, bytes_accessed=1000, transcendentals=0),
    )(*operands)


def run_first(section, core, x, spread, cosine, sine, place, first, second):
    outs = [
        shape(ROWS, D), shape(ROWS, 3 * D), shape(COUNT * HEADS, LENGTH, LENGTH), shape(ROWS + 16, LATE),
        shape(ROWS, D, dtype=FULL), shape(ROWS, EARLY), shape(ROWS, 2 * FF), shape(ROWS, 4 * HALF),
        shape(2, D, dtype=FULL),
    ]
    scratch = [vmem(ROWS, D, dtype=FULL), vmem(2, D, dtype=FULL), vmem(ROWS, HD, dtype=FULL), vmem(ROWS, HD, dtype=FULL)]
    scratch += [vmem(D, D), W_QKV, W_OUT, W_GATE, W_DOWN]
    scratch += [vmem(ROWS, 3 * D), vmem(COUNT * HEADS, LENGTH, LENGTH), vmem(ROWS, D), vmem(ROWS, D)]
    scratch += [vmem(ROWS, D, dtype=FULL), vmem(ROWS, D), vmem(ROWS, 2 * FF), vmem(ROWS, FF), vmem(ROWS, D)]
    scratch += [vmem(2, D, D), vmem(D, PAD)]
    operands = [section, core, x, spread, cosine, sine, place, *first, *second]
    return call(kernel_first, operands, 2, outs, scratch, 24 + Y_COPIES + 2 * Z_COPIES + QKV_COPIES + DOWN_COPIES)


def run_last(section, counts, x_low, upstream, gain, cosine, sine, place, picked, first, second, kept):
    outs = [shape(ROWS, EARLY), shape(ROWS + 16, LATE), shape(ROWS, 4 * HALF), shape(ROWS, D, dtype=FULL)]
    outs += [shape(ROWS, D), shape(ROWS, WIDE)]
    scratch = [vmem(ROWS, D), vmem(ROWS, D, dtype=FULL), vmem(ROWS, D), vmem(2, D, dtype=FULL)]
    scratch += [vmem(ROWS, HD, dtype=FULL), vmem(ROWS, HD, dtype=FULL), vmem(D, D), vmem(2, COUNT, HEADS, LENGTH, HD)]
    scratch += [W_QKV, W_OUT, W_GATE, W_DOWN]
    scratch += [vmem(ROWS, D, dtype=FULL), vmem(ROWS, 3 * D), vmem(ROWS, D)]
    scratch += [vmem(COUNT * HEADS, LENGTH, LENGTH)] * 2
    scratch += [vmem(ROWS, D), vmem(ROWS, D), vmem(ROWS, D, dtype=FULL), vmem(ROWS, D), vmem(ROWS, 2 * FF)]
    scratch += [vmem(ROWS, FF), vmem(ROWS, D, dtype=FULL)]
    scratch += [vmem(ROWS, 2 * FF), vmem(ROWS, D, dtype=FULL), vmem(ROWS, D), vmem(ROWS, 3 * D), vmem(ROWS, D)]
    scratch += [vmem(2, D, dtype=FULL), vmem(16, D)]
    operands = [section, counts, x_low, upstream, gain, cosine, sine, place, picked, *first, *second, *kept]
    aliases = {len(operands) - 3 + i: i for i in range(3)}
    return call(kernel_last, operands, 2, outs, scratch, 24 + Y_COPIES + Z_COPIES + QKV_COPIES + DOWN_COPIES, aliases)


def run_back_gate(section, upstream, gate_up, first, second, early, grad_ff, own):
    outs = [shape(ROWS, WIDE), shape(ROWS, 4 * HALF)]
    scratch = [vmem(ROWS, D), vmem(ROWS, 2 * FF), W_DOWN, vmem(ROWS, 2 * FF)]
    operands = [section, upstream, gate_up, *first, *second, early, grad_ff, own]
    at = len(operands) - 2
    return call(
        kernel_back_gate, operands, 1, outs, scratch, 16 + DOWN_COPIES, {at: 0, at + 1: 1}
    )


def run_back_ff(section, upstream, gain, middle, grad_ff, first, after):
    outs = [shape(ROWS, D, dtype=FULL), shape(2, D, dtype=FULL)]
    scratch = [vmem(ROWS, D), vmem(2, D, dtype=FULL), vmem(ROWS, D, dtype=FULL), vmem(ROWS, 2 * FF)]
    scratch += [W_GATE, vmem(ROWS, D, dtype=FULL), vmem(2, D, dtype=FULL)]
    operands = [section, upstream, gain, middle, grad_ff, *first, after]
    return call(kernel_back_ff, operands, 1, outs, scratch, 10 + Y_COPIES)


def run_back_attend(section, x, gain, cosine, sine, place, qkv, near, grad_middle, gain_part, second, after, kept):
    outs = [shape(ROWS + 16, LATE), shape(ROWS, 4 * HALF), shape(ROWS, D, dtype=FULL)]
    scratch = [vmem(ROWS, D, dtype=FULL), vmem(2, D, dtype=FULL), vmem(ROWS, HD, dtype=FULL), vmem(ROWS, HD, dtype=FULL)]
    scratch += [vmem(D, D), vmem(ROWS, 3 * D), vmem(COUNT * HEADS, LENGTH, LENGTH), vmem(ROWS, D, dtype=FULL)]
    scratch += [W_QKV, W_OUT, vmem(ROWS, D), vmem(ROWS, D), vmem(ROWS, 3 * D), vmem(ROWS, D), vmem(ROWS, D, dtype=FULL)]
    scratch += [vmem(2, D, dtype=FULL), vmem(16, D)]
    operands = [section, x, gain, cosine, sine, place, qkv, near, grad_middle, gain_part, *second, after, *kept]
    at = len(operands) - 3
    return call(
        kernel_back_attend, operands, 1, outs, scratch, 20 + Z_COPIES + QKV_COPIES, {at + i: i for i in range(3)}
    )


def pick_kernel(memory, index, out):
    chosen = index[0, 0]
    hot = (lax.broadcasted_iota(jnp.int32, (memory.shape[2], LENGTH), 0) == chosen).astype(FULL).astype(LOW)
    for kind in range(2):
        out[kind, 0, 0] = dot_tn(hot, memory[0, kind]).astype(LOW)


def run_pick(memory, mem_index):
    slots = memory.shape[2]
    return pl.pallas_call(
        pick_kernel,
        grid=(COUNT, HEADS),
        in_specs=[
            pl.BlockSpec((1, 2, slots, HD), lambda n, h: (n, 0, 0, h)),
            pl.BlockSpec((1, 1, 1, LENGTH), lambda n, h: (n, h, 0, 0)),
        ],
        out_specs=pl.BlockSpec((2, 1, 1, LENGTH, HD), lambda n, h: (0, n, h, 0, 0)),
        out_shape=shape(2, COUNT, HEADS, LENGTH, HD),
    )(memory, mem_index.reshape(COUNT, HEADS, 1, LENGTH))


def z_first(rows):
    return jnp.concatenate([rows[span(dy * PART + dz * RUN, RUN), :] for dz in range(NZ) for dy in range(NY)], axis=0)


HALVES = PART // 2
QKV_CUT = 17 * 128
N_FF, N_Y, N_Z = FF + FF // 2, QKV_CUT, 3 * D - QKV_CUT + D + PAD
FF_PARTS = (
    (0, "e", "early", HALF, FF // 2, FF), (1, "e", "early", HALF + FF // 2, FF // 2, FF),
    (0, "h2", "wide", 0, FF, 0), (1, "h2", "wide", FF, FF, 0),
)
QKV_PARTS = (
    (1, "o", "late", 3 * D, D, 3 * D - QKV_CUT), (0, "h1", "late", 0, QKV_CUT, 0),
    (1, "h1", "late", QKV_CUT, 3 * D - QKV_CUT, 0), (1, None, None, 0, PAD, 3 * D - QKV_CUT + D),
)


def put(copies, staged, columns, targets):
    for source, (ref, rows, shift) in targets.items():
        at = span(columns.start + shift, columns.stop - columns.start)
        copies.start("done", staged.at[span(source * HALVES, HALVES), columns], ref.at[rows, at])


def products(copies, parts, sides, rights, stages, targets, extra=None):
    for z, left, right, first, size, at in parts:
        stage = stages[z]
        if left is None:
            stage[:, span(at, size)] = extra()
        else:
            own, other = sides(left)
            if z:
                own, other = z_first(own), z_first(other)
            mine, theirs = rights(right, first)
            for start in range(0, size, TILE):
                width = min(TILE, size - start)
                columns = span(first + start, width)
                product = dot(own, mine[:, columns]) + dot(other, theirs[:, columns])
                stage[:, span(at + start, width)] = product.astype(LOW)
        put(copies, stage, span(at, size), targets[z])


def ff_targets(own, ahead, behind, low, high):
    upper, lower = span(0, HALVES), span(HALVES, HALVES)
    return {
        4: (ahead, upper, 0), 3: (ahead, lower, 0), 5: (behind, upper, 0), 6: (behind, lower, 0),
        2: (low, upper, 0), 7: (high, upper, 0), 0: (own, upper, 0), 1: (own, lower, 0),
    }


def kernel_grad_ff(early, other_early, wide, other_wide, own, after, *refs):
    outs, (er, oer, wi, owi, ow, stage_y, stage_z, semaphores) = refs[:10], refs[10:]
    copies = Copies(semaphores)
    tail = span(2 * FF, HALF)
    copies.start("a", other_wide.at[:, tail], owi.at[:, tail])
    for source, target in ((early, er), (other_early, oer), (own, ow)):
        copies.start("a", source, target)
    for at in range(2):
        for source, target in ((wide, wi), (other_wide, owi)):
            copies.start(f"b{at * FF}", source.at[:, span(at * FF, FF)], target.at[:, span(at * FF, FF)])
    copies.wait("a")
    left = {"e": (ow[:, OWN["e"]].T, owi[:, tail].T), "h2": (ow[:, OWN["h2"]].T, oer[:, LOWER].T)}

    def rights(name, first):
        if name == "wide":
            copies.wait(f"b{first}")
        return (wi, owi) if name == "wide" else (er, oer)

    targets = ff_targets(*outs[:5]), ff_targets(*outs[5:])
    products(copies, FF_PARTS, left.get, rights, (stage_y, stage_z), targets)
    copies.finish()


def run_grad_ff(early, other_early, wide, other_wide, own, after):
    scratch = [vmem(ROWS, EARLY)] * 2 + [vmem(ROWS, WIDE)] * 2 + [vmem(ROWS, 4 * HALF)] + [vmem(HALF, N_FF)] * 2
    outs = [shape(rows, N_FF) for rows in (PART, PART, PART, HALVES, HALVES)] * 2
    operands = [early, other_early, wide, other_wide, own, after]
    outs = call(kernel_grad_ff, operands, 0, outs, scratch, 8 + 8 * 4)
    return outs[:5], outs[5:]


def kernel_grad_attend(late, other_late, own, pack, *refs):
    outs, (la, ola, ow, pa, stage_y, stage_z, semaphores) = refs[:10], refs[10:]
    copies = Copies(semaphores)
    copies.start("a", own, ow)
    tail = span(3 * D, LATE - 3 * D)
    for name, columns in (("a", tail), ("b0", span(0, QKV_CUT)), (f"b{QKV_CUT}", span(QKV_CUT, 3 * D - QKV_CUT))):
        for source, target in ((late, la), (other_late, ola)):
            copies.start(name, source.at[:, columns], target.at[:, columns])
    copies.start("pack", pack, pa)
    copies.wait("a")
    left = {
        "h1": (ow[:, OWN["h1"]].T, ola[span(0, ROWS), span(4 * D, HALF)].T),
        "o": (ow[:, OWN["o"]].T, ola[span(0, ROWS), span(4 * D + HALF, HALF)].T),
    }

    def extra():
        copies.wait("pack")
        mine, theirs = la[GAINS, span(0, D)], ola[GAINS, span(0, D)]
        theirs = jnp.concatenate([theirs[:, UPPER], theirs[:, LOWER]], axis=1)
        columns = []
        for at in range(2):
            matrix = pa[at]
            first = dot(mine, matrix[:D]) + dot(theirs, matrix[:D])
            second = dot(mine, matrix[D:]) + dot(theirs, matrix[D:])
            columns.append(first[0:1] + first[2:3] + second[1:2] + second[3:4])
        rows = jnp.concatenate(columns + [jnp.zeros((PAD - 2, HALF), FULL)], axis=0)
        return z_first(rows.T).astype(LOW)

    mine, theirs = la.at[span(0, ROWS), :], ola.at[span(0, ROWS), :]

    def rights(name, first):
        if first < 3 * D:
            copies.wait(f"b{first}")
        return mine, theirs

    targets = ff_targets(*outs[:5]), ff_targets(*outs[5:])
    products(copies, QKV_PARTS, left.get, rights, (stage_y, stage_z), targets, extra)
    copies.finish()


def run_grad_attend(late, other_late, own, pack):
    scratch = [vmem(ROWS + 16, LATE)] * 2 + [vmem(ROWS, 4 * HALF), vmem(2, 2 * D, HALF), vmem(HALF, N_Y), vmem(HALF, N_Z)]
    outs = [shape(rows, width) for width in (N_Y, N_Z) for rows in (PART, PART, PART, HALVES, HALVES)]
    operands = [late, other_late, own, pack]
    outs = call(kernel_grad_attend, operands, 0, outs, scratch, 10 + 8 * 4)
    return outs[:5], outs[5:]


def kernel_low(gate_up, down, qkv, out, gains, first, second):
    first[:, span(0, 2 * FF)] = gate_up[0].astype(LOW)
    first[:, span(2 * FF, FF - CUT)] = down[0, :, CUT:].astype(LOW)
    second[:, span(0, 3 * D)] = qkv[0].astype(LOW)
    second[:, span(3 * D, D)] = out[0].astype(LOW)
    second[:, span(4 * D, CUT)] = down[0, :, :CUT].astype(LOW)
    row = lax.broadcasted_iota(jnp.int32, (BLOCK, 2 * BLOCK), 0)
    lane = lax.broadcasted_iota(jnp.int32, (BLOCK, 2 * BLOCK), 1)
    column = lax.broadcasted_iota(jnp.int32, (BLOCK, PAD), 1)
    block = jnp.zeros((BLOCK, PAD), FULL)
    for at in range(2):
        own = jnp.sum(jnp.where(lane == row + at * BLOCK, gains[...], 0.0), axis=1, keepdims=True)
        block = block + jnp.where(column == at, own, 0.0)
    second[:, span(4 * D + CUT, PAD)] = block.astype(LOW)


def run_low(gate_up, down, qkv, out, gains):
    return pl.pallas_call(
        kernel_low, out_shape=[shape(BLOCK, 3 * FF - CUT), shape(BLOCK, 4 * D + CUT + PAD)]
    )(gate_up, down, qkv, out, gains)


def kernel_last_sums(y, z, *refs):
    blocks, (qkv, out, gate_up, down, gains) = refs[:8], refs[8:]
    rest = 3 * D - QKV_CUT
    total_y, total_z = y[:BLOCK].astype(FULL), z[:BLOCK].astype(FULL)
    for at in range(3):
        total_y = total_y + blocks[at][:BLOCK].astype(FULL)
        total_z = total_z + blocks[4 + at][:BLOCK].astype(FULL)
    total_y = total_y + blocks[3][...].astype(FULL)
    total_z = total_z + blocks[7][...].astype(FULL)
    gate_up[0, :, span(0, FF)] = total_y[:, :FF]
    gate_up[0, :, span(FF, FF)] = total_z[:, :FF]
    down[0, :, span(0, FF // 2)] = total_y[:, FF:N_FF]
    down[0, :, span(FF // 2, FF // 2)] = total_z[:, FF:N_FF]
    qkv[0, :, span(0, QKV_CUT)] = total_y[:, N_FF:]
    qkv[0, :, span(QKV_CUT, rest)] = total_z[:, N_FF : N_FF + rest]
    out[0] = total_z[:, N_FF + rest : N_FF + rest + D]
    gains[...] = total_z[:, N_FF + rest + D :]


def run_last_sums(y, z):
    outs = [shape(1, BLOCK, size, dtype=FULL) for size in (3 * D, D, 2 * FF, FF)] + [shape(BLOCK, PAD, dtype=FULL)]
    return pl.pallas_call(kernel_last_sums, out_shape=outs)(y[0], z[0], *y[1:], *z[1:])


def hop(block, axis, step):
    count = lax.axis_size(axis)
    return lax.ppermute(block, axis, [(at, (at + step) % count) for at in range(count)])


def gather_near(block, axis):
    pair = jnp.concatenate([block, hop(block, "xh", 1)])
    ahead = hop(pair, axis, -1)
    behind = hop(pair, axis, 1)
    across = hop(ahead, axis, -1)
    return jnp.concatenate([pair, ahead, across, behind])


def gather_far(whole, behind, ahead, axis):
    low = hop(behind[: PART // 2], axis, 1)
    high = hop(ahead[PART // 2 :], axis, -1)
    own = [whole, ahead, low, high, behind]
    return own + [hop(piece, "core", 1) for piece in own]


def total(*terms):
    result = terms[0].astype(FULL)
    for term in terms[1:]:
        result = result + term.astype(FULL)
    return result


def scatter_begin(blocks, axis):
    return hop(blocks[1], axis, 1), hop(blocks[2], axis, -1)


def scatter_sums(blocks, begun):
    return total(blocks[3], begun[0][:HALVES]).astype(LOW), total(blocks[4], begun[1][:HALVES]).astype(LOW)


def scatter_main(sums, axis):
    return hop(sums[0], axis, 1), hop(sums[1], axis, -1)


def scatter_halves(blocks, begun, main):
    low, high = [], []
    for block, (ahead, behind), (main_low, main_high) in zip(blocks, begun, main):
        low.append(total(block[0][:HALVES], behind[HALVES:], main_low))
        high.append(total(block[0][HALVES:], ahead[HALVES:], main_high))
    return jnp.concatenate(low, axis=1), jnp.concatenate(high, axis=1)


def scatter_end(low, high, axis, in_turn=False):
    three = hop(high[RUN:].astype(LOW), axis, -1)
    two = hop(high[:RUN].astype(LOW), axis, 2)
    one = low[RUN:].astype(LOW)
    if in_turn:
        one, three = lax.optimization_barrier((one, three))
    one = hop(one, axis, 1)
    low = low[:RUN].astype(LOW)
    other = hop(total(low[BLOCK:], one[BLOCK:], two[BLOCK:], three[BLOCK:]).astype(LOW), "xh", 1)
    return low, one, two, three, other


def natural_of(rel, run, at):
    lane = rel % run
    rel = rel // run
    xx = (rel % NX + at[2]) % NX
    zz = (rel // NX % NZ + at[1]) % NZ
    yy = (rel // (NX * NZ) % NY + at[0]) % NY
    cc = (rel // (NX * NZ * NY) + at[3]) % NC
    return (((yy * NZ + zz) * NX + xx) * NC + cc) * run + lane


def place_matrix(at):
    natural = natural_of(jnp.arange(D), BLOCK, at)
    return (jnp.arange(D)[:, None] == natural[None, :]).astype(LOW)


def spread_matrix(at):
    natural = natural_of(jnp.arange(D), BLOCK, at)
    wanted = natural // (2 * BLOCK) * BLOCK + natural % BLOCK + jnp.arange(2)[:, None] * HALF
    return (natural[None, :, None] == wanted[:, None, :]).astype(LOW)


def pack_matrix(at):
    row = natural_of(jnp.arange(HALF), BLOCK, at)
    wanted = (row // BLOCK * (2 * BLOCK) + row % BLOCK)[None, :] + jnp.arange(2)[:, None] * BLOCK
    source = (jnp.arange(2)[:, None] * D + natural_of(jnp.arange(D), BLOCK, at)[None, :]).reshape(-1)
    return (wanted[:, None, :] == source[None, :, None]).astype(LOW)


def rotary_tables():
    half_dim = HD // 2
    rate_list = 10000.0 ** (-jnp.arange(half_dim, dtype=FULL) / half_dim)
    angles = jnp.arange(LENGTH, dtype=FULL)[:, None] * rate_list[None, :]
    cosine, sine = jnp.cos(angles), jnp.sin(angles)
    cosine = jnp.concatenate([cosine, cosine], axis=1)
    sine = jnp.concatenate([-sine, sine], axis=1)
    return jnp.tile(cosine, (COUNT, 1)), jnp.tile(sine, (COUNT, 1))


def local(boundary, w_qkv, w_out, w_gate_up, w_down_t, gains, memory, mem_index, mem_counts):
    section = lax.axis_index("section").astype(jnp.int32).reshape(1)
    core = lax.axis_index("core").astype(jnp.int32).reshape(1)
    first, second = run_low(w_gate_up, w_down_t, w_qkv, w_out, gains)
    first = gather_near(first, "z")
    second = gather_near(second, "y")
    at = tuple(lax.axis_index(name) for name in DP)
    at, boundary, first, second = lax.optimization_barrier((at, boundary, first, second))
    first_behind, first_ahead = hop(first, "y", 1), hop(first, "y", -1)
    second_behind, second_ahead = hop(second, "z", 1), hop(second, "z", -1)
    place = place_matrix(at)
    pack = pack_matrix(at)
    spread = spread_matrix(at)
    cosine, sine = rotary_tables()
    edge = dot(boundary.reshape(ROWS, D), place, lax.Precision.HIGHEST)
    moved, prepared = lax.optimization_barrier(
        ((first_behind, first_ahead, second_behind, second_ahead), (place, pack, spread, cosine, sine, edge))
    )
    first_behind, first_ahead, second_behind, second_ahead = moved
    place, pack, spread, cosine, sine, edge = prepared
    first = gather_far(first, first_behind, first_ahead, "y")
    second = gather_far(second, second_behind, second_ahead, "z")
    picked = run_pick(memory, mem_index)

    sent, qkv, near, late, middle, early, gate_up, own, gain = run_first(
        section, core, edge, spread, cosine, sine, place, first, second
    )
    moved = lax.ppermute(sent, "section", [(0, 1)])
    early, late, own, result, sent, wide = run_last(
        section, mem_counts, moved, edge, gain, cosine, sine, place, picked, first, second, (early, late, own)
    )
    upstream = lax.ppermute(sent, "section", [(1, 0)])
    other_early = hop(early, "core", 1)
    wide, own = run_back_gate(section, upstream, gate_up, first, second, other_early, wide, own)
    other_wide = hop(wide, "core", 1)
    gate_y, gate_z = run_grad_ff(early, other_early, wide, other_wide, own, upstream)
    begun_gate_y = scatter_begin(gate_y, "y")
    begun_gate_z = scatter_begin(gate_z, "z")
    grad_middle, gain_part = run_back_ff(section, upstream, gain, middle, wide, first, gate_z[0])
    late, own, result = run_back_attend(
        section, edge, gain, cosine, sine, place, qkv, near, grad_middle, gain_part, second, gate_z[0],
        (late, own, result),
    )
    other_late = hop(late, "core", 1)
    sums_y, sums_z = scatter_sums(gate_y, begun_gate_y), scatter_sums(gate_z, begun_gate_z)
    other_late, sums_y, sums_z = lax.optimization_barrier((other_late, sums_y, sums_z))
    main_gate_y, main_gate_z = scatter_main(sums_y, "y"), scatter_main(sums_z, "z")
    qkv_y, qkv_z = run_grad_attend(late, other_late, own, pack)
    qkv_y, qkv_z, main_gate_y, main_gate_z = lax.optimization_barrier((qkv_y, qkv_z, main_gate_y, main_gate_z))
    begun_qkv_y = scatter_begin(qkv_y, "y")
    begun_qkv_z = scatter_begin(qkv_z, "z")
    finals = dot(result, place.T, lax.Precision.HIGHEST).reshape(1, COUNT, LENGTH, D)
    begun_qkv_y, begun_qkv_z, finals = lax.optimization_barrier((begun_qkv_y, begun_qkv_z, finals))
    main_qkv_y = scatter_main(scatter_sums(qkv_y, begun_qkv_y), "y")
    main_qkv_z = scatter_main(scatter_sums(qkv_z, begun_qkv_z), "z")
    low_y, high_y = scatter_halves((gate_y, qkv_y), (begun_gate_y, begun_qkv_y), (main_gate_y, main_qkv_y))
    low_z, high_z = scatter_halves((gate_z, qkv_z), (begun_gate_z, begun_qkv_z), (main_gate_z, main_qkv_z))
    y, z = scatter_end(low_y, high_y, "z"), scatter_end(low_z, high_z, "y", True)
    qkv_grad, out_grad, gate_grad, down_grad, gain_grad = run_last_sums(y, z)
    return finals, qkv_grad, out_grad, gate_grad, down_grad, gain_grad[:, :2].T.reshape(1, -1)


def solution(mesh):
    mesh = Mesh(mesh.devices.reshape(2, NY, NZ, NX, NC), ("section",) + DP)
    in_specs = (
        P("section", DP, None, None),
        P("section", DP, None),
        P("section", DP, None),
        P("section", DP, None),
        P("section", DP, None),
        P("section", DP),
        P(DP, None, None, None),
        P(DP, None, None),
        P(DP),
    )
    return jax.shard_map(local, mesh=mesh, in_specs=in_specs, out_specs=in_specs[:6], check_vma=False)
```
